128 devices in a mesh: role: 2 (over core), dp: 64 (over y, z, x).
Axes of the slice: x: 4, y: 4, z: 4, core: 2. Of those that a mesh axis runs over, the one named last changes fastest.
Arguments:
- patch_rows: bfloat16 [81920, 768], P(('role', 'dp')), may hold values from -6 to 6
- patch_order: int32 [1024, 196], replicated, may hold values from 0 to 195, each once within a row
- visible_count: int32 [1024], replicated, may hold values from 20 to 78, as said below
- encoded_image: int32 [1024], replicated, may hold values from 0 to 1023, as said below
- first_gain: bfloat16 [768], P(('role', 'dp')), may hold values from 0.5 to 1.5
- first_shift: bfloat16 [768], P(('role', 'dp')), may hold values from -1.75 to 1.75
- query_key_value: bfloat16 [768, 2304], P(('role', 'dp')), may hold values from -0.21875 to 0.21875
- query_bias: bfloat16 [768], P(('role', 'dp')), may hold values from -1.75 to 1.75
- value_bias: bfloat16 [768], P(('role', 'dp')), may hold values from -1.75 to 1.75
- output_weight: bfloat16 [768, 768], P(('role', 'dp')), may hold values from -1.5 to 1.5
- output_bias: bfloat16 [768], P(('role', 'dp')), may hold values from -1.75 to 1.75
- second_gain: bfloat16 [768], P(('role', 'dp')), may hold values from 0.5 to 1.5
- second_shift: bfloat16 [768], P(('role', 'dp')), may hold values from -1.75 to 1.75
- up_weight: bfloat16 [768, 3072], P(('role', 'dp')), may hold values from -0.21875 to 0.21875
- up_bias: bfloat16 [3072], P(('role', 'dp')), may hold values from -1.75 to 1.75
- down_weight: bfloat16 [3072, 768], P(('role', 'dp')), may hold values from -0.109375 to 0.109375
- down_bias: bfloat16 [768], P(('role', 'dp')), may hold values from -1.75 to 1.75
- embed_weight: bfloat16 [768, 512], P(('role', 'dp')), may hold values from -0.21875 to 0.21875
- embed_bias: bfloat16 [512], P(('role', 'dp')), may hold values from -1.75 to 1.75
- mask_token: bfloat16 [512], P(('role', 'dp')), may hold values from -6 to 6
- decoder_gain: bfloat16 [512], P(('role', 'dp')), may hold values from 0.5 to 1.5
- decoder_shift: bfloat16 [512], P(('role', 'dp')), may hold values from -1.75 to 1.75
- pixel_weight: bfloat16 [512, 768], P(('role', 'dp')), may hold values from -0.25 to 0.25
- pixel_bias: bfloat16 [768], P(('role', 'dp')), may hold values from -1.75 to 1.75
- pixel_grad: bfloat16 [1024, 196, 768], P(('role', 'dp')), may hold values from -6 to 6
Outputs:
- pixels: bfloat16 [1024, 196, 768], P(('role', 'dp'))
- patch_grad: bfloat16 [81920, 768], P(('role', 'dp'))
- first_gain_grad: float32 [768], P(('role', 'dp'))
- first_shift_grad: float32 [768], P(('role', 'dp'))
- query_key_value_grad: float32 [768, 2304], P(('role', 'dp'))
- query_bias_grad: float32 [768], P(('role', 'dp'))
- value_bias_grad: float32 [768], P(('role', 'dp'))
- output_weight_grad: float32 [768, 768], P(('role', 'dp'))
- output_bias_grad: float32 [768], P(('role', 'dp'))
- second_gain_grad: float32 [768], P(('role', 'dp'))
- second_shift_grad: float32 [768], P(('role', 'dp'))
- up_weight_grad: float32 [768, 3072], P(('role', 'dp'))
- up_bias_grad: float32 [3072], P(('role', 'dp'))
- down_weight_grad: float32 [3072, 768], P(('role', 'dp'))
- down_bias_grad: float32 [768], P(('role', 'dp'))
- embed_weight_grad: float32 [768, 512], P(('role', 'dp'))
- embed_bias_grad: float32 [512], P(('role', 'dp'))
- mask_token_grad: float32 [512], P(('role', 'dp'))
- decoder_gain_grad: float32 [512], P(('role', 'dp'))
- decoder_shift_grad: float32 [512], P(('role', 'dp'))
- pixel_weight_grad: float32 [512, 768], P(('role', 'dp'))
- pixel_bias_grad: float32 [768], P(('role', 'dp'))
The draws below stay inside these ranges and needn't reach their ends.
Inputs may be any that keep to these rules, and one draw needn't show every extreme that they name: `visible_count`: some image has exactly 20 visible patches and some exactly 78. `encoded_image`: each image stands once; slot j is on device j // 8 (devices counted over role and dp, role first); with that device at role index r and dp index p, the image of slot j has its grid on the device at role index 1 - r and dp index (p + j % 8) % 64, and the grid of image i is on device i // 8.
All inputs are finite; a program needn't handle non-finite values.
Results may differ from the reference program's by a relative error of at most 0.019.
Values may be sent and summed in bfloat16 or wider, within the bound.
No kernel may reach another device: no remote copies, remote signals or barrier semaphores. Data moves between devices by JAX's collectives and lax.ppermute only.
A program may use at most 256 MiB of HBM per device.

```python
import jax
import jax.numpy as jnp
from jax import lax

D = 768
H = 12
HD = 64
FF = 3072
DD = 512
PIX = 768
SIDE = 14
VMIN = 20
VMAX = 78
SLOT = 80
IMG_DEV = 8
GRID = 196
IMAGES = 1024
N_ROLE = 2
N_DP = 64


def draw_visible_count(key, part):
    key = jax.random.fold_in(key, 11)
    first_key, second_key = jax.random.split(key)
    counts = jax.random.randint(first_key, (IMAGES,), VMIN, VMAX + 1)
    chosen = jax.random.randint(second_key, (2,), 0, IMAGES // 2)
    counts = counts.at[chosen[0]].set(VMAX)
    counts = counts.at[IMAGES // 2 + chosen[1]].set(VMIN)
    return counts.astype(jnp.int32)


def draw_encoded_image(key, part):
    key = jax.random.fold_in(key, 23)
    device_count = N_ROLE * N_DP
    scores = jax.random.randint(key, (device_count, IMG_DEV), 0, 1 << 20) * IMG_DEV + jnp.arange(IMG_DEV)[None, :]
    within = jnp.argsort(scores, axis=1).astype(jnp.int32)
    device = jnp.arange(device_count)[:, None]
    position = jnp.arange(IMG_DEV)[None, :]
    half_index = device // N_DP
    column = (device % N_DP + position) % N_DP
    target = (N_ROLE - 1 - half_index) * N_DP + column
    image = target * IMG_DEV + within[target, position]
    return image.reshape(-1).astype(jnp.int32)


def level_of(rng, shape, cuts, low, top_value):
    loudness = 1.0
    for axis_at, parts in cuts:
        draws = jax.random.uniform(jax.random.fold_in(jax.random.fold_in(rng, 6), axis_at), (parts,), jnp.float32, low / len(cuts), top_value / len(cuts))
        loudness = loudness * jnp.repeat(jnp.exp(draws), shape[axis_at] // parts).reshape((-1,) + (1,) * (len(shape) - 1 - axis_at))
    return loudness


def gaussian(stream_key, dims, spread, reach, cuts=(), kind=jnp.bfloat16):
    values = jax.random.normal(stream_key, dims, jnp.float32) * spread
    if len(cuts) > 0:
        values = level_of(stream_key, dims, cuts, -0.22, 0.18) * values
    return jnp.clip(values, min=-reach, max=reach).astype(kind)


def setup_inputs(seed: int = 0) -> dict:
    arg_keys = jax.random.split(jax.random.key(seed), 26)
    patch_rows = gaussian(arg_keys[0], (IMAGES * SLOT, D), 1.0, 6.0, ((0, 128),))
    patch_order = jax.vmap(lambda own: jax.random.permutation(own, GRID))(jax.random.split(arg_keys[1], IMAGES)).reshape((IMAGES, GRID)).astype(jnp.int32)
    visible_count = draw_visible_count(jax.random.fold_in(arg_keys[25], 71), 0)
    encoded_image = draw_encoded_image(jax.random.fold_in(arg_keys[25], 71), 0)
    first_gain = jnp.clip(1.0 + 0.1 * jax.random.normal(arg_keys[4], (D,), jnp.float32), 0.5, 1.5).astype(jnp.bfloat16)
    first_shift = gaussian(arg_keys[5], (D,), 0.3, 1.75, ((0, 128),))
    query_key_value = gaussian(arg_keys[6], (D, 3 * D), D ** -0.5, 0.21875, ((0, 128),))
    query_bias = gaussian(arg_keys[7], (D,), 0.3, 1.75, ((0, 128),))
    value_bias = gaussian(arg_keys[8], (D,), 0.3, 1.75, ((0, 128),))
    output_weight = gaussian(arg_keys[9], (D, D), (2 * D // (VMIN + VMAX)) ** -0.5, 1.5, ((0, 128),))
    output_bias = gaussian(arg_keys[10], (D,), 0.3, 1.75, ((0, 128),))
    second_gain = jnp.clip(1.0 + 0.1 * jax.random.normal(arg_keys[11], (D,), jnp.float32), 0.5, 1.5).astype(jnp.bfloat16)
    second_shift = gaussian(arg_keys[12], (D,), 0.3, 1.75, ((0, 128),))
    up_weight = gaussian(arg_keys[13], (D, FF), D ** -0.5, 0.21875, ((0, 128),))
    up_bias = gaussian(arg_keys[14], (FF,), 0.3, 1.75, ((0, 128),))
    down_weight = gaussian(arg_keys[15], (FF, D), FF ** -0.5, 0.109375, ((0, 128),))
    down_bias = gaussian(arg_keys[16], (D,), 0.3, 1.75, ((0, 128),))
    embed_weight = gaussian(arg_keys[17], (D, DD), D ** -0.5, 0.21875, ((0, 128),))
    embed_bias = gaussian(arg_keys[18], (DD,), 0.3, 1.75, ((0, 128),))
    mask_token = gaussian(arg_keys[19], (DD,), 1.0, 6.0, ((0, 128),))
    decoder_gain = jnp.clip(1.0 + 0.1 * jax.random.normal(arg_keys[20], (DD,), jnp.float32), 0.5, 1.5).astype(jnp.bfloat16)
    decoder_shift = gaussian(arg_keys[21], (DD,), 0.3, 1.75, ((0, 128),))
    pixel_weight = gaussian(arg_keys[22], (DD, PIX), DD ** -0.5, 0.25, ((0, 128),))
    pixel_bias = gaussian(arg_keys[23], (PIX,), 0.3, 1.75, ((0, 128),))
    pixel_grad = gaussian(arg_keys[24], (IMAGES, GRID, PIX), 1.0, 6.0, ((0, 128),))
    return dict(patch_rows=patch_rows, patch_order=patch_order, visible_count=visible_count, encoded_image=encoded_image, first_gain=first_gain, first_shift=first_shift, query_key_value=query_key_value, query_bias=query_bias, value_bias=value_bias, output_weight=output_weight, output_bias=output_bias, second_gain=second_gain, second_shift=second_shift, up_weight=up_weight, up_bias=up_bias, down_weight=down_weight, down_bias=down_bias, embed_weight=embed_weight, embed_bias=embed_bias, mask_token=mask_token, decoder_gain=decoder_gain, decoder_shift=decoder_shift, pixel_weight=pixel_weight, pixel_bias=pixel_bias, pixel_grad=pixel_grad)


@jax.custom_vjp
def low(v):
    return lax.optimization_barrier(v.astype(jnp.bfloat16)).astype(jnp.float32)

@jax.custom_vjp
def low_back(v):
    return v

def low_keep(v):
    return (low(v), None)

def low_pass(kept, grad):
    return (grad,)

def back_keep(v):
    return (v, None)

def back_low(kept, grad):
    return (low(grad),)
low.defvjp(low_keep, low_pass)
low_back.defvjp(back_keep, back_low)
epsilon = 1e-06
masked_score = -1e+30
highest = lax.Precision.HIGHEST

def layer_norm(values, gain, shift):
    average = lax.optimization_barrier(jnp.mean(values, axis=-1, keepdims=True))
    centered = values - average
    variance = lax.optimization_barrier(jnp.mean(centered * centered, axis=-1, keepdims=True))
    return centered * lax.rsqrt(variance + epsilon) * gain + shift

def positions():
    quarter = DD // 4
    frequency = 10000.0 ** (-jnp.arange(quarter, dtype=jnp.float32) / quarter)
    places = jnp.arange(GRID, dtype=jnp.int32)
    row_angle = (places // SIDE).astype(jnp.float32)[:, None] * frequency[None, :]
    col_angle = (places % SIDE).astype(jnp.float32)[:, None] * frequency[None, :]
    return jnp.concatenate([jnp.sin(row_angle), jnp.cos(row_angle), jnp.sin(col_angle), jnp.cos(col_angle)], axis=1)

def smooth_gate(values):
    return jax.nn.gelu(values, approximate=True)

def reference(patch_rows, patch_order, visible_count, encoded_image, first_gain, first_shift, query_key_value, query_bias, value_bias, output_weight, output_bias, second_gain, second_shift, up_weight, up_bias, down_weight, down_bias, embed_weight, embed_bias, mask_token, decoder_gain, decoder_shift, pixel_weight, pixel_bias, pixel_grad):
    image_count = encoded_image.shape[0]
    slot_count = visible_count[encoded_image]
    live = jnp.arange(SLOT, dtype=jnp.int32)[None, :] < slot_count[:, None]
    inverse = jnp.zeros((image_count,), jnp.int32).at[encoded_image].set(jnp.arange(image_count, dtype=jnp.int32))
    shown_order = patch_order[:, :SLOT]
    placement = ((shown_order[:, None, :] == jnp.arange(GRID, dtype=jnp.int32)[None, :, None]) & (jnp.arange(SLOT, dtype=jnp.int32)[None, None, :] < visible_count[:, None, None])).astype(jnp.float32)
    masked_share = 1.0 - lax.optimization_barrier(jnp.sum(placement, axis=2))
    table = positions()
    scale = HD ** (-0.5)

    def forward(patches, weights):
        gain_one, shift_one, mix_weight, bias_query, bias_value, out_weight, out_bias, gain_two, shift_two, hidden_weight, hidden_bias, back_weight, back_bias, emb_weight, emb_bias, token_mask, gain_three, shift_three, pix_weight, pix_bias = weights
        inputs = patches.reshape(image_count, SLOT, D)
        normed = low(layer_norm(inputs, gain_one, shift_one))
        bias_mix = jnp.concatenate([bias_query, jnp.zeros_like(bias_query), bias_value])
        mixed = low(low_back(jnp.einsum('std,de->ste', normed, mix_weight, precision=highest) + bias_mix))
        queries = mixed[..., :D].reshape(image_count, SLOT, H, HD)
        keys_all = mixed[..., D:2 * D].reshape(image_count, SLOT, H, HD)
        values_all = mixed[..., 2 * D:].reshape(image_count, SLOT, H, HD)
        scores = low_back(jnp.einsum('sqhe,skhe->shqk', queries, keys_all, precision=highest) * scale)
        scores = jnp.where(live[:, None, None, :], scores, masked_score)
        probs = low(jax.nn.softmax(scores, axis=-1))
        attended = jnp.einsum('shqk,skhe->sqhe', probs, values_all, precision=highest).reshape(image_count, SLOT, D)
        attended = low(low_back(attended))
        branch = low_back(jnp.einsum('sqd,de->sqe', attended, out_weight, precision=highest) + out_bias)
        resid = inputs + branch
        normed_two = low(layer_norm(resid, gain_two, shift_two))
        hidden = low_back(jnp.einsum('sqd,df->sqf', normed_two, hidden_weight, precision=highest) + hidden_bias)
        active = low(smooth_gate(hidden))
        branch_two = low_back(jnp.einsum('sqf,fd->sqd', active, back_weight, precision=highest) + back_bias)
        encoded = resid + branch_two
        embedded = low(low_back(jnp.einsum('sqd,dc->sqc', low(encoded), emb_weight, precision=highest) + emb_bias))
        by_image = embedded[inverse]
        grid = jnp.einsum('igt,itc->igc', placement, by_image, precision=highest) + masked_share[..., None] * token_mask + table[None]
        decoded = low(layer_norm(grid, gain_three, shift_three))
        return jnp.einsum('igc,cp->igp', decoded, pix_weight, precision=highest) + pix_bias
    weights = (first_gain, first_shift, query_key_value, query_bias, value_bias, output_weight, output_bias, second_gain, second_shift, up_weight, up_bias, down_weight, down_bias, embed_weight, embed_bias, mask_token, decoder_gain, decoder_shift, pixel_weight, pixel_bias)
    weights = tuple((item.astype(jnp.float32) for item in weights))
    pixels, pullback = jax.vjp(forward, patch_rows.astype(jnp.float32), weights)
    patch_back, grads = pullback(pixel_grad.astype(jnp.float32))
    return (pixels.astype(jnp.bfloat16), patch_back.astype(jnp.bfloat16), grads[0], grads[1], grads[2], grads[3], grads[4], grads[5], grads[6], grads[7], grads[8], grads[9], grads[10], grads[11], grads[12], grads[13], grads[14], grads[15], grads[16], grads[17], grads[18], grads[19])
```

```python
import jax
import jax.numpy as jnp
from jax import lax
from jax.sharding import Mesh
from jax.sharding import PartitionSpec as P

D = 768
H = 12
HD = 64
FF = 3072
DD = 512
PIX = 768
SIDE = 14
SLOT = 80
IMG_DEV = 8
GRID = 196
N_DP = 64
PART = FF // D

ALL = ("role", "y", "z", "x")

epsilon = 1e-06
masked_score = -1e30

def layer_norm(values, gain, shift):
    average = jnp.mean(values, axis=-1, keepdims=True)
    centered = values - average
    variance = jnp.mean(centered * centered, axis=-1, keepdims=True)
    return centered * lax.rsqrt(variance + epsilon) * gain + shift


def positions():
    quarter = DD // 4
    frequency = 10000.0 ** (-jnp.arange(quarter, dtype=jnp.float32) / quarter)
    places = jnp.arange(GRID, dtype=jnp.int32)
    row_angle = (places // SIDE).astype(jnp.float32)[:, None] * frequency[None, :]
    col_angle = (places % SIDE).astype(jnp.float32)[:, None] * frequency[None, :]
    return jnp.concatenate(
        [jnp.sin(row_angle), jnp.cos(row_angle), jnp.sin(col_angle), jnp.cos(col_angle)], axis=1
    )


def smooth_gate(values):
    return jax.nn.gelu(values, approximate=True)


def transpose_dot(left, right):
    return lax.dot_general(
        left, right, (((0,), (0,)), ((), ())), preferred_element_type=jnp.float32
    )


def dot_right(left, right):
    return lax.dot_general(
        left, right, (((1,), (1,)), ((), ())), preferred_element_type=jnp.float32
    )


def plain_dot(left, right):
    return jnp.dot(left, right, preferred_element_type=jnp.float32)


def column_sum(values):
    return jnp.sum(values.astype(jnp.float32), axis=0)


PAIRS = {
    "high": [(0, 3), (3, 0), (1, 2), (2, 1)],
    "low": [(0, 1), (1, 0), (2, 3), (3, 2)],
}


def halve(state, axis, dim, which):
    at = lax.axis_index(axis)
    bit = at // 2 if which == "high" else at % 2
    half = state.shape[dim] // 2
    kept = lax.dynamic_slice_in_dim(state, bit * half, half, dim)
    sent = lax.dynamic_slice_in_dim(state, (1 - bit) * half, half, dim)
    came = lax.ppermute(sent, axis, PAIRS[which])
    return kept.astype(jnp.float32) + came.astype(jnp.float32)


def scatter_sum(whole, order):
    columns = whole.shape[1]
    role = lax.axis_index("role")
    half = D // 2
    kept = lax.dynamic_slice_in_dim(whole, role * half, half, 0)
    sent = lax.dynamic_slice_in_dim(whole, (1 - role) * half, half, 0)
    came = lax.ppermute(sent, "role", [(0, 1), (1, 0)])
    state = (kept.astype(jnp.float32) + came.astype(jnp.float32)).astype(jnp.bfloat16)
    state = state.reshape(4, 4, 24, columns)
    for axis in order:
        dim = 0 if axis == "y" else 1
        for which in ("high", "low"):
            state = halve(state, axis, dim, which).astype(jnp.bfloat16)
    state = state.reshape(4, 6, columns)
    state = halve(state, "x", 0, "high").astype(jnp.bfloat16)
    return halve(state, "x", 0, "low").reshape(6, columns)


def layer_norm_back(values, gain, upstream):
    average = jnp.mean(values, axis=-1, keepdims=True)
    centered = values - average
    variance = jnp.mean(centered * centered, axis=-1, keepdims=True)
    inverse = lax.rsqrt(variance + epsilon)
    h = centered * inverse
    dh = upstream * gain
    dv = (
        dh
        - jnp.mean(dh, axis=-1, keepdims=True)
        - h * jnp.mean(dh * h, axis=-1, keepdims=True)
    ) * inverse
    lead = tuple(range(values.ndim - 1))
    return dv, jnp.sum(upstream * h, axis=lead), jnp.sum(upstream, axis=lead)


def body(
    patch_rows,
    patch_order,
    visible_count,
    encoded_image,
    first_gain,
    first_shift,
    query_key_value,
    query_bias,
    value_bias,
    output_weight,
    output_bias,
    second_gain,
    second_shift,
    up_weight,
    up_bias,
    down_weight,
    down_bias,
    embed_weight,
    embed_bias,
    mask_token,
    decoder_gain,
    decoder_shift,
    pixel_weight,
    pixel_bias,
    pixel_grad,
):
    device = lax.axis_index(ALL)
    n_dev = 2 * N_DP
    small = jnp.concatenate([embed_bias, mask_token, decoder_gain, decoder_shift])
    small = jnp.pad(small, (0, 2)).reshape(6, 3)
    vectors = jnp.stack(
        [
            first_gain,
            first_shift,
            query_bias,
            value_bias,
            output_bias,
            second_gain,
            second_shift,
            down_bias,
            pixel_bias,
        ],
        axis=1,
    )
    packed = jnp.concatenate(
        [
            query_key_value,
            output_weight,
            up_weight.reshape(6, D, PART).transpose(0, 2, 1).reshape(6, FF),
            down_weight.reshape(6, FF),
            embed_weight,
            pixel_weight.reshape(6, DD),
            vectors,
            up_bias.reshape(6, PART),
            small,
            jnp.zeros((6, 112), jnp.bfloat16),
        ],
        axis=1,
    )
    whole = lax.all_gather(packed, "x", tiled=True)
    whole = lax.all_gather(whole, ("role", "y", "z"), tiled=True)
    at = 0

    def take(width):
        nonlocal at
        at += width
        return whole[:, at - width : at]

    mix_weight = take(3 * D)
    out_weight = take(D)
    hidden_weight = take(FF)
    back_weight = jnp.concatenate([take(D) for _ in range(PART)], axis=0)
    emb_weight = take(DD)
    pix_weight = take(DD).reshape(DD, PIX)
    rest = take(128)[:, :16].astype(jnp.float32)
    rows = rest.T
    gain_one, shift_one, bias_query, bias_value, out_bias, gain_two, shift_two, back_bias, pix_bias = (
        rows[k] for k in range(9)
    )
    hidden_bias = rows[9:13].reshape(FF)
    fours = rest[:, 13:16].reshape(n_dev, 18)[:, :16].reshape(n_dev, 4, 4)
    fours = fours.transpose(1, 0, 2).reshape(4, DD)
    emb_bias, token_mask, gain_three, shift_three = (fours[k] for k in range(4))

    row_count = IMG_DEV * SLOT
    image_count = encoded_image.shape[0]
    scale = HD ** (-0.5)
    held = lax.dynamic_slice_in_dim(encoded_image, device * IMG_DEV, IMG_DEV)
    held_count = visible_count[held]
    held_order = patch_order[held][:, :SLOT]
    live_slot = jnp.arange(SLOT, dtype=jnp.int32)[None, :] < held_count[:, None]

    own_images = device * IMG_DEV + jnp.arange(IMG_DEV, dtype=jnp.int32)
    found = encoded_image[None, :] == own_images[:, None]
    source_slot = jnp.sum(
        jnp.where(found, jnp.arange(image_count, dtype=jnp.int32)[None, :], 0), axis=1
    )
    source_place = source_slot % IMG_DEV
    image_of = jnp.sum(
        jnp.where(
            source_place[None, :] == jnp.arange(IMG_DEV, dtype=jnp.int32)[:, None],
            jnp.arange(IMG_DEV, dtype=jnp.int32)[None, :],
            0,
        ),
        axis=1,
    )

    def across(step):
        return [
            (r * N_DP + p, (1 - r) * N_DP + (p + step) % N_DP) for r in range(2) for p in range(N_DP)
        ]

    upstream = jnp.stack(
        [
            lax.ppermute(
                lax.dynamic_index_in_dim(pixel_grad, image_of[s], 0, keepdims=False), ALL, across(-s)
            )
            for s in range(IMG_DEV)
        ]
    )

    shape_four = (IMG_DEV, SLOT, H, HD)
    inputs = patch_rows.astype(jnp.float32)
    normed_low = layer_norm(inputs, gain_one, shift_one).astype(jnp.bfloat16)
    bias_mix = jnp.concatenate([bias_query, jnp.zeros((D,), jnp.float32), bias_value])
    mixed = (plain_dot(normed_low, mix_weight) + bias_mix).astype(jnp.bfloat16)
    queries = mixed[:, :D].reshape(shape_four)
    keys_all = mixed[:, D : 2 * D].reshape(shape_four)
    values_all = mixed[:, 2 * D :].reshape(shape_four)
    raw_scores = (
        jnp.einsum("sqhe,skhe->shqk", queries, keys_all, preferred_element_type=jnp.float32) * scale
    )
    scores = jnp.where(live_slot[:, None, None, :], raw_scores, masked_score)
    probs = jax.nn.softmax(scores, axis=-1)
    probs_low = probs.astype(jnp.bfloat16)
    attended = (
        jnp.einsum("shqk,skhe->sqhe", probs_low, values_all, preferred_element_type=jnp.float32)
        .reshape(row_count, D)
        .astype(jnp.bfloat16)
    )
    resid = inputs + (plain_dot(attended, out_weight) + out_bias)
    normed_two_low = layer_norm(resid, gain_two, shift_two).astype(jnp.bfloat16)
    hidden = plain_dot(normed_two_low, hidden_weight) + hidden_bias
    active_low = smooth_gate(hidden).astype(jnp.bfloat16)
    encoded = resid + (plain_dot(active_low, back_weight) + back_bias)
    encoded_low = encoded.astype(jnp.bfloat16)
    embedded = (plain_dot(encoded_low, emb_weight) + emb_bias).astype(jnp.bfloat16)
    blocks = embedded.reshape(IMG_DEV, SLOT, DD)
    placement = (
        held_order[:, None, :] == jnp.arange(GRID, dtype=jnp.int32)[None, :, None]
    ) & live_slot[:, None, :]
    place_low = placement.astype(jnp.bfloat16)
    masked_share = 1.0 - jnp.sum(placement.astype(jnp.float32), axis=2)
    grid = (
        jnp.einsum("pgt,ptc->pgc", place_low, blocks, preferred_element_type=jnp.float32)
        + masked_share[..., None] * token_mask
        + positions()[None]
    )
    decoded_low = layer_norm(grid, gain_three, shift_three).astype(jnp.bfloat16)
    pixels_held = (
        jnp.einsum("pgc,cx->pgx", decoded_low, pix_weight, preferred_element_type=jnp.float32)
        + pix_bias
    ).astype(jnp.bfloat16)
    pixels = jnp.zeros((IMG_DEV, GRID, PIX), jnp.bfloat16)
    for s in range(IMG_DEV):
        came = lax.ppermute(pixels_held[s], ALL, across(s))
        pixels = lax.dynamic_update_index_in_dim(pixels, came, image_of[s], 0)

    grad_pixel_weight = jnp.einsum(
        "pgc,pgx->cx", decoded_low, upstream, preferred_element_type=jnp.float32
    )
    grad_pixel_bias = jnp.sum(upstream.astype(jnp.float32), axis=(0, 1))
    grad_decoded = jnp.einsum(
        "pgx,cx->pgc", upstream, pix_weight, preferred_element_type=jnp.float32
    )
    grad_grid, grad_decoder_gain, grad_decoder_shift = layer_norm_back(grid, gain_three, grad_decoded)
    grad_mask_token = jnp.sum(masked_share[..., None] * grad_grid, axis=(0, 1))
    grad_embedded = (
        jnp.einsum(
            "pgt,pgc->ptc",
            place_low,
            grad_grid.astype(jnp.bfloat16),
            preferred_element_type=jnp.float32,
        )
        .astype(jnp.bfloat16)
        .reshape(row_count, DD)
    )
    grad_embed_weight = transpose_dot(encoded_low, grad_embedded)
    grad_embed_bias = column_sum(grad_embedded)
    grad_encoded = dot_right(grad_embedded, emb_weight)
    grad_branch_two = grad_encoded.astype(jnp.bfloat16)
    grad_down_weight = [
        transpose_dot(active_low[:, j * D : (j + 1) * D], grad_branch_two) for j in range(PART)
    ]
    group_one = jnp.concatenate(
        [
            g.astype(jnp.bfloat16)
            for g in grad_down_weight + [grad_embed_weight, grad_pixel_weight.reshape(D, DD)]
        ],
        axis=1,
    )
    shard_one = scatter_sum(group_one, "yz")
    grad_down_bias = column_sum(grad_branch_two)
    grad_active = dot_right(grad_branch_two, back_weight)
    gate_back = jax.vjp(smooth_gate, hidden)[1]
    grad_hidden = gate_back(grad_active)[0].astype(jnp.bfloat16)
    grad_up_weight = transpose_dot(normed_two_low, grad_hidden)
    grad_up_bias = column_sum(grad_hidden)
    grad_normed_two = dot_right(grad_hidden, hidden_weight)
    grad_resid_part, grad_second_gain, grad_second_shift = layer_norm_back(
        resid, gain_two, grad_normed_two
    )
    grad_resid = grad_encoded + grad_resid_part
    grad_branch = grad_resid.astype(jnp.bfloat16)
    grad_output_weight = transpose_dot(attended, grad_branch)
    group_two = jnp.concatenate(
        [grad_up_weight.astype(jnp.bfloat16), grad_output_weight.astype(jnp.bfloat16)], axis=1
    )
    shard_two = scatter_sum(group_two, "zy")
    grad_output_bias = column_sum(grad_branch)
    grad_attended = dot_right(grad_branch, out_weight).astype(jnp.bfloat16).reshape(shape_four)
    grad_probs = jnp.einsum(
        "sqhe,skhe->shqk", grad_attended, values_all, preferred_element_type=jnp.float32
    )
    grad_values = jnp.einsum(
        "shqk,sqhe->skhe", probs_low, grad_attended, preferred_element_type=jnp.float32
    )
    grad_scores = (
        probs * (grad_probs - jnp.sum(probs * grad_probs, axis=-1, keepdims=True))
    ).astype(jnp.bfloat16)
    grad_queries = (
        jnp.einsum("shqk,skhe->sqhe", grad_scores, keys_all, preferred_element_type=jnp.float32)
        * scale
    )
    grad_keys = (
        jnp.einsum("shqk,sqhe->skhe", grad_scores, queries, preferred_element_type=jnp.float32)
        * scale
    )
    grad_mixed = jnp.concatenate(
        [
            grad_queries.reshape(row_count, D),
            grad_keys.reshape(row_count, D),
            grad_values.reshape(row_count, D),
        ],
        axis=1,
    ).astype(jnp.bfloat16)
    grad_mix_weight = transpose_dot(normed_low, grad_mixed)
    grad_query_bias = column_sum(grad_mixed[:, :D])
    grad_value_bias = column_sum(grad_mixed[:, 2 * D :])
    grad_normed = dot_right(grad_mixed, mix_weight)
    grad_input_part, grad_first_gain, grad_first_shift = layer_norm_back(
        inputs, gain_one, grad_normed
    )
    patch_grad = (grad_resid + grad_input_part).astype(jnp.bfloat16)
    nines = jnp.stack(
        [
            grad_first_gain,
            grad_first_shift,
            grad_query_bias,
            grad_value_bias,
            grad_output_bias,
            grad_second_gain,
            grad_second_shift,
            grad_down_bias,
            grad_pixel_bias,
        ]
    )
    fours = jnp.stack([grad_embed_bias, grad_mask_token, grad_decoder_gain, grad_decoder_shift])
    fours = fours.reshape(4, n_dev, 4).transpose(1, 0, 2).reshape(n_dev, 16)
    fours = jnp.pad(fours, ((0, 0), (0, 2))).reshape(D, 3)
    rows = jnp.concatenate([nines, grad_up_bias.reshape(PART, D)]).T
    group_three = jnp.concatenate(
        [
            grad_mix_weight.astype(jnp.bfloat16),
            rows.astype(jnp.bfloat16),
            fours.astype(jnp.bfloat16),
            jnp.zeros((D, 112), jnp.bfloat16),
        ],
        axis=1,
    )
    shard_three = scatter_sum(group_three, "yz")
    vec = shard_three[:, 3 * D :]
    tail = vec[:, 13:16].reshape(18)
    return (
        pixels,
        patch_grad,
        vec[:, 0],
        vec[:, 1],
        shard_three[:, : 3 * D],
        vec[:, 2],
        vec[:, 3],
        shard_two[:, FF:],
        vec[:, 4],
        vec[:, 5],
        vec[:, 6],
        shard_two[:, :FF].reshape(6, PART, D).transpose(0, 2, 1).reshape(6, FF),
        vec[:, 9:13].reshape(6 * PART),
        shard_one[:, :FF].reshape(6 * PART, D),
        vec[:, 7],
        shard_one[:, FF : FF + DD],
        tail[0:4],
        tail[4:8],
        tail[8:12],
        tail[12:16],
        shard_one[:, FF + DD :].reshape(4, PIX),
        vec[:, 8],
    )


def solution(mesh):
    mesh = Mesh(mesh.devices.reshape(2, 4, 4, 4), ALL)
    two, one = P(ALL, None), P(ALL)
    placed = (two, P(), P(), P(), one, one, two, one, one, two, one, one, one, two, one, two, one)
    placed += (two, one, one, one, one, two, one, P(ALL, None, None))
    given = (P(ALL, None, None), two, one, one, two, one, one, two, one, one, one, two, one, two, one)
    given += (two, one, one, one, one, two, one)
    return jax.shard_map(body, mesh=mesh, in_specs=placed, out_specs=given, check_vma=False)
```

```python
import functools

import jax
import jax.numpy as jnp
from jax import lax
from jax.experimental import pallas as pl
from jax.experimental.pallas import tpu as pltpu
from jax.sharding import Mesh
from jax.sharding import PartitionSpec as P

D = 768
H = 12
HD = 64
FF = 3072
DD = 512
PIX = 768
SIDE = 14
SLOT = 80
IMG_DEV = 8
GRID = 196
N_DP = 64
PART = FF // D

ALL = ("role", "y", "z", "x")

epsilon = 1e-06
masked_score = -1e30

def positions():
    quarter = DD // 4
    frequency = 10000.0 ** (-jnp.arange(quarter, dtype=jnp.float32) / quarter)
    places = jnp.arange(GRID, dtype=jnp.int32)
    row_angle = (places // SIDE).astype(jnp.float32)[:, None] * frequency[None, :]
    col_angle = (places % SIDE).astype(jnp.float32)[:, None] * frequency[None, :]
    return jnp.concatenate(
        [jnp.sin(row_angle), jnp.cos(row_angle), jnp.sin(col_angle), jnp.cos(col_angle)], axis=1
    )


HALF = D // 2
ROWS = IMG_DEV * SLOT
CHUNK = ROWS // 2
OUT_AT, UP_AT, DOWN_AT, EMB_AT, PIX_AT, VEC_AT = 3 * D, 4 * D, 8 * D, 12 * D, 12 * D + DD, 12 * D + 2 * DD
WIDE = VEC_AT + 128
G1, S1, QB, VB, OB, G2, S2, DB, PB, UB = range(10)
EB, TOK, G3, S3 = range(4)

MIB = 1 << 20


def cost(us):
    return pl.CostEstimate(flops=int(us * 1e9), bytes_accessed=0, transcendentals=0)


def params(mib):
    return pltpu.CompilerParams(
        dimension_semantics=("arbitrary",), vmem_limit_bytes=mib * MIB
    )


def const(*shape):
    return pl.BlockSpec(shape, lambda i, *_: (0,) * len(shape))


def columns(width, at):
    return pl.BlockSpec((D, width), lambda i, *_: (0, at // width))


def tile_columns(at):
    return pl.BlockSpec((D, D), lambda i, *_: (0, at // D + i))


def dot_nn(a, b):
    return lax.dot_general(a, b, (((1,), (0,)), ((), ())), preferred_element_type=jnp.float32)


def dot_nt(a, b):
    return lax.dot_general(a, b, (((1,), (1,)), ((), ())), preferred_element_type=jnp.float32)


def dot_tn(a, b):
    return lax.dot_general(a, b, (((0,), (0,)), ((), ())), preferred_element_type=jnp.float32)


def normalised(values):
    average = jnp.mean(values, axis=-1, keepdims=True)
    centered = values - average
    variance = jnp.mean(centered * centered, axis=-1, keepdims=True)
    inverse = lax.rsqrt(variance + epsilon)
    return centered * inverse, inverse


def norm_back(values, gain, upstream):
    h, inverse = normalised(values)
    dh = upstream * gain
    dv = (
        dh - jnp.mean(dh, axis=-1, keepdims=True) - h * jnp.mean(dh * h, axis=-1, keepdims=True)
    ) * inverse
    return (
        dv,
        jnp.sum(upstream * h, axis=0, keepdims=True),
        jnp.sum(upstream, axis=0, keepdims=True),
    )


def strips(count, body, size=16, at_once=10):
    def some(i, carry):
        for n in range(at_once):
            body(pl.ds(pl.multiple_of((i * at_once + n) * size, size), size))
        return carry

    lax.fori_loop(0, count // (at_once * size), some, 0)


def spread():
    row = lax.broadcasted_iota(jnp.int32, (D, DD), 0)
    col = lax.broadcasted_iota(jnp.int32, (D, DD), 1)
    return (row == 6 * (col // 4) + col % 4).astype(jnp.bfloat16)


def head_masks():
    lane = lax.broadcasted_iota(jnp.int32, (1, 2 * HD), 1)
    low = (lane < HD).astype(jnp.bfloat16)
    return low, (1.0 - low.astype(jnp.float32)).astype(jnp.bfloat16)


def stacked(pair, masks):
    return jnp.concatenate([pair * masks[0], pair * masks[1]], axis=0)


def key_probs(scores, live):
    both = []
    for k in range(2):
        s = jnp.where(live, scores[SLOT * k : SLOT * k + SLOT] * HD ** (-0.5), masked_score)
        e = jnp.exp(s - jnp.max(s, axis=0, keepdims=True))
        both.append(e * (1.0 / jnp.sum(e, axis=0, keepdims=True)))
    return both


def attention_kernel(count_ref, x_ref, w_ref, vec_ref, normed_ref, mixed_ref, att_ref, rows_ref, fours_ref, held):
    step = pl.program_id(0)

    @pl.when(step == 0)
    def _():
        turned = vec_ref[...].astype(jnp.float32).T
        rows_ref[...] = turned[:24]
        fours_ref[...] = dot_nn(turned[16:24].astype(jnp.bfloat16), spread())

    def norm(at):
        h, _ = normalised(x_ref[at].astype(jnp.float32))
        normed_ref[at] = (h * rows_ref[G1 : G1 + 1] + rows_ref[S1 : S1 + 1]).astype(jnp.bfloat16)

    strips(CHUNK, norm)
    for part, bias in ((0, QB), (1, None), (2, VB)):
        m = dot_nn(normed_ref[...], w_ref[:, part * D : part * D + D])
        if bias is not None:
            m = m + rows_ref[bias : bias + 1]
        mixed_ref[:, part * D : part * D + D] = m.astype(jnp.bfloat16)
    masks = head_masks()
    place = lax.broadcasted_iota(jnp.int32, (SLOT, SLOT), 0)

    def one_slot(s, carry):
        at = pl.ds(pl.multiple_of(s * SLOT, SLOT), SLOT)
        live = place < count_ref[step * (CHUNK // SLOT) + s]
        for pair in range(H // 2):
            c = pair * 128
            keys = stacked(mixed_ref[at, D + c : D + c + 128], masks)
            held[pair] = dot_nt(keys, mixed_ref[at, c : c + 128])
        for pair in range(H // 2):
            c = pair * 128
            probs = jnp.concatenate(key_probs(held[pair], live), axis=0).astype(jnp.bfloat16)
            values = stacked(mixed_ref[at, 2 * D + c : 2 * D + c + 128], masks)
            att_ref[at, c : c + 128] = dot_tn(probs, values).astype(jnp.bfloat16)
        return carry

    lax.fori_loop(0, CHUNK // SLOT, one_slot, 0)


def attention(count, patch_rows, whole):
    rows = pl.BlockSpec((CHUNK, D), lambda i: (i, 0))
    return pl.pallas_call(
        attention_kernel,
        grid=(2,),
        in_specs=[
            pl.BlockSpec(memory_space=pltpu.SMEM),
            rows,
            columns(3 * D, 0),
            columns(128, VEC_AT),
        ],
        out_specs=[rows, pl.BlockSpec((CHUNK, 3 * D), lambda i: (i, 0)), rows, const(24, D), const(8, DD)],
        out_shape=[
            jax.ShapeDtypeStruct((ROWS, D), jnp.bfloat16),
            jax.ShapeDtypeStruct((ROWS, 3 * D), jnp.bfloat16),
            jax.ShapeDtypeStruct((ROWS, D), jnp.bfloat16),
            jax.ShapeDtypeStruct((24, D), jnp.float32),
            jax.ShapeDtypeStruct((8, DD), jnp.float32),
        ],
        scratch_shapes=[pltpu.VMEM((H // 2, 2 * SLOT, SLOT), jnp.float32)],
        compiler_params=params(48),
        cost_estimate=cost(11),
        name="attention",
    )(count, patch_rows, whole, whole)


GELU_C = 0.7978845608028654


def in_halves(kernel, half, earlier, in_specs, out_specs, out_shape, shared, mib, name, scratch, args):
    aliases = {}
    if earlier is not None:
        n = len(args)
        inner = kernel

        def kernel(*refs):
            return inner(*refs[:n], *refs[n + len(shared) :])

        aliases = {n + i: out for i, out in enumerate(shared)}
        in_specs = in_specs + [pl.BlockSpec(memory_space=pl.ANY)] * len(shared)
        args = args + [earlier[out] for out in shared]
    return pl.pallas_call(
        kernel,
        grid=(PART,),
        in_specs=in_specs,
        out_specs=out_specs,
        out_shape=out_shape,
        scratch_shapes=scratch,
        input_output_aliases=aliases,
        compiler_params=params(mib),
        cost_estimate=cost(11),
        name=name,
    )(*args)


def rows_of(half, width):
    return pl.BlockSpec((CHUNK, width), lambda j: (half, 0))


def tile_of(half):
    return pl.BlockSpec((CHUNK, D), lambda j: (half, j))


def forward_kernel(x_ref, att_ref, wo_ref, wu_ref, wd_ref, we_ref, rows_ref, fours_ref,
                   resid_ref, n2_ref, act_ref, slope_ref, enc_ref, emb_ref, total):
    j = pl.program_id(0)

    @pl.when(j == 0)
    def _():
        resid = x_ref[...].astype(jnp.float32) + (
            dot_nn(att_ref[...], wo_ref[...]) + rows_ref[OB : OB + 1]
        )
        resid_ref[...] = resid
        h, _ = normalised(resid)
        n2_ref[...] = (h * rows_ref[G2 : G2 + 1] + rows_ref[S2 : S2 + 1]).astype(jnp.bfloat16)
        total[...] = resid + rows_ref[DB : DB + 1]

    v = dot_nn(n2_ref[...], wu_ref[...]) + rows_ref[pl.ds(UB + j, 1)]
    square = v * v
    t = jnp.tanh(v * (GELU_C + 0.044715 * GELU_C * square))
    lift = 0.5 + 0.5 * t
    active = v * lift
    act_ref[...] = active.astype(jnp.bfloat16)
    slope_ref[...] = (
        lift + active * (1.0 - t) * (GELU_C + 3 * 0.044715 * GELU_C * square)
    ).astype(jnp.bfloat16)
    total[...] += dot_nn(act_ref[...], wd_ref[...])

    @pl.when(j == PART - 1)
    def _():
        enc_ref[...] = total[...].astype(jnp.bfloat16)
        emb_ref[...] = (dot_nn(enc_ref[...], we_ref[...]) + fours_ref[EB : EB + 1]).astype(jnp.bfloat16)


def forward(half, earlier, patch_rows, attended, whole, rows, fours):
    return in_halves(
        forward_kernel,
        half,
        earlier,
        [
            rows_of(half, D),
            rows_of(half, D),
            columns(D, OUT_AT),
            tile_columns(UP_AT),
            tile_columns(DOWN_AT),
            columns(DD, EMB_AT),
            const(24, D),
            const(8, DD),
        ],
        [rows_of(half, D), rows_of(half, D), tile_of(half), tile_of(half), rows_of(half, D), const(CHUNK, DD)],
        [
            jax.ShapeDtypeStruct((ROWS, D), jnp.float32),
            jax.ShapeDtypeStruct((ROWS, D), jnp.bfloat16),
            jax.ShapeDtypeStruct((ROWS, FF), jnp.bfloat16),
            jax.ShapeDtypeStruct((ROWS, FF), jnp.bfloat16),
            jax.ShapeDtypeStruct((ROWS, D), jnp.bfloat16),
            jax.ShapeDtypeStruct((CHUNK, DD), jnp.bfloat16),
        ],
        (0, 1, 2, 3, 4),
        48,
        "forward",
        [pltpu.VMEM((CHUNK, D), jnp.float32)],
        [patch_rows, attended, whole, whole, whole, whole, rows, fours],
    )


def grid_kernel(image_ref, count_ref, order_ref, emb_ref, table_ref, w_ref, fours_ref, up_ref, start_ref,
                gemb_ref, dec_ref, dvec_ref):
    s = pl.program_id(0)
    cell = lax.broadcasted_iota(jnp.int32, (GRID, SLOT), 0)
    place = lax.broadcasted_iota(jnp.int32, (GRID, SLOT), 1)
    placed = jnp.where((order_ref[0] == cell) & (place < count_ref[s]), 1.0, 0.0)
    masked = 1.0 - jnp.sum(placed, axis=1, keepdims=True)
    placed = placed.astype(jnp.bfloat16)
    grid = dot_nn(placed, emb_ref[0]) + masked * fours_ref[TOK : TOK + 1] + table_ref[...]
    gain = fours_ref[G3 : G3 + 1]
    h, inverse = normalised(grid)
    dec_ref[0] = (h * gain + fours_ref[S3 : S3 + 1]).astype(jnp.bfloat16)
    grad = dot_nt(up_ref[0], w_ref[...])
    dh = grad * gain
    back = (
        dh - jnp.mean(dh, axis=-1, keepdims=True) - h * jnp.mean(dh * h, axis=-1, keepdims=True)
    ) * inverse
    gemb_ref[0] = dot_tn(placed, back.astype(jnp.bfloat16)).astype(jnp.bfloat16)

    @pl.when(s == 0)
    def _():
        dvec_ref[...] = start_ref[...]

    dvec_ref[...] += jnp.concatenate(
        [
            jnp.zeros((1, DD), jnp.float32),
            jnp.sum(masked * back, axis=0, keepdims=True),
            jnp.sum(grad * h, axis=0, keepdims=True),
            jnp.sum(grad, axis=0, keepdims=True),
            jnp.zeros((4, DD), jnp.float32),
        ],
        axis=0,
    )


def block(*shape):
    return pl.BlockSpec((1, *shape), lambda s, *_: (s, 0, 0))


def of_image(*shape):
    return pl.BlockSpec((1, *shape), lambda s, image, *_: (image[s], 0, 0))


def decoder_grid(image, count, order, embedded, table, pix_weight, fours, pixel_grad, start):
    n = image.shape[0]
    return pl.pallas_call(
        grid_kernel,
        grid_spec=pltpu.PrefetchScalarGridSpec(
            num_scalar_prefetch=2,
            grid=(n,),
            in_specs=[
                block(1, SLOT),
                block(SLOT, DD),
                const(GRID, DD),
                const(DD, PIX),
                const(8, DD),
                of_image(GRID, PIX),
                const(8, DD),
            ],
            out_specs=[block(SLOT, DD), block(GRID, DD), const(8, DD)],
        ),
        out_shape=[
            jax.ShapeDtypeStruct((n, SLOT, DD), jnp.bfloat16),
            jax.ShapeDtypeStruct((n, GRID, DD), jnp.bfloat16),
            jax.ShapeDtypeStruct((8, DD), jnp.float32),
        ],
        compiler_params=params(32),
        cost_estimate=cost(n),
        name="decoder_grid",
    )(image, count, order, embedded, table, pix_weight, fours, pixel_grad, start)


def pixel_kernel(image_ref, dec_ref, up_ref, w_ref, rows_ref, start_ref, bias_ref, *refs):
    pix_ref, dw_ref, dbias_ref = refs[-3:]
    s = pl.program_id(0)
    pix_ref[0] = (dot_nn(dec_ref[0], w_ref[...]) + rows_ref[PB : PB + 1]).astype(jnp.bfloat16)
    dw = dot_tn(dec_ref[0], up_ref[0])
    dbias = jnp.sum(up_ref[0].astype(jnp.float32), axis=0, keepdims=True)

    @pl.when(s == 0)
    def _():
        dw_ref[...] = start_ref[...] + dw
        dbias_ref[...] = bias_ref[...] + dbias

    @pl.when(s > 0)
    def _():
        dw_ref[...] += dw
        dbias_ref[...] += dbias


def decoder_pixels(image, decoded, pixel_grad, pix_weight, rows, start, bias, pixels=None):
    n = image.shape[0]
    args = [image, decoded, pixel_grad, pix_weight, rows, start, bias]
    specs = [block(GRID, DD), of_image(GRID, PIX), const(DD, PIX), const(24, D), const(DD, PIX), const(1, PIX)]
    if pixels is not None:
        args.append(pixels)
        specs.append(pl.BlockSpec(memory_space=pl.ANY))
    return pl.pallas_call(
        pixel_kernel,
        grid_spec=pltpu.PrefetchScalarGridSpec(
            num_scalar_prefetch=1,
            grid=(n,),
            in_specs=specs,
            out_specs=[of_image(GRID, PIX), const(DD, PIX), const(1, PIX)],
        ),
        out_shape=[
            jax.ShapeDtypeStruct((IMG_DEV, GRID, PIX), jnp.bfloat16),
            jax.ShapeDtypeStruct((DD, PIX), jnp.float32),
            jax.ShapeDtypeStruct((1, PIX), jnp.float32),
        ],
        input_output_aliases={} if pixels is None else {7: 0},
        compiler_params=params(32),
        cost_estimate=cost(0.8 * n),
        name="decoder_pixels",
    )(*args)


def with_role(kernel, grid, in_specs, out_specs, out_shape, mib, name, scratch=()):
    return pl.pallas_call(
        kernel,
        grid_spec=pltpu.PrefetchScalarGridSpec(
            num_scalar_prefetch=1,
            grid=grid,
            in_specs=in_specs,
            out_specs=out_specs,
            scratch_shapes=list(scratch),
        ),
        out_shape=out_shape,
        compiler_params=params(mib),
        cost_estimate=cost(10),
        name=name,
    )


def half_columns(mine):
    return pl.BlockSpec((ROWS, HALF), lambda i, role: (0, role[0] if mine else 1 - role[0]))


def half_tiles(mine):
    return pl.BlockSpec(
        (ROWS, HALF), lambda i, role: (0, 2 * i + (role[0] if mine else 1 - role[0]))
    )


C_ONE, C_TWO, C_THREE = FF + 2 * DD, FF + D, 3 * D + 128


def down_grad_kernel(role_ref, gemb_ref, gb2_ref, enc_mine, enc_other, act_mine, act_other, pix_mine, pix_other,
                     mine_ref, other_ref, dbias_ref, demb_ref):
    j = pl.program_id(0)

    @pl.when(j == 0)
    def _():
        dbias_ref[...] = jnp.sum(gb2_ref[...].astype(jnp.float32), axis=0, keepdims=True)
        demb_ref[...] = jnp.sum(gemb_ref[...].astype(jnp.float32), axis=0, keepdims=True)
        for ref, enc, pix in ((mine_ref, enc_mine, pix_mine), (other_ref, enc_other, pix_other)):
            ref[:, FF : FF + DD] = dot_tn(enc[...], gemb_ref[...]).astype(jnp.bfloat16)
            ref[:, FF + DD :] = pix[...]

    at = pl.ds(pl.multiple_of(j * D, D), D)
    mine_ref[:, at] = dot_tn(act_mine[...], gb2_ref[...]).astype(jnp.bfloat16)
    other_ref[:, at] = dot_tn(act_other[...], gb2_ref[...]).astype(jnp.bfloat16)


def down_grad(role, gemb, gb2, enc, act, dpix):
    return with_role(
        down_grad_kernel,
        (PART,),
        [
            const(ROWS, DD),
            const(ROWS, D),
            half_columns(True),
            half_columns(False),
            half_tiles(True),
            half_tiles(False),
            pl.BlockSpec((HALF, DD), lambda i, role: (role[0], 0)),
            pl.BlockSpec((HALF, DD), lambda i, role: (1 - role[0], 0)),
        ],
        [const(HALF, C_ONE), const(HALF, C_ONE), const(1, D), const(1, DD)],
        [
            jax.ShapeDtypeStruct((HALF, C_ONE), jnp.bfloat16),
            jax.ShapeDtypeStruct((HALF, C_ONE), jnp.bfloat16),
            jax.ShapeDtypeStruct((1, D), jnp.float32),
            jax.ShapeDtypeStruct((1, DD), jnp.float32),
        ],
        48,
        "down_grad",
    )(role, gemb, gb2, enc, enc, act, act, dpix, dpix)


def hidden_back_kernel(gemb_ref, we_ref, wd_ref, wu_ref, slope_ref, resid_ref, wo_ref, rows_ref,
                       gb2_ref, gh_ref, gres_ref, gb_ref, gatt_ref, dup_ref, dvec_ref, total, genc):
    j = pl.program_id(0)

    @pl.when(j == 0)
    def _():
        genc[...] = dot_nt(gemb_ref[...], we_ref[...])
        gb2_ref[...] = genc[...].astype(jnp.bfloat16)
        dup_ref[...] = jnp.zeros_like(dup_ref)

    gh = (dot_nt(gb2_ref[...], wd_ref[...]) * slope_ref[...].astype(jnp.float32)).astype(jnp.bfloat16)
    gh_ref[...] = gh
    dup_ref[pl.ds(j, 1)] = jnp.sum(gh.astype(jnp.float32), axis=0, keepdims=True)
    part = dot_nt(gh, wu_ref[...])

    @pl.when(j == 0)
    def _():
        total[...] = part

    @pl.when(j > 0)
    def _():
        total[...] += part

    @pl.when(j == PART - 1)
    def _():
        back, dgain, dshift = norm_back(resid_ref[...], rows_ref[G2 : G2 + 1], total[...])
        gres = genc[...] + back
        gres_ref[...] = gres
        gb = gres.astype(jnp.bfloat16)
        gb_ref[...] = gb
        gatt_ref[...] = dot_nt(gb, wo_ref[...]).astype(jnp.bfloat16)
        dvec_ref[...] = jnp.concatenate(
            [
                dgain,
                dshift,
                jnp.sum(gb.astype(jnp.float32), axis=0, keepdims=True),
                jnp.zeros((5, D), jnp.float32),
            ],
            axis=0,
        )


def hidden_back(half, earlier, gemb, whole, slope, resid, rows):
    return in_halves(
        hidden_back_kernel,
        half,
        earlier,
        [
            const(CHUNK, DD),
            columns(DD, EMB_AT),
            tile_columns(DOWN_AT),
            tile_columns(UP_AT),
            tile_of(half),
            rows_of(half, D),
            columns(D, OUT_AT),
            const(24, D),
        ],
        [
            rows_of(half, D),
            tile_of(half),
            rows_of(half, D),
            rows_of(half, D),
            rows_of(half, D),
            const(8, D),
            const(8, D),
        ],
        [
            jax.ShapeDtypeStruct((ROWS, D), jnp.bfloat16),
            jax.ShapeDtypeStruct((ROWS, FF), jnp.bfloat16),
            jax.ShapeDtypeStruct((ROWS, D), jnp.float32),
            jax.ShapeDtypeStruct((ROWS, D), jnp.bfloat16),
            jax.ShapeDtypeStruct((ROWS, D), jnp.bfloat16),
            jax.ShapeDtypeStruct((8, D), jnp.float32),
            jax.ShapeDtypeStruct((8, D), jnp.float32),
        ],
        (0, 1, 2, 3, 4),
        48,
        "hidden_back",
        [pltpu.VMEM((CHUNK, D), jnp.float32)] * 2,
        [gemb, whole, whole, whole, slope, resid, whole, rows],
    )


def up_grad_kernel(role_ref, n2_mine, n2_other, gh_ref, att_mine, att_other, gb_ref, mine_ref, other_ref):
    j = pl.program_id(0)
    at = pl.ds(pl.multiple_of(j * D, D), D)
    mine_ref[:, at] = dot_tn(n2_mine[...], gh_ref[...]).astype(jnp.bfloat16)
    other_ref[:, at] = dot_tn(n2_other[...], gh_ref[...]).astype(jnp.bfloat16)

    @pl.when(j == PART - 1)
    def _():
        mine_ref[:, FF:] = dot_tn(att_mine[...], gb_ref[...]).astype(jnp.bfloat16)
        other_ref[:, FF:] = dot_tn(att_other[...], gb_ref[...]).astype(jnp.bfloat16)


def up_grad(role, n2, gh, attended, gb):
    return with_role(
        up_grad_kernel,
        (PART,),
        [
            half_columns(True),
            half_columns(False),
            pl.BlockSpec((ROWS, D), lambda j, role: (0, j)),
            half_columns(True),
            half_columns(False),
            const(ROWS, D),
        ],
        [const(HALF, C_TWO), const(HALF, C_TWO)],
        [
            jax.ShapeDtypeStruct((HALF, C_TWO), jnp.bfloat16),
            jax.ShapeDtypeStruct((HALF, C_TWO), jnp.bfloat16),
        ],
        40,
        "up_grad",
    )(role, n2, n2, gh, attended, attended, gb)


def attention_back_kernel(count_ref, mixed_ref, gatt_ref, gmix_ref, held, gheld):
    live = lax.broadcasted_iota(jnp.int32, (SLOT, SLOT), 0) < count_ref[pl.program_id(0)]
    masks = head_masks()
    low_lane = lax.broadcasted_iota(jnp.int32, (SLOT, 128), 1) < HD
    scale = HD ** (-0.5)
    for pair in range(H // 2):
        c = pair * 128
        held[pair] = dot_nt(stacked(mixed_ref[:, D + c : D + c + 128], masks), mixed_ref[:, c : c + 128])
        gheld[pair] = dot_nt(
            stacked(mixed_ref[:, 2 * D + c : 2 * D + c + 128], masks), gatt_ref[:, c : c + 128]
        )
    for pair in range(H // 2):
        c = pair * 128
        probs = key_probs(held[pair], live)
        gscores = []
        for k in range(2):
            p, g = probs[k], gheld[pair, SLOT * k : SLOT * k + SLOT]
            gscores.append(p * (g - jnp.sum(p * g, axis=0, keepdims=True)))
        gscores = jnp.concatenate(gscores, axis=0).astype(jnp.bfloat16)
        probs = jnp.concatenate(probs, axis=0).astype(jnp.bfloat16)
        gv = dot_nn(probs, gatt_ref[:, c : c + 128])
        gk = dot_nn(gscores, mixed_ref[:, c : c + 128]) * scale
        gq = dot_tn(gscores, stacked(mixed_ref[:, D + c : D + c + 128], masks)) * scale
        gmix_ref[:, c : c + 128] = gq.astype(jnp.bfloat16)
        gmix_ref[:, D + c : D + c + 128] = jnp.where(low_lane, gk[:SLOT], gk[SLOT:]).astype(jnp.bfloat16)
        gmix_ref[:, 2 * D + c : 2 * D + c + 128] = jnp.where(
            low_lane, gv[:SLOT], gv[SLOT:]
        ).astype(jnp.bfloat16)


def attention_back(count, mixed, gatt):
    wide = pl.BlockSpec((SLOT, 3 * D), lambda s: (s, 0))
    return pl.pallas_call(
        attention_back_kernel,
        grid=(IMG_DEV,),
        in_specs=[
            pl.BlockSpec(memory_space=pltpu.SMEM),
            wide,
            pl.BlockSpec((SLOT, D), lambda s: (s, 0)),
        ],
        out_specs=wide,
        out_shape=jax.ShapeDtypeStruct((ROWS, 3 * D), jnp.bfloat16),
        scratch_shapes=[pltpu.VMEM((H // 2, 2 * SLOT, SLOT), jnp.float32)] * 2,
        compiler_params=params(32),
        cost_estimate=cost(7),
        name="attention_back",
    )(count, mixed, gatt)


def input_back_kernel(role_ref, gmix_ref, w_ref, x_ref, gres_ref, rows_ref, normed_mine, normed_other,
                      dup_ref, d2_ref, ddown_ref, dpb_ref, d3_ref, demb_ref,
                      pg_ref, mine_ref, other_ref, total, turned):
    j = pl.program_id(0)
    at = pl.ds(pl.multiple_of(j * D, D), D)
    gmix = gmix_ref[...]
    mine_ref[:, at] = dot_tn(normed_mine[...], gmix).astype(jnp.bfloat16)
    other_ref[:, at] = dot_tn(normed_other[...], gmix).astype(jnp.bfloat16)
    part = dot_nt(gmix, w_ref[...])
    dbias = jnp.sum(gmix.astype(jnp.float32), axis=0, keepdims=True)

    @pl.when(j == 0)
    def _():
        total[...] = part
        turned[QB : QB + 1] = dbias

    @pl.when(j > 0)
    def _():
        total[...] += part

    @pl.when(j == 2)
    def _():
        back, dgain, dshift = norm_back(
            x_ref[...].astype(jnp.float32), rows_ref[G1 : G1 + 1], total[...]
        )
        pg_ref[...] = (gres_ref[...] + back).astype(jnp.bfloat16)
        turned[G1 : G1 + 1] = dgain
        turned[S1 : S1 + 1] = dshift
        turned[VB : VB + 1] = dbias
        turned[OB : OB + 1] = d2_ref[2:3]
        turned[G2 : G2 + 1] = d2_ref[0:1]
        turned[S2 : S2 + 1] = d2_ref[1:2]
        turned[DB : DB + 1] = ddown_ref[...]
        turned[PB : PB + 1] = dpb_ref[...]
        turned[UB : UB + 4] = dup_ref[0:4]
        turned[13:16] = jnp.zeros((3, D), jnp.float32)
        four = jnp.concatenate([demb_ref[...], d3_ref[1:4], jnp.zeros((4, DD), jnp.float32)], axis=0)
        turned[16:24] = dot_nt(four.astype(jnp.bfloat16), spread())
        block = jnp.concatenate([turned[...], jnp.zeros((104, D), jnp.float32)], axis=0).T
        first, second = block[:HALF].astype(jnp.bfloat16), block[HALF:].astype(jnp.bfloat16)
        up = role_ref[0] == 1
        mine_ref[:, 3 * D :] = jnp.where(up, second, first)
        other_ref[:, 3 * D :] = jnp.where(up, first, second)


def input_back(role, gmix, whole, x, gres, rows, normed, dup, d2, ddown, dpb, d3, demb):
    return with_role(
        input_back_kernel,
        (3,),
        [
            pl.BlockSpec((ROWS, D), lambda j, role: (0, j)),
            pl.BlockSpec((D, D), lambda j, role: (0, j)),
            const(ROWS, D),
            const(ROWS, D),
            const(24, D),
            half_columns(True),
            half_columns(False),
            const(8, D),
            const(8, D),
            const(1, D),
            const(1, D),
            const(8, DD),
            const(1, DD),
        ],
        [const(ROWS, D), const(HALF, C_THREE), const(HALF, C_THREE)],
        [
            jax.ShapeDtypeStruct((ROWS, D), jnp.bfloat16),
            jax.ShapeDtypeStruct((HALF, C_THREE), jnp.bfloat16),
            jax.ShapeDtypeStruct((HALF, C_THREE), jnp.bfloat16),
        ],
        48,
        "input_back",
        [pltpu.VMEM((ROWS, D), jnp.float32), pltpu.VMEM((24, D), jnp.float32)],
    )(role, gmix, whole, x, gres, rows, normed, normed, dup, d2, ddown, dpb, d3, demb)


def hot(shape, test):
    return test(
        lax.broadcasted_iota(jnp.int32, shape, 0), lax.broadcasted_iota(jnp.int32, shape, 1)
    ).astype(jnp.bfloat16)


def hidden_order():
    return hot((512, 512), lambda l, c: l == 4 * (c % 128) + c // 128)


def pack_kernel(qkv_ref, out_ref, up_ref, down_ref, emb_ref, pix_ref, vec_ref, packed_ref):
    packed_ref[:, :OUT_AT] = qkv_ref[...]
    packed_ref[:, OUT_AT:UP_AT] = out_ref[...]
    order = hidden_order()
    for r in range(D // 128):
        turned = dot_nn(up_ref[:, 512 * r : 512 * r + 512], order).astype(jnp.bfloat16)
        for j in range(PART):
            at = UP_AT + j * D + 128 * r
            packed_ref[:, at : at + 128] = turned[:, 128 * j : 128 * j + 128]
    for j in range(PART):
        rows = hot((6, 24), lambda i, l: l == 4 * i + j)
        packed_ref[:, DOWN_AT + j * D : DOWN_AT + j * D + D] = dot_nn(rows, down_ref[...]).astype(jnp.bfloat16)
    packed_ref[:, EMB_AT:PIX_AT] = emb_ref[...]
    for t in range(2):
        part = jnp.zeros((6, 256), jnp.float32)
        for s in range(3):
            rows = hot((6, 4), lambda r, i: 2 * r + t == 3 * i + s)
            part = part + dot_nn(rows, pix_ref[:, 256 * s : 256 * s + 256])
        packed_ref[:, PIX_AT + 256 * t : PIX_AT + 256 * t + 256] = part.astype(jnp.bfloat16)
    row = lax.broadcasted_iota(jnp.int32, (6, 128), 0)
    block = jnp.zeros((6, 128), jnp.float32)
    line = jnp.broadcast_to(vec_ref[...], (16, 128))
    for i in range(6):
        pick = hot(
            (128, 128),
            lambda m, c: ((c < 9) & (m == 6 * c + i))
            | ((c >= UB) & (c < UB + PART) & (m == 54 + 4 * i + c - UB))
            | ((c >= 16) & (c < 20) & (m == 78 + 4 * (c - 16) + i) & (i < 4)),
        )
        block = jnp.where(row == i, dot_nn(line, pick)[:6], block)
    packed_ref[:, VEC_AT:] = block.astype(jnp.bfloat16)


def pack(*args):
    return pl.pallas_call(
        pack_kernel,
        out_shape=jax.ShapeDtypeStruct((6, WIDE), jnp.bfloat16),
        compiler_params=pltpu.CompilerParams(vmem_limit_bytes=16 * MIB),
        cost_estimate=cost(4),
        name="pack",
    )(*args)


def unpack_kernel(kept_ref, came_ref, qkv_ref, out_ref, up_ref, down_ref, emb_ref, pix_ref, vec_ref):
    one, two = C_ONE, C_ONE + C_TWO

    def total(at, width):
        return kept_ref[:, at : at + width].astype(jnp.float32) + came_ref[:, at : at + width].astype(
            jnp.float32
        )

    def shuffled(dot):
        return dot(kept_ref) + dot(came_ref)

    qkv_ref[...] = total(two, 3 * D)
    out_ref[...] = total(one + FF, D)
    emb_ref[...] = total(FF, DD)
    vec_ref[...] = total(two + 3 * D, 128)
    order = hidden_order()
    for r in range(D // 128):

        def turned(ref):
            parts = [ref[:, one + j * D + 128 * r : one + j * D + 128 * r + 128] for j in range(PART)]
            return dot_nt(jnp.concatenate(parts, axis=1), order)

        up_ref[:, 512 * r : 512 * r + 512] = shuffled(turned)
    down = jnp.zeros((24, D), jnp.float32)
    for j in range(PART):
        rows = hot((24, 6), lambda l, i: l == 4 * i + j)
        down = down + shuffled(lambda ref: dot_nn(rows, ref[:, j * D : j * D + D]))
    down_ref[...] = down
    for s in range(3):
        part = jnp.zeros((4, 256), jnp.float32)
        for t in range(2):
            rows = hot((4, 6), lambda i, r: 2 * r + t == 3 * i + s)
            at = FF + DD + 256 * t
            part = part + shuffled(lambda ref: dot_nn(rows, ref[:, at : at + 256]))
        pix_ref[:, 256 * s : 256 * s + 256] = part


def unpack(kept, came):
    return pl.pallas_call(
        unpack_kernel,
        out_shape=[
            jax.ShapeDtypeStruct(shape, jnp.float32)
            for shape in ((6, 3 * D), (6, D), (6, FF), (24, D), (6, DD), (4, PIX), (6, 128))
        ],
        compiler_params=pltpu.CompilerParams(vmem_limit_bytes=16 * MIB),
        cost_estimate=cost(4),
        name="unpack",
    )(kept, came)


PAIRS = {
    "high": [(0, 3), (3, 0), (1, 2), (2, 1)],
    "low": [(0, 1), (1, 0), (2, 3), (3, 2)],
}


def halve(state, axis, dim, which):
    at = lax.axis_index(axis)
    bit = at // 2 if which == "high" else at % 2
    half = state.shape[dim] // 2
    kept = lax.dynamic_slice_in_dim(state, bit * half, half, dim)
    sent = lax.dynamic_slice_in_dim(state, (1 - bit) * half, half, dim)
    came = lax.ppermute(sent, axis, PAIRS[which])
    return (kept.astype(jnp.float32) + came.astype(jnp.float32)).astype(jnp.bfloat16)


ROLE_PAIR = [(0, 1), (1, 0)]


def tie(*arrays):
    return lax.optimization_barrier(arrays)


def moved(images, step, crossing=False):
    pairs = [
        (r * N_DP + p, (r ^ crossing) * N_DP + (p + step) % N_DP)
        for r in range(2)
        for p in range(N_DP)
    ]
    return lax.ppermute(images, ALL, pairs)


def added(mine, came):
    return (mine.astype(jnp.float32) + came.astype(jnp.float32)).astype(jnp.bfloat16)


def split(state):
    at = (state.shape[1] // 128 + 1) // 2 * 128
    return state[:, :at], state[:, at:]


class Halving:
    def __init__(self, state, order):
        self.columns = state.shape[1]
        self.state = state.reshape(4, 4, 24, self.columns)
        self.steps = [(axis, which) for axis in order for which in ("high", "low")]
        self.halve()

    def halve(self):
        self.step = axis, which = self.steps.pop(0)
        dim = 0 if axis == "y" else 1
        at = lax.axis_index(axis)
        bit = at // 2 if which == "high" else at % 2
        half = self.state.shape[dim] // 2
        self.kept = lax.dynamic_slice_in_dim(self.state, bit * half, half, dim)
        self.sent = lax.dynamic_slice_in_dim(self.state, (1 - bit) * half, half, dim)

    def send(self):
        axis, which = self.step
        self.came = lax.ppermute(self.sent, axis, PAIRS[which])

    def take(self):
        self.state = added(self.kept, self.came)

    def go(self):
        self.take()
        if self.steps:
            self.halve()
            self.send()

    def finish(self):
        return self.state.reshape(24, self.columns)


def over_line(state):
    columns = state.shape[1]
    state = state.reshape(4, 6, columns)
    state = halve(state, "x", 0, "high")
    at = lax.axis_index("x") % 2
    kept = lax.dynamic_index_in_dim(state, at, 0, keepdims=False)
    sent = lax.dynamic_index_in_dim(state, 1 - at, 0, keepdims=False)
    came = lax.ppermute(sent, "x", PAIRS["low"])
    return kept, came


def body(
    patch_rows,
    patch_order,
    visible_count,
    encoded_image,
    first_gain,
    first_shift,
    query_key_value,
    query_bias,
    value_bias,
    output_weight,
    output_bias,
    second_gain,
    second_shift,
    up_weight,
    up_bias,
    down_weight,
    down_bias,
    embed_weight,
    embed_bias,
    mask_token,
    decoder_gain,
    decoder_shift,
    pixel_weight,
    pixel_bias,
    pixel_grad,
):
    device = lax.axis_index(ALL)
    role = lax.axis_index("role").astype(jnp.int32).reshape(1)
    image_count = encoded_image.shape[0]

    own_images = device * IMG_DEV + jnp.arange(IMG_DEV, dtype=jnp.int32)
    found = encoded_image[None, :] == own_images[:, None]
    source_slot = jnp.sum(
        jnp.where(found, jnp.arange(image_count, dtype=jnp.int32)[None, :], 0), axis=1
    )
    source_place = source_slot % IMG_DEV
    image_of = jnp.sum(
        jnp.where(
            source_place[None, :] == jnp.arange(IMG_DEV, dtype=jnp.int32)[:, None],
            jnp.arange(IMG_DEV, dtype=jnp.int32)[None, :],
            0,
        ),
        axis=1,
    )
    own_count = lax.dynamic_slice_in_dim(visible_count, device * IMG_DEV, IMG_DEV)
    own_order = lax.dynamic_slice_in_dim(patch_order, device * IMG_DEV, IMG_DEV, 0)[:, None, :SLOT]
    first, later = image_of[jnp.array([0, 4])], image_of[jnp.array([1, 5, 2, 6, 3, 7])]

    vectors = jnp.concatenate(
        [
            first_gain,
            first_shift,
            query_bias,
            value_bias,
            output_bias,
            second_gain,
            second_shift,
            down_bias,
            pixel_bias,
            up_bias,
            embed_bias,
            mask_token,
            decoder_gain,
            decoder_shift,
            jnp.zeros((34,), jnp.bfloat16),
        ]
    ).reshape(1, 128)
    packed = pack(
        query_key_value, output_weight, up_weight, down_weight, embed_weight, pixel_weight, vectors
    )
    whole = lax.all_gather(packed, "x", tiled=True)
    whole = lax.all_gather(whole, ("role", "y", "z"), tiled=True)
    pix_weight = whole[:, PIX_AT:VEC_AT].reshape(DD, PIX)

    held = lax.dynamic_slice_in_dim(encoded_image, device * IMG_DEV, IMG_DEV)
    count = visible_count[held]

    normed, mixed, attended, rows, fours = attention(count, patch_rows, whole)
    half = forward(1, None, patch_rows, attended, whole, rows, fours)
    high = moved(half[5].reshape(4, SLOT, DD), 4, True)
    half = forward(0, half, patch_rows, attended, whole, rows, fours)
    resid, normed_two, active, slope, encoded, embedded = half
    low = moved(embedded.reshape(4, SLOT, DD), 0, True)
    steps = [
        moved(jnp.concatenate([low[s : s + 1], high[s : s + 1]]), s) for s in range(1, 4)
    ]
    table = positions()
    zeros = jnp.zeros((8, DD), jnp.float32), jnp.zeros((DD, PIX), jnp.float32), jnp.zeros((1, PIX), jnp.float32)
    grad_first, decoded, d_three = decoder_grid(
        first,
        own_count[first],
        own_order[first],
        jnp.concatenate([low[:1], high[:1]]),
        table,
        pix_weight,
        fours,
        pixel_grad,
        zeros[0],
    )
    pixels, d_pix, d_pix_bias = decoder_pixels(
        first, decoded, pixel_grad, pix_weight, rows, zeros[1], zeros[2]
    )
    d_pix, *steps = tie(d_pix, *steps)
    grad_later, decoded, d_three = decoder_grid(
        later,
        own_count[later],
        own_order[later],
        jnp.concatenate(steps),
        table,
        pix_weight,
        fours,
        pixel_grad,
        d_three,
    )
    steps = [moved(grad_later[2 * s - 2 : 2 * s], -s) for s in range(1, 4)]
    pixels, d_pix, d_pix_bias = decoder_pixels(
        later, decoded, pixel_grad, pix_weight, rows, d_pix, d_pix_bias, pixels
    )
    d_pix, *steps = tie(d_pix, *steps)
    high = moved(jnp.concatenate([grad_first[1:]] + [s[1:] for s in steps]), -4, True).reshape(CHUNK, DD)
    low = moved(jnp.concatenate([grad_first[:1]] + [s[:1] for s in steps]), 0, True).reshape(CHUNK, DD)
    half = hidden_back(0, None, low, whole, slope, resid, rows)
    d_up_bias, d_two = half[5:]
    high, part = tie(high, half[0])
    half = hidden_back(1, [part, *half[1:]], high, whole, slope, resid, rows)
    branch_two, grad_hidden, grad_resid, grad_branch, grad_attended = half[:5]
    d_up_bias, d_two = d_up_bias + half[5], d_two + half[6]
    mine_one, other_one, d_down_bias, d_emb_bias = down_grad(
        role,
        jnp.concatenate([low, high]),
        branch_two,
        encoded,
        active,
        d_pix.astype(jnp.bfloat16).reshape(D, DD),
    )
    grad_hidden, other_one = tie(grad_hidden, other_one)
    came_one = lax.ppermute(other_one, "role", ROLE_PAIR)
    mine_two, other_two = up_grad(role, normed_two, grad_hidden, attended, grad_branch)
    mine_one, came_one, other_two = tie(mine_one, came_one, other_two)
    part_one, grad_attended, other_two = tie(added(mine_one, came_one), grad_attended, other_two)
    part_one = lax.psum_scatter(part_one, "y", tiled=True)
    came_two = lax.ppermute(other_two, "role", ROLE_PAIR)
    grad_mixed = attention_back(count, mixed, grad_attended)
    grad_mixed, came_two = tie(grad_mixed, came_two)
    two = [Halving(part, order) for part, order in zip(split(added(mine_two, came_two)), ("zy", "yz"))]
    grad_mixed, two[0].sent, two[1].sent = tie(grad_mixed, two[0].sent, two[1].sent)
    for part in two:
        part.send()
    patch_grad, mine, other = input_back(
        role,
        grad_mixed,
        whole,
        patch_rows,
        grad_resid,
        rows,
        normed,
        d_up_bias,
        d_two,
        d_down_bias,
        d_pix_bias,
        d_three,
        d_emb_bias,
    )
    mine, other, two[0].came, two[1].came = tie(mine, other, two[0].came, two[1].came)
    came_three = lax.ppermute(other, "role", ROLE_PAIR)
    for part in two:
        part.go()
    mine, came_three, two[0].sent, two[1].sent = tie(mine, came_three, two[0].sent, two[1].sent)
    three = [Halving(part, order) for part, order in zip(split(added(mine, came_three)), ("zy", "yz"))]
    for part in three:
        part.send()
    for part in two:
        part.go()
    part_one, three[0].came, three[1].came, two[0].came, two[1].came = tie(
        part_one, three[0].came, three[1].came, two[0].came, two[1].came
    )
    part_one = lax.psum_scatter(part_one, "z", tiled=True)
    for step in range(2):
        for part in three + two:
            part.go()
    for step in range(2):
        for part in three:
            part.go()
    parts = [part_one] + [part.finish() for part in two + three]
    kept, came = over_line(jnp.concatenate(parts, axis=1))
    d_qkv, d_out, d_up, d_down, d_emb, d_pix, vec = unpack(kept, came)
    return (
        pixels,
        patch_grad,
        vec[:, G1],
        vec[:, S1],
        d_qkv,
        vec[:, QB],
        vec[:, VB],
        d_out,
        vec[:, OB],
        vec[:, G2],
        vec[:, S2],
        d_up,
        vec[:, UB : UB + PART].reshape(6 * PART),
        d_down,
        vec[:, DB],
        d_emb,
        vec[:4, 16 + EB],
        vec[:4, 16 + TOK],
        vec[:4, 16 + G3],
        vec[:4, 16 + S3],
        d_pix,
        vec[:, PB],
    )


def solution(mesh):
    mesh = Mesh(mesh.devices.reshape(2, 4, 4, 4), ALL)
    two, one = P(ALL, None), P(ALL)
    placed = (two, P(), P(), P(), one, one, two, one, one, two, one, one, one, two, one, two, one)
    placed += (two, one, one, one, one, two, one, P(ALL, None, None))
    given = (P(ALL, None, None), two, one, one, two, one, one, two, one, one, one, two, one, two, one)
    given += (two, one, one, one, one, two, one)
    return jax.shard_map(body, mesh=mesh, in_specs=placed, out_specs=given, check_vma=False)
```

```python
import functools

import jax
import jax.numpy as jnp
from jax import lax
from jax.experimental import pallas as pl
from jax.experimental.pallas import tpu as pltpu
from jax.sharding import Mesh
from jax.sharding import PartitionSpec as P

D = 768
H = 12
HD = 64
FF = 3072
DD = 512
PIX = 768
SIDE = 14
SLOT = 80
IMG_DEV = 8
GRID = 196
N_DP = 64
PART = FF // D

ALL = ("role", "y", "z", "x")

epsilon = 1e-06
masked_score = -1e30

def positions():
    quarter = DD // 4
    frequency = 10000.0 ** (-jnp.arange(quarter, dtype=jnp.float32) / quarter)
    places = jnp.arange(GRID, dtype=jnp.int32)
    row_angle = (places // SIDE).astype(jnp.float32)[:, None] * frequency[None, :]
    col_angle = (places % SIDE).astype(jnp.float32)[:, None] * frequency[None, :]
    return jnp.concatenate(
        [jnp.sin(row_angle), jnp.cos(row_angle), jnp.sin(col_angle), jnp.cos(col_angle)], axis=1
    )


HALF = D // 2
ROWS = IMG_DEV * SLOT
CHUNK = ROWS // 2
OUT_AT, UP_AT, DOWN_AT, EMB_AT, PIX_AT, VEC_AT = 3 * D, 4 * D, 8 * D, 12 * D, 12 * D + DD, 12 * D + 2 * DD
WIDE = VEC_AT + 128
G1, S1, QB, VB, OB, G2, S2, DB, PB, UB = range(10)
EB, TOK, G3, S3 = range(4)

MIB = 1 << 20


def cost(us):
    return pl.CostEstimate(flops=int(us * 1e9), bytes_accessed=0, transcendentals=0)


def params(mib):
    return pltpu.CompilerParams(
        dimension_semantics=("arbitrary",), vmem_limit_bytes=mib * MIB
    )


def const(*shape):
    return pl.BlockSpec(shape, lambda i, *_: (0,) * len(shape))


def columns(width, at):
    return pl.BlockSpec((D, width), lambda i, *_: (0, at // width))


def tile_columns(at):
    return pl.BlockSpec((D, D), lambda i, *_: (0, at // D + i))


def dot_nn(a, b):
    return lax.dot_general(a, b, (((1,), (0,)), ((), ())), preferred_element_type=jnp.float32)


def dot_nt(a, b):
    return lax.dot_general(a, b, (((1,), (1,)), ((), ())), preferred_element_type=jnp.float32)


def dot_tn(a, b):
    return lax.dot_general(a, b, (((0,), (0,)), ((), ())), preferred_element_type=jnp.float32)


def normalised(values):
    average = jnp.mean(values, axis=-1, keepdims=True)
    centered = values - average
    variance = jnp.mean(centered * centered, axis=-1, keepdims=True)
    inverse = lax.rsqrt(variance + epsilon)
    return centered * inverse, inverse


def norm_back(values, gain, upstream):
    h, inverse = normalised(values)
    dh = upstream * gain
    dv = (
        dh - jnp.mean(dh, axis=-1, keepdims=True) - h * jnp.mean(dh * h, axis=-1, keepdims=True)
    ) * inverse
    return (
        dv,
        jnp.sum(upstream * h, axis=0, keepdims=True),
        jnp.sum(upstream, axis=0, keepdims=True),
    )


def strips(count, body, size=16, at_once=10):
    def some(i, carry):
        for n in range(at_once):
            body(pl.ds(pl.multiple_of((i * at_once + n) * size, size), size))
        return carry

    lax.fori_loop(0, count // (at_once * size), some, 0)


def spread():
    row = lax.broadcasted_iota(jnp.int32, (D, DD), 0)
    col = lax.broadcasted_iota(jnp.int32, (D, DD), 1)
    return (row == 6 * (col // 4) + col % 4).astype(jnp.bfloat16)


def head_masks():
    lane = lax.broadcasted_iota(jnp.int32, (1, 2 * HD), 1)
    low = (lane < HD).astype(jnp.bfloat16)
    return low, (1.0 - low.astype(jnp.float32)).astype(jnp.bfloat16)


def stacked(pair, masks):
    return jnp.concatenate([pair * masks[0], pair * masks[1]], axis=0)


def key_probs(scores, live):
    both = []
    for k in range(2):
        s = jnp.where(live, scores[SLOT * k : SLOT * k + SLOT] * HD ** (-0.5), masked_score)
        e = jnp.exp(s - jnp.max(s, axis=0, keepdims=True))
        both.append(e * (1.0 / jnp.sum(e, axis=0, keepdims=True)))
    return both


def attention_kernel(count_ref, x_ref, w_ref, vec_ref, normed_ref, mixed_ref, att_ref, rows_ref, fours_ref, held):
    step = pl.program_id(0)

    @pl.when(step == 0)
    def _():
        turned = vec_ref[...].astype(jnp.float32).T
        rows_ref[...] = turned[:24]
        fours_ref[...] = dot_nn(turned[16:24].astype(jnp.bfloat16), spread())

    def norm(at):
        h, _ = normalised(x_ref[at].astype(jnp.float32))
        normed_ref[at] = (h * rows_ref[G1 : G1 + 1] + rows_ref[S1 : S1 + 1]).astype(jnp.bfloat16)

    strips(CHUNK, norm)
    for part, bias in ((0, QB), (1, None), (2, VB)):
        m = dot_nn(normed_ref[...], w_ref[:, part * D : part * D + D])
        if bias is not None:
            m = m + rows_ref[bias : bias + 1]
        mixed_ref[:, part * D : part * D + D] = m.astype(jnp.bfloat16)
    masks = head_masks()
    place = lax.broadcasted_iota(jnp.int32, (SLOT, SLOT), 0)

    def one_slot(s, carry):
        at = pl.ds(pl.multiple_of(s * SLOT, SLOT), SLOT)
        live = place < count_ref[step * (CHUNK // SLOT) + s]
        for pair in range(H // 2):
            c = pair * 128
            keys = stacked(mixed_ref[at, D + c : D + c + 128], masks)
            held[pair] = dot_nt(keys, mixed_ref[at, c : c + 128])
        for pair in range(H // 2):
            c = pair * 128
            probs = jnp.concatenate(key_probs(held[pair], live), axis=0).astype(jnp.bfloat16)
            values = stacked(mixed_ref[at, 2 * D + c : 2 * D + c + 128], masks)
            att_ref[at, c : c + 128] = dot_tn(probs, values).astype(jnp.bfloat16)
        return carry

    lax.fori_loop(0, CHUNK // SLOT, one_slot, 0)


def attention(count, patch_rows, whole):
    rows = pl.BlockSpec((CHUNK, D), lambda i: (i, 0))
    return pl.pallas_call(
        attention_kernel,
        grid=(2,),
        in_specs=[
            pl.BlockSpec(memory_space=pltpu.SMEM),
            rows,
            columns(3 * D, 0),
            columns(128, VEC_AT),
        ],
        out_specs=[rows, pl.BlockSpec((CHUNK, 3 * D), lambda i: (i, 0)), rows, const(24, D), const(8, DD)],
        out_shape=[
            jax.ShapeDtypeStruct((ROWS, D), jnp.bfloat16),
            jax.ShapeDtypeStruct((ROWS, 3 * D), jnp.bfloat16),
            jax.ShapeDtypeStruct((ROWS, D), jnp.bfloat16),
            jax.ShapeDtypeStruct((24, D), jnp.float32),
            jax.ShapeDtypeStruct((8, DD), jnp.float32),
        ],
        scratch_shapes=[pltpu.VMEM((H // 2, 2 * SLOT, SLOT), jnp.float32)],
        compiler_params=params(48),
        cost_estimate=cost(11),
        name="attention",
    )(count, patch_rows, whole, whole)


GELU_C = 0.7978845608028654


def in_halves(kernel, half, earlier, in_specs, out_specs, out_shape, shared, mib, name, scratch, args):
    aliases = {}
    if earlier is not None:
        n = len(args)
        inner = kernel

        def kernel(*refs):
            return inner(*refs[:n], *refs[n + len(shared) :])

        aliases = {n + i: out for i, out in enumerate(shared)}
        in_specs = in_specs + [pl.BlockSpec(memory_space=pl.ANY)] * len(shared)
        args = args + [earlier[out] for out in shared]
    return pl.pallas_call(
        kernel,
        grid=(PART,),
        in_specs=in_specs,
        out_specs=out_specs,
        out_shape=out_shape,
        scratch_shapes=scratch,
        input_output_aliases=aliases,
        compiler_params=params(mib),
        cost_estimate=cost(11),
        name=name,
    )(*args)


def rows_of(half, width):
    return pl.BlockSpec((CHUNK, width), lambda j: (half, 0))


def tile_of(half):
    return pl.BlockSpec((CHUNK, D), lambda j: (half, j))


def forward_kernel(x_ref, att_ref, wo_ref, wu_ref, wd_ref, we_ref, rows_ref, fours_ref,
                   resid_ref, n2_ref, act_ref, slope_ref, enc_ref, emb_ref, total):
    j = pl.program_id(0)

    @pl.when(j == 0)
    def _():
        resid = x_ref[...].astype(jnp.float32) + (
            dot_nn(att_ref[...], wo_ref[...]) + rows_ref[OB : OB + 1]
        )
        resid_ref[...] = resid
        h, _ = normalised(resid)
        n2_ref[...] = (h * rows_ref[G2 : G2 + 1] + rows_ref[S2 : S2 + 1]).astype(jnp.bfloat16)
        total[...] = resid + rows_ref[DB : DB + 1]

    v = dot_nn(n2_ref[...], wu_ref[...]) + rows_ref[pl.ds(UB + j, 1)]
    square = v * v
    t = jnp.tanh(v * (GELU_C + 0.044715 * GELU_C * square))
    lift = 0.5 + 0.5 * t
    active = v * lift
    act_ref[...] = active.astype(jnp.bfloat16)
    slope_ref[...] = (
        lift + active * (1.0 - t) * (GELU_C + 3 * 0.044715 * GELU_C * square)
    ).astype(jnp.bfloat16)
    total[...] += dot_nn(act_ref[...], wd_ref[...])

    @pl.when(j == PART - 1)
    def _():
        enc_ref[...] = total[...].astype(jnp.bfloat16)
        emb_ref[...] = (dot_nn(enc_ref[...], we_ref[...]) + fours_ref[EB : EB + 1]).astype(jnp.bfloat16)


def forward(half, earlier, patch_rows, attended, whole, rows, fours):
    return in_halves(
        forward_kernel,
        half,
        earlier,
        [
            rows_of(half, D),
            rows_of(half, D),
            columns(D, OUT_AT),
            tile_columns(UP_AT),
            tile_columns(DOWN_AT),
            columns(DD, EMB_AT),
            const(24, D),
            const(8, DD),
        ],
        [rows_of(half, D), rows_of(half, D), tile_of(half), tile_of(half), rows_of(half, D), const(CHUNK, DD)],
        [
            jax.ShapeDtypeStruct((ROWS, D), jnp.float32),
            jax.ShapeDtypeStruct((ROWS, D), jnp.bfloat16),
            jax.ShapeDtypeStruct((ROWS, FF), jnp.bfloat16),
            jax.ShapeDtypeStruct((ROWS, FF), jnp.bfloat16),
            jax.ShapeDtypeStruct((ROWS, D), jnp.bfloat16),
            jax.ShapeDtypeStruct((CHUNK, DD), jnp.bfloat16),
        ],
        (0, 1, 2, 3, 4),
        48,
        "forward",
        [pltpu.VMEM((CHUNK, D), jnp.float32)],
        [patch_rows, attended, whole, whole, whole, whole, rows, fours],
    )


def grid_kernel(image_ref, count_ref, order_ref, emb_ref, table_ref, w_ref, fours_ref, up_ref, start_ref,
                gemb_ref, dec_ref, dvec_ref):
    s = pl.program_id(0)
    cell = lax.broadcasted_iota(jnp.int32, (GRID, SLOT), 0)
    place = lax.broadcasted_iota(jnp.int32, (GRID, SLOT), 1)
    placed = jnp.where((order_ref[0] == cell) & (place < count_ref[s]), 1.0, 0.0)
    masked = 1.0 - jnp.sum(placed, axis=1, keepdims=True)
    placed = placed.astype(jnp.bfloat16)
    grid = dot_nn(placed, emb_ref[0]) + masked * fours_ref[TOK : TOK + 1] + table_ref[...]
    gain = fours_ref[G3 : G3 + 1]
    h, inverse = normalised(grid)
    dec_ref[0] = (h * gain + fours_ref[S3 : S3 + 1]).astype(jnp.bfloat16)
    grad = dot_nt(up_ref[0], w_ref[...])
    dh = grad * gain
    back = (
        dh - jnp.mean(dh, axis=-1, keepdims=True) - h * jnp.mean(dh * h, axis=-1, keepdims=True)
    ) * inverse
    gemb_ref[0] = dot_tn(placed, back.astype(jnp.bfloat16)).astype(jnp.bfloat16)

    @pl.when(s == 0)
    def _():
        dvec_ref[...] = start_ref[...]

    dvec_ref[...] += jnp.concatenate(
        [
            jnp.zeros((1, DD), jnp.float32),
            jnp.sum(masked * back, axis=0, keepdims=True),
            jnp.sum(grad * h, axis=0, keepdims=True),
            jnp.sum(grad, axis=0, keepdims=True),
            jnp.zeros((4, DD), jnp.float32),
        ],
        axis=0,
    )


def block(*shape):
    return pl.BlockSpec((1, *shape), lambda s, *_: (s, 0, 0))


def of_image(*shape):
    return pl.BlockSpec((1, *shape), lambda s, image, *_: (image[s], 0, 0))


def decoder_grid(image, count, order, embedded, table, pix_weight, fours, pixel_grad, start):
    n = image.shape[0]
    return pl.pallas_call(
        grid_kernel,
        grid_spec=pltpu.PrefetchScalarGridSpec(
            num_scalar_prefetch=2,
            grid=(n,),
            in_specs=[
                block(1, SLOT),
                block(SLOT, DD),
                const(GRID, DD),
                const(DD, PIX),
                const(8, DD),
                of_image(GRID, PIX),
                const(8, DD),
            ],
            out_specs=[block(SLOT, DD), block(GRID, DD), const(8, DD)],
        ),
        out_shape=[
            jax.ShapeDtypeStruct((n, SLOT, DD), jnp.bfloat16),
            jax.ShapeDtypeStruct((n, GRID, DD), jnp.bfloat16),
            jax.ShapeDtypeStruct((8, DD), jnp.float32),
        ],
        compiler_params=params(32),
        cost_estimate=cost(n),
        name="decoder_grid",
    )(image, count, order, embedded, table, pix_weight, fours, pixel_grad, start)


def pixel_kernel(image_ref, dec_ref, up_ref, w_ref, rows_ref, start_ref, bias_ref, *refs):
    pix_ref, dw_ref, dbias_ref = refs[-3:]
    s = pl.program_id(0)
    pix_ref[0] = (dot_nn(dec_ref[0], w_ref[...]) + rows_ref[PB : PB + 1]).astype(jnp.bfloat16)
    dw = dot_tn(dec_ref[0], up_ref[0])
    dbias = jnp.sum(up_ref[0].astype(jnp.float32), axis=0, keepdims=True)

    @pl.when(s == 0)
    def _():
        dw_ref[...] = start_ref[...] + dw
        dbias_ref[...] = bias_ref[...] + dbias

    @pl.when(s > 0)
    def _():
        dw_ref[...] += dw
        dbias_ref[...] += dbias


def decoder_pixels(image, decoded, pixel_grad, pix_weight, rows, start, bias, pixels=None):
    n = image.shape[0]
    args = [image, decoded, pixel_grad, pix_weight, rows, start, bias]
    specs = [block(GRID, DD), of_image(GRID, PIX), const(DD, PIX), const(24, D), const(DD, PIX), const(1, PIX)]
    if pixels is not None:
        args.append(pixels)
        specs.append(pl.BlockSpec(memory_space=pl.ANY))
    return pl.pallas_call(
        pixel_kernel,
        grid_spec=pltpu.PrefetchScalarGridSpec(
            num_scalar_prefetch=1,
            grid=(n,),
            in_specs=specs,
            out_specs=[of_image(GRID, PIX), const(DD, PIX), const(1, PIX)],
        ),
        out_shape=[
            jax.ShapeDtypeStruct((IMG_DEV, GRID, PIX), jnp.bfloat16),
            jax.ShapeDtypeStruct((DD, PIX), jnp.float32),
            jax.ShapeDtypeStruct((1, PIX), jnp.float32),
        ],
        input_output_aliases={} if pixels is None else {7: 0},
        compiler_params=params(32),
        cost_estimate=cost(0.8 * n),
        name="decoder_pixels",
    )(*args)


def with_role(kernel, grid, in_specs, out_specs, out_shape, mib, name, scratch=()):
    return pl.pallas_call(
        kernel,
        grid_spec=pltpu.PrefetchScalarGridSpec(
            num_scalar_prefetch=1,
            grid=grid,
            in_specs=in_specs,
            out_specs=out_specs,
            scratch_shapes=list(scratch),
        ),
        out_shape=out_shape,
        compiler_params=params(mib),
        cost_estimate=cost(10),
        name=name,
    )


def half_columns(mine):
    return pl.BlockSpec((ROWS, HALF), lambda i, role: (0, role[0] if mine else 1 - role[0]))


def half_tiles(mine):
    return pl.BlockSpec(
        (ROWS, HALF), lambda i, role: (0, 2 * i + (role[0] if mine else 1 - role[0]))
    )


C_ONE, C_TWO, C_THREE = FF + 2 * DD, FF + D, 3 * D + 128
THREE_CUT = (C_THREE // 128 + 1) // 2 * 128


def line_first():
    to = lax.broadcasted_iota(jnp.int32, (HALF, HALF), 0)
    place = to % 96 // 24 * 96 + to % 24 // 6 * 24 + to // 96 * 6 + to % 6
    return (lax.broadcasted_iota(jnp.int32, (HALF, HALF), 1) == place).astype(jnp.bfloat16)


def down_grad_kernel(role_ref, turn_ref, gemb_ref, gb2_ref, enc_mine, enc_other, act_mine, act_other, pix_mine, pix_other,
                     mine_ref, other_ref, dbias_ref, demb_ref):
    j = pl.program_id(0)

    def turned(rows):
        return dot_nn(turn_ref[...], rows.astype(jnp.bfloat16)).astype(jnp.bfloat16)

    @pl.when(j == 0)
    def _():
        dbias_ref[...] = jnp.sum(gb2_ref[...].astype(jnp.float32), axis=0, keepdims=True)
        demb_ref[...] = jnp.sum(gemb_ref[...].astype(jnp.float32), axis=0, keepdims=True)
        for ref, enc, pix in ((mine_ref, enc_mine, pix_mine), (other_ref, enc_other, pix_other)):
            ref[:, FF : FF + DD] = turned(dot_tn(enc[...], gemb_ref[...]))
            ref[:, FF + DD :] = turned(pix[...])

    at = pl.ds(pl.multiple_of(j * D, D), D)
    mine_ref[:, at] = turned(dot_tn(act_mine[...], gb2_ref[...]))
    other_ref[:, at] = turned(dot_tn(act_other[...], gb2_ref[...]))


def down_grad(role, gemb, gb2, enc, act, dpix):
    return with_role(
        down_grad_kernel,
        (PART,),
        [
            const(HALF, HALF),
            const(ROWS, DD),
            const(ROWS, D),
            half_columns(True),
            half_columns(False),
            half_tiles(True),
            half_tiles(False),
            pl.BlockSpec((HALF, DD), lambda i, role: (role[0], 0)),
            pl.BlockSpec((HALF, DD), lambda i, role: (1 - role[0], 0)),
        ],
        [const(HALF, C_ONE), const(HALF, C_ONE), const(1, D), const(1, DD)],
        [
            jax.ShapeDtypeStruct((HALF, C_ONE), jnp.bfloat16),
            jax.ShapeDtypeStruct((HALF, C_ONE), jnp.bfloat16),
            jax.ShapeDtypeStruct((1, D), jnp.float32),
            jax.ShapeDtypeStruct((1, DD), jnp.float32),
        ],
        48,
        "down_grad",
    )(role, line_first(), gemb, gb2, enc, enc, act, act, dpix, dpix)


def hidden_back_kernel(gemb_ref, we_ref, wd_ref, wu_ref, slope_ref, resid_ref, wo_ref, rows_ref,
                       gb2_ref, gh_ref, gres_ref, gb_ref, gatt_ref, dup_ref, dvec_ref, total, genc):
    j = pl.program_id(0)

    @pl.when(j == 0)
    def _():
        genc[...] = dot_nt(gemb_ref[...], we_ref[...])
        gb2_ref[...] = genc[...].astype(jnp.bfloat16)
        dup_ref[...] = jnp.zeros_like(dup_ref)

    gh = (dot_nt(gb2_ref[...], wd_ref[...]) * slope_ref[...].astype(jnp.float32)).astype(jnp.bfloat16)
    gh_ref[...] = gh
    dup_ref[pl.ds(j, 1)] = jnp.sum(gh.astype(jnp.float32), axis=0, keepdims=True)
    part = dot_nt(gh, wu_ref[...])

    @pl.when(j == 0)
    def _():
        total[...] = part

    @pl.when(j > 0)
    def _():
        total[...] += part

    @pl.when(j == PART - 1)
    def _():
        back, dgain, dshift = norm_back(resid_ref[...], rows_ref[G2 : G2 + 1], total[...])
        gres = genc[...] + back
        gres_ref[...] = gres
        gb = gres.astype(jnp.bfloat16)
        gb_ref[...] = gb
        gatt_ref[...] = dot_nt(gb, wo_ref[...]).astype(jnp.bfloat16)
        dvec_ref[...] = jnp.concatenate(
            [
                dgain,
                dshift,
                jnp.sum(gb.astype(jnp.float32), axis=0, keepdims=True),
                jnp.zeros((5, D), jnp.float32),
            ],
            axis=0,
        )


def hidden_back(half, earlier, gemb, whole, slope, resid, rows):
    return in_halves(
        hidden_back_kernel,
        half,
        earlier,
        [
            const(CHUNK, DD),
            columns(DD, EMB_AT),
            tile_columns(DOWN_AT),
            tile_columns(UP_AT),
            tile_of(half),
            rows_of(half, D),
            columns(D, OUT_AT),
            const(24, D),
        ],
        [
            rows_of(half, D),
            tile_of(half),
            rows_of(half, D),
            rows_of(half, D),
            rows_of(half, D),
            const(8, D),
            const(8, D),
        ],
        [
            jax.ShapeDtypeStruct((ROWS, D), jnp.bfloat16),
            jax.ShapeDtypeStruct((ROWS, FF), jnp.bfloat16),
            jax.ShapeDtypeStruct((ROWS, D), jnp.float32),
            jax.ShapeDtypeStruct((ROWS, D), jnp.bfloat16),
            jax.ShapeDtypeStruct((ROWS, D), jnp.bfloat16),
            jax.ShapeDtypeStruct((8, D), jnp.float32),
            jax.ShapeDtypeStruct((8, D), jnp.float32),
        ],
        (0, 1, 2, 3, 4),
        48,
        "hidden_back",
        [pltpu.VMEM((CHUNK, D), jnp.float32)] * 2,
        [gemb, whole, whole, whole, slope, resid, whole, rows],
    )


BLOCKS = HALF // 24


def put_blocks(ref, columns, rows):
    for n in range(BLOCKS):
        ref[n, :, columns] = rows[24 * n : 24 * n + 24].astype(jnp.bfloat16)


def up_grad_kernel(role_ref, n2_mine, n2_other, gh_ref, att_mine, att_other, gb_ref, mine_ref, other_ref):
    j = pl.program_id(0)
    at = pl.ds(pl.multiple_of(j * D, D), D)
    put_blocks(mine_ref, at, dot_tn(n2_mine[...], gh_ref[...]))
    put_blocks(other_ref, at, dot_tn(n2_other[...], gh_ref[...]))

    @pl.when(j == PART - 1)
    def _():
        put_blocks(mine_ref, slice(FF, C_TWO), dot_tn(att_mine[...], gb_ref[...]))
        put_blocks(other_ref, slice(FF, C_TWO), dot_tn(att_other[...], gb_ref[...]))


def up_grad(role, n2, gh, attended, gb):
    return with_role(
        up_grad_kernel,
        (PART,),
        [
            half_columns(True),
            half_columns(False),
            pl.BlockSpec((ROWS, D), lambda j, role: (0, j)),
            half_columns(True),
            half_columns(False),
            const(ROWS, D),
        ],
        [const(BLOCKS, 24, C_TWO), const(BLOCKS, 24, C_TWO)],
        [
            jax.ShapeDtypeStruct((BLOCKS, 24, C_TWO), jnp.bfloat16),
            jax.ShapeDtypeStruct((BLOCKS, 24, C_TWO), jnp.bfloat16),
        ],
        40,
        "up_grad",
    )(role, n2, n2, gh, attended, attended, gb)


def attention_back_kernel(count_ref, mixed_ref, gatt_ref, gmix_ref, held, gheld):
    live = lax.broadcasted_iota(jnp.int32, (SLOT, SLOT), 0) < count_ref[pl.program_id(0)]
    masks = head_masks()
    low_lane = lax.broadcasted_iota(jnp.int32, (SLOT, 128), 1) < HD
    scale = HD ** (-0.5)
    for pair in range(H // 2):
        c = pair * 128
        held[pair] = dot_nt(stacked(mixed_ref[:, D + c : D + c + 128], masks), mixed_ref[:, c : c + 128])
        gheld[pair] = dot_nt(
            stacked(mixed_ref[:, 2 * D + c : 2 * D + c + 128], masks), gatt_ref[:, c : c + 128]
        )
    for pair in range(H // 2):
        c = pair * 128
        probs = key_probs(held[pair], live)
        gscores = []
        for k in range(2):
            p, g = probs[k], gheld[pair, SLOT * k : SLOT * k + SLOT]
            gscores.append(p * (g - jnp.sum(p * g, axis=0, keepdims=True)))
        gscores = jnp.concatenate(gscores, axis=0).astype(jnp.bfloat16)
        probs = jnp.concatenate(probs, axis=0).astype(jnp.bfloat16)
        gv = dot_nn(probs, gatt_ref[:, c : c + 128])
        gk = dot_nn(gscores, mixed_ref[:, c : c + 128]) * scale
        gq = dot_tn(gscores, stacked(mixed_ref[:, D + c : D + c + 128], masks)) * scale
        gmix_ref[:, c : c + 128] = gq.astype(jnp.bfloat16)
        gmix_ref[:, D + c : D + c + 128] = jnp.where(low_lane, gk[:SLOT], gk[SLOT:]).astype(jnp.bfloat16)
        gmix_ref[:, 2 * D + c : 2 * D + c + 128] = jnp.where(
            low_lane, gv[:SLOT], gv[SLOT:]
        ).astype(jnp.bfloat16)


def attention_back(count, mixed, gatt):
    wide = pl.BlockSpec((SLOT, 3 * D), lambda s: (s, 0))
    return pl.pallas_call(
        attention_back_kernel,
        grid=(IMG_DEV,),
        in_specs=[
            pl.BlockSpec(memory_space=pltpu.SMEM),
            wide,
            pl.BlockSpec((SLOT, D), lambda s: (s, 0)),
        ],
        out_specs=wide,
        out_shape=jax.ShapeDtypeStruct((ROWS, 3 * D), jnp.bfloat16),
        scratch_shapes=[pltpu.VMEM((H // 2, 2 * SLOT, SLOT), jnp.float32)] * 2,
        compiler_params=params(32),
        cost_estimate=cost(7),
        name="attention_back",
    )(count, mixed, gatt)


def input_back_kernel(role_ref, gmix_ref, w_ref, x_ref, gres_ref, rows_ref, normed_mine, normed_other,
                      dup_ref, d2_ref, ddown_ref, dpb_ref, d3_ref, demb_ref,
                      pg_ref, mine_ref, other_ref, total, turned):
    j = pl.program_id(0)
    at = pl.ds(pl.multiple_of(j * D, D), D)
    gmix = gmix_ref[...]
    put_blocks(mine_ref, at, dot_tn(normed_mine[...], gmix))
    put_blocks(other_ref, at, dot_tn(normed_other[...], gmix))
    part = dot_nt(gmix, w_ref[...])
    dbias = jnp.sum(gmix.astype(jnp.float32), axis=0, keepdims=True)

    @pl.when(j == 0)
    def _():
        total[...] = part
        turned[QB : QB + 1] = dbias

    @pl.when(j > 0)
    def _():
        total[...] += part

    @pl.when(j == 2)
    def _():
        back, dgain, dshift = norm_back(
            x_ref[...].astype(jnp.float32), rows_ref[G1 : G1 + 1], total[...]
        )
        pg_ref[...] = (gres_ref[...] + back).astype(jnp.bfloat16)
        turned[G1 : G1 + 1] = dgain
        turned[S1 : S1 + 1] = dshift
        turned[VB : VB + 1] = dbias
        turned[OB : OB + 1] = d2_ref[2:3]
        turned[G2 : G2 + 1] = d2_ref[0:1]
        turned[S2 : S2 + 1] = d2_ref[1:2]
        turned[DB : DB + 1] = ddown_ref[...]
        turned[PB : PB + 1] = dpb_ref[...]
        turned[UB : UB + 4] = dup_ref[0:4]
        turned[13:16] = jnp.zeros((3, D), jnp.float32)
        four = jnp.concatenate([demb_ref[...], d3_ref[1:4], jnp.zeros((4, DD), jnp.float32)], axis=0)
        turned[16:24] = dot_nt(four.astype(jnp.bfloat16), spread())
        block = jnp.concatenate([turned[...], jnp.zeros((104, D), jnp.float32)], axis=0).T
        first, second = block[:HALF], block[HALF:]
        up = role_ref[0] == 1
        put_blocks(mine_ref, slice(3 * D, C_THREE), jnp.where(up, second, first))
        put_blocks(other_ref, slice(3 * D, C_THREE), jnp.where(up, first, second))


def input_back(role, gmix, whole, x, gres, rows, normed, dup, d2, ddown, dpb, d3, demb):
    return with_role(
        input_back_kernel,
        (3,),
        [
            pl.BlockSpec((ROWS, D), lambda j, role: (0, j)),
            pl.BlockSpec((D, D), lambda j, role: (0, j)),
            const(ROWS, D),
            const(ROWS, D),
            const(24, D),
            half_columns(True),
            half_columns(False),
            const(8, D),
            const(8, D),
            const(1, D),
            const(1, D),
            const(8, DD),
            const(1, DD),
        ],
        [const(ROWS, D), const(BLOCKS, 24, C_THREE), const(BLOCKS, 24, C_THREE)],
        [
            jax.ShapeDtypeStruct((ROWS, D), jnp.bfloat16),
            jax.ShapeDtypeStruct((BLOCKS, 24, C_THREE), jnp.bfloat16),
            jax.ShapeDtypeStruct((BLOCKS, 24, C_THREE), jnp.bfloat16),
        ],
        48,
        "input_back",
        [pltpu.VMEM((ROWS, D), jnp.float32), pltpu.VMEM((24, D), jnp.float32)],
    )(role, gmix, whole, x, gres, rows, normed, normed, dup, d2, ddown, dpb, d3, demb)


def hot(shape, test):
    return test(
        lax.broadcasted_iota(jnp.int32, shape, 0), lax.broadcasted_iota(jnp.int32, shape, 1)
    ).astype(jnp.bfloat16)


def hidden_order():
    return hot((512, 512), lambda l, c: l == 4 * (c % 128) + c // 128)


def pack_kernel(qkv_ref, out_ref, up_ref, down_ref, emb_ref, pix_ref, *refs):
    six_refs, bias_ref, four_refs, packed_ref = refs[:9], refs[9], refs[10:14], refs[14]
    packed_ref[:, :OUT_AT] = qkv_ref[...]
    packed_ref[:, OUT_AT:UP_AT] = out_ref[...]
    order = hidden_order()
    for r in range(D // 128):
        turned = dot_nn(up_ref[:, 512 * r : 512 * r + 512], order).astype(jnp.bfloat16)
        for j in range(PART):
            at = UP_AT + j * D + 128 * r
            packed_ref[:, at : at + 128] = turned[:, 128 * j : 128 * j + 128]
    for j in range(PART):
        rows = hot((6, 24), lambda i, l: l == 4 * i + j)
        packed_ref[:, DOWN_AT + j * D : DOWN_AT + j * D + D] = dot_nn(rows, down_ref[...]).astype(jnp.bfloat16)
    packed_ref[:, EMB_AT:PIX_AT] = emb_ref[...]
    for t in range(2):
        part = jnp.zeros((6, 256), jnp.float32)
        for s in range(3):
            rows = hot((6, 4), lambda r, i: 2 * r + t == 3 * i + s)
            part = part + dot_nn(rows, pix_ref[:, 256 * s : 256 * s + 256])
        packed_ref[:, PIX_AT + 256 * t : PIX_AT + 256 * t + 256] = part.astype(jnp.bfloat16)
    lane = lax.broadcasted_iota(jnp.int32, (6, 128), 1)
    block = jnp.zeros((6, 128), jnp.float32)

    def put(block, ref, count, start, pick):
        size = ref.shape[0]
        line = jnp.broadcast_to(ref[...].astype(jnp.float32).reshape(1, size), (6, size))
        row = lax.broadcasted_iota(jnp.int32, (6, size), 0)
        at = lax.broadcasted_iota(jnp.int32, (6, size), 1)
        for c in range(count):
            column = jnp.sum(jnp.where(at == pick(row, c), line, 0.0), axis=1, keepdims=True)
            block = jnp.where(lane == start + c, column, block)
        return block

    for n, ref in enumerate(six_refs):
        block = put(block, ref, 1, n, lambda row, c: row)
    block = put(block, bias_ref, PART, UB, lambda row, c: PART * row + c)
    for n, ref in enumerate(four_refs):
        block = put(block, ref, 1, 16 + n, lambda row, c: row)
    packed_ref[:, VEC_AT:] = block.astype(jnp.bfloat16)


def packing_kernel(*refs):
    n = (len(refs) - 2) // 2
    given, packed_ref, held, sems = refs[:n], refs[n], refs[n + 1 : 2 * n + 1], refs[-1]
    copies = [
        pltpu.make_async_copy(source, place, sems.at[i])
        for i, (source, place) in enumerate(zip(given, held))
    ]
    for copy in copies:
        copy.start()
    for copy in copies:
        copy.wait()
    pack_kernel(*held, packed_ref)


def pack(*args):
    return pl.pallas_call(
        packing_kernel,
        in_specs=[pl.BlockSpec(memory_space=pltpu.HBM)] * len(args),
        out_shape=jax.ShapeDtypeStruct((6, WIDE), jnp.bfloat16),
        scratch_shapes=[pltpu.VMEM(arg.shape, arg.dtype) for arg in args]
        + [pltpu.SemaphoreType.DMA((len(args),))],
        compiler_params=pltpu.CompilerParams(vmem_limit_bytes=64 * MIB - 65536),
        cost_estimate=cost(4),
        name="pack",
    )(*args)


def unpack_kernel(kept_one, came_one, kept_two, came_two, qkv_ref, out_ref, up_ref, down_ref, emb_ref, pix_ref, vec_ref):
    first, second = (kept_one, came_one), (kept_two, came_two)

    def total(pair, at, width):
        return sum(ref[:, at : at + width].astype(jnp.float32) for ref in pair)

    def shuffled(pair, dot):
        return dot(pair[0]) + dot(pair[1])

    two_at, three_at = C_TWO // 2, THREE_CUT

    def spot(group, column):
        if group == 2:
            return column if column < two_at else column + three_at
        return column + two_at if column < three_at else column + C_TWO

    for column in range(0, 3 * D, 128):
        qkv_ref[:, column : column + 128] = total(second, spot(3, column), 128)
    for column in range(0, D, 128):
        out_ref[:, column : column + 128] = total(second, spot(2, FF + column), 128)
    emb_ref[...] = total(first, FF, DD)
    vec_ref[...] = total(second, spot(3, 3 * D), 128)
    order = hidden_order()
    for r in range(D // 128):

        def turned(ref):
            starts = [spot(2, j * D + 128 * r) for j in range(PART)]
            parts = [ref[:, at : at + 128] for at in starts]
            return dot_nt(jnp.concatenate(parts, axis=1), order)

        up_ref[:, 512 * r : 512 * r + 512] = shuffled(second, turned)
    down = jnp.zeros((24, D), jnp.float32)
    for j in range(PART):
        rows = hot((24, 6), lambda l, i: l == 4 * i + j)
        down = down + shuffled(first, lambda ref: dot_nn(rows, ref[:, j * D : j * D + D]))
    down_ref[...] = down
    for s in range(3):
        part = jnp.zeros((4, 256), jnp.float32)
        for t in range(2):
            rows = hot((4, 6), lambda i, r: 2 * r + t == 3 * i + s)
            at = FF + DD + 256 * t
            part = part + shuffled(first, lambda ref: dot_nn(rows, ref[:, at : at + 256]))
        pix_ref[:, 256 * s : 256 * s + 256] = part


def turn_kernel(plan, bits_ref, *refs):
    inputs = [len(term) for group in plan for term in group["terms"]]
    given = iter(refs[: sum(inputs)])
    out = iter(refs[sum(inputs) :])
    for group in plan:
        terms = [([next(given) for _ in term], group["columns"]) for term in group["terms"]]
        kept_ref, sent_ref = next(out), next(out)
        bit = bits_ref[group["bit"]]
        column = 0
        for term, columns in terms:
            start, width = columns or (0, term[0].shape[-1])
            source, to = slice(start, start + width), slice(column, column + width)
            column += width

            def added(*at):
                return sum(ref[(*at, slice(None), source)].astype(jnp.float32) for ref in term)

            if group["dim"] is None:
                rows = term[0].shape[-2] // 2
                value = added(*[0] * (len(term[0].shape) - 2))
                low, high = value[:rows], value[rows:]
                kept_ref[:, to] = jnp.where(bit == 1, high, low).astype(jnp.bfloat16)
                sent_ref[:, to] = jnp.where(bit == 1, low, high).astype(jnp.bfloat16)
                continue
            p, q = kept_ref.shape[:2]
            for ref, half in ((kept_ref, bit), (sent_ref, 1 - bit)):
                for i in range(p):
                    for j in range(q):
                        at = (half * p + i, j) if group["dim"] == 0 else (i, half * q + j)
                        ref[i, j, :, to] = added(*at).astype(jnp.bfloat16)


def turn(bits, *groups):
    plan, args, shapes = [], [], []
    for terms, dim, bit, columns in groups:
        plan.append(dict(terms=terms, dim=dim, bit=bit, columns=columns))
        for term in terms:
            args += term
        width = sum(columns[1] if columns else term[0].shape[-1] for term in terms)
        shape = list(terms[0][0].shape[:-1])
        if dim is None:
            shape = [shape[-1] // 2]
        else:
            shape[dim] //= 2
        shapes += [jax.ShapeDtypeStruct((*shape, width), jnp.bfloat16)] * 2
    plan = [dict(group, terms=[[None] * len(term) for term in group["terms"]]) for group in plan]
    out = pl.pallas_call(
        functools.partial(turn_kernel, plan),
        in_specs=[pl.BlockSpec(memory_space=pltpu.SMEM)]
        + [pl.BlockSpec(memory_space=pltpu.VMEM)] * len(args),
        out_shape=shapes,
        compiler_params=pltpu.CompilerParams(vmem_limit_bytes=32 * MIB),
        cost_estimate=cost(3),
        name="turn",
    )(bits, *args)
    return [tuple(out[n : n + 2]) for n in range(0, len(out), 2)]


def unpack(*terms):
    return pl.pallas_call(
        unpack_kernel,
        out_shape=[
            jax.ShapeDtypeStruct(shape, jnp.float32)
            for shape in ((6, 3 * D), (6, D), (6, FF), (24, D), (6, DD), (4, PIX), (6, 128))
        ],
        compiler_params=pltpu.CompilerParams(vmem_limit_bytes=16 * MIB),
        cost_estimate=cost(4),
        name="unpack",
    )(*terms)


PAIRS = {
    "high": [(0, 3), (3, 0), (1, 2), (2, 1)],
    "low": [(0, 1), (1, 0), (2, 3), (3, 2)],
}


ROLE_PAIR = [(0, 1), (1, 0)]


def tie(*arrays):
    return lax.optimization_barrier(arrays)


def moved(images, step, crossing=False):
    pairs = [
        (r * N_DP + p, (r ^ crossing) * N_DP + (p + step) % N_DP)
        for r in range(2)
        for p in range(N_DP)
    ]
    return lax.ppermute(images, ALL, pairs)


def added(mine, came):
    return (mine.astype(jnp.float32) + came.astype(jnp.float32)).astype(jnp.bfloat16)


def sent_on(axis, which, halves):
    return halves[0], lax.ppermute(halves[1], axis, PAIRS[which])


def body(
    patch_rows,
    patch_order,
    visible_count,
    encoded_image,
    first_gain,
    first_shift,
    query_key_value,
    query_bias,
    value_bias,
    output_weight,
    output_bias,
    second_gain,
    second_shift,
    up_weight,
    up_bias,
    down_weight,
    down_bias,
    embed_weight,
    embed_bias,
    mask_token,
    decoder_gain,
    decoder_shift,
    pixel_weight,
    pixel_bias,
    pixel_grad,
):
    device = lax.axis_index(ALL)
    role = lax.axis_index("role").astype(jnp.int32).reshape(1)
    image_count = encoded_image.shape[0]

    own_images = device * IMG_DEV + jnp.arange(IMG_DEV, dtype=jnp.int32)
    found = encoded_image[None, :] == own_images[:, None]
    source_slot = jnp.sum(
        jnp.where(found, jnp.arange(image_count, dtype=jnp.int32)[None, :], 0), axis=1
    )
    source_place = source_slot % IMG_DEV
    image_of = jnp.sum(
        jnp.where(
            source_place[None, :] == jnp.arange(IMG_DEV, dtype=jnp.int32)[:, None],
            jnp.arange(IMG_DEV, dtype=jnp.int32)[None, :],
            0,
        ),
        axis=1,
    )
    own_count = lax.dynamic_slice_in_dim(visible_count, device * IMG_DEV, IMG_DEV)
    own_order = lax.dynamic_slice_in_dim(patch_order, device * IMG_DEV, IMG_DEV, 0)[:, None, :SLOT]
    first, later = image_of[jnp.array([0, 4])], image_of[jnp.array([1, 5, 2, 6, 3, 7])]

    packed = pack(
        query_key_value,
        output_weight,
        up_weight,
        down_weight,
        embed_weight,
        pixel_weight,
        first_gain,
        first_shift,
        query_bias,
        value_bias,
        output_bias,
        second_gain,
        second_shift,
        down_bias,
        pixel_bias,
        up_bias,
        embed_bias,
        mask_token,
        decoder_gain,
        decoder_shift,
    )
    whole = lax.all_gather(packed, "x", tiled=True)
    whole = lax.all_gather(whole, ("role", "y", "z"), tiled=True)
    pix_weight = whole[:, PIX_AT:VEC_AT].reshape(DD, PIX)

    held = lax.dynamic_slice_in_dim(encoded_image, device * IMG_DEV, IMG_DEV)
    count = visible_count[held]

    normed, mixed, attended, rows, fours = attention(count, patch_rows, whole)
    half = forward(1, None, patch_rows, attended, whole, rows, fours)
    high = moved(half[5].reshape(4, SLOT, DD), 4, True)
    half = forward(0, half, patch_rows, attended, whole, rows, fours)
    resid, normed_two, active, slope, encoded, embedded = half
    embedded, high = tie(embedded, high)
    low = moved(embedded.reshape(4, SLOT, DD), 0, True)
    steps = [
        moved(jnp.concatenate([low[s : s + 1], high[s : s + 1]]), s) for s in range(1, 4)
    ]
    table = positions()
    zeros = jnp.zeros((8, DD), jnp.float32), jnp.zeros((DD, PIX), jnp.float32), jnp.zeros((1, PIX), jnp.float32)
    grad_first, decoded, d_three = decoder_grid(
        first,
        own_count[first],
        own_order[first],
        jnp.concatenate([low[:1], high[:1]]),
        table,
        pix_weight,
        fours,
        pixel_grad,
        zeros[0],
    )
    pixels, d_pix, d_pix_bias = decoder_pixels(
        first, decoded, pixel_grad, pix_weight, rows, zeros[1], zeros[2]
    )
    d_pix, *steps = tie(d_pix, *steps)
    grad_later, decoded, d_three = decoder_grid(
        later,
        own_count[later],
        own_order[later],
        jnp.concatenate(steps),
        table,
        pix_weight,
        fours,
        pixel_grad,
        d_three,
    )
    steps = [moved(grad_later[2 * s - 2 : 2 * s], -s) for s in range(1, 4)]
    pixels, d_pix, d_pix_bias = decoder_pixels(
        later, decoded, pixel_grad, pix_weight, rows, d_pix, d_pix_bias, pixels
    )
    d_pix, *steps = tie(d_pix, *steps)
    high = moved(jnp.concatenate([grad_first[1:]] + [s[1:] for s in steps]), -4, True).reshape(CHUNK, DD)
    low = moved(jnp.concatenate([grad_first[:1]] + [s[:1] for s in steps]), 0, True).reshape(CHUNK, DD)
    half = hidden_back(0, None, low, whole, slope, resid, rows)
    d_up_bias, d_second = half[5:]
    high, part = tie(high, half[0])
    half = hidden_back(1, [part, *half[1:]], high, whole, slope, resid, rows)
    branch_two, grad_hidden, grad_resid, grad_branch, grad_attended = half[:5]
    d_up_bias, d_second = d_up_bias + half[5], d_second + half[6]
    mine_one, other_one, d_down_bias, d_emb_bias = down_grad(
        role,
        jnp.concatenate([low, high]),
        branch_two,
        encoded,
        active,
        d_pix.astype(jnp.bfloat16).reshape(D, DD),
    )
    grad_hidden, other_one = tie(grad_hidden, other_one)
    came_one = lax.ppermute(other_one, "role", ROLE_PAIR)
    mine_two, other_two = up_grad(role, normed_two, grad_hidden, attended, grad_branch)
    mine_one, came_one, other_two = tie(mine_one, came_one, other_two)
    part_one, grad_attended, other_two = tie(added(mine_one, came_one), grad_attended, other_two)
    part_one = lax.psum_scatter(part_one, "x", tiled=True)
    came_two = lax.ppermute(other_two, "role", ROLE_PAIR)
    grad_mixed = attention_back(count, mixed, grad_attended)
    grad_mixed, came_two = tie(grad_mixed, came_two)
    ring = [lax.axis_index(axis) for axis in "yzx"]
    bits = jnp.stack([at // 2 for at in ring] + [at % 2 for at in ring]).astype(jnp.int32)
    y_high, z_high, x_high, y_low, z_low, x_low = range(6)

    def in_planes(array):
        return array.reshape(4, 4, 24, array.shape[-1])

    def parted(mine, came, cut):
        term = [in_planes(mine), in_planes(came)]
        width = mine.shape[-1]
        return ([term], 1, z_high, (0, cut)), ([term], 0, y_high, (cut, width - cut))

    first_two, second_two = turn(bits, *parted(mine_two, came_two, C_TWO // 2))
    grad_mixed, *both = tie(grad_mixed, *first_two, *second_two)
    first_two, second_two = sent_on("z", "high", both[:2]), sent_on("y", "high", both[2:])
    patch_grad, mine, other = input_back(
        role,
        grad_mixed,
        whole,
        patch_rows,
        grad_resid,
        rows,
        normed,
        d_up_bias,
        d_second,
        d_down_bias,
        d_pix_bias,
        d_three,
        d_emb_bias,
    )
    mine, other, came_a, came_b = tie(mine, other, first_two[1], second_two[1])
    first_two, second_two = (first_two[0], came_a), (second_two[0], came_b)
    came_three = lax.ppermute(other, "role", ROLE_PAIR)
    first_three, second_three = turn(bits, *parted(mine, came_three, THREE_CUT))
    first_three = sent_on("z", "high", first_three)
    second_three = sent_on("y", "high", second_three)
    one = part_one.reshape(4, 1, 24, C_ONE)
    first, second, one = turn(
        bits,
        ([first_two, first_three], 1, z_low, None),
        ([second_two, second_three], 0, y_low, None),
        ([[one]], 0, y_high, None),
    )
    first, second, one = sent_on("z", "low", first), sent_on("y", "low", second), sent_on("y", "high", one)
    first, second, one = turn(
        bits, ([first], 0, y_high, None), ([second], 1, z_high, None), ([one], 0, y_low, None)
    )
    first, second, one = sent_on("y", "high", first), sent_on("z", "high", second), sent_on("y", "low", one)
    first, second, one = turn(
        bits, ([first], 0, y_low, None), ([second], 1, z_low, None), ([one], None, z_high, None)
    )
    first, second, one = sent_on("y", "low", first), sent_on("z", "low", second), sent_on("z", "high", one)
    rest, one = turn(bits, ([first, second], None, x_high, None), ([one], None, z_low, None))
    rest, one = sent_on("x", "high", rest), sent_on("z", "low", one)
    (rest,) = turn(bits, ([rest], None, x_low, None))
    rest = sent_on("x", "low", rest)
    d_qkv, d_out, d_up, d_down, d_emb, d_pix, vec = unpack(*one, *rest)
    return (
        pixels,
        patch_grad,
        vec[:, G1],
        vec[:, S1],
        d_qkv,
        vec[:, QB],
        vec[:, VB],
        d_out,
        vec[:, OB],
        vec[:, G2],
        vec[:, S2],
        d_up,
        vec[:, UB : UB + PART].reshape(6 * PART),
        d_down,
        vec[:, DB],
        d_emb,
        vec[:4, 16 + EB],
        vec[:4, 16 + TOK],
        vec[:4, 16 + G3],
        vec[:4, 16 + S3],
        d_pix,
        vec[:, PB],
    )


def solution(mesh):
    mesh = Mesh(mesh.devices.reshape(2, 4, 4, 4), ALL)
    two, one = P(ALL, None), P(ALL)
    placed = (two, P(), P(), P(), one, one, two, one, one, two, one, one, one, two, one, two, one)
    placed += (two, one, one, one, one, two, one, P(ALL, None, None))
    given = (P(ALL, None, None), two, one, one, two, one, one, two, one, one, one, two, one, two, one)
    given += (two, one, one, one, one, two, one)
    return jax.shard_map(body, mesh=mesh, in_specs=placed, out_specs=given, check_vma=False)
```

```python
import functools

import jax
import jax.numpy as jnp
from jax import lax
from jax.experimental import pallas as pl
from jax.experimental.pallas import tpu as pltpu
from jax.sharding import Mesh
from jax.sharding import PartitionSpec as P

D = 768
H = 12
HD = 64
FF = 3072
DD = 512
PIX = 768
SIDE = 14
SLOT = 80
IMG_DEV = 8
GRID = 196
N_DP = 64
PART = FF // D

ALL = ("role", "y", "z", "x")

epsilon = 1e-06
masked_score = -1e30

def positions():
    quarter = DD // 4
    frequency = 10000.0 ** (-jnp.arange(quarter, dtype=jnp.float32) / quarter)
    places = jnp.arange(GRID, dtype=jnp.int32)
    row_angle = (places // SIDE).astype(jnp.float32)[:, None] * frequency[None, :]
    col_angle = (places % SIDE).astype(jnp.float32)[:, None] * frequency[None, :]
    return jnp.concatenate(
        [jnp.sin(row_angle), jnp.cos(row_angle), jnp.sin(col_angle), jnp.cos(col_angle)], axis=1
    )


HALF = D // 2
ROWS = IMG_DEV * SLOT
CHUNK = ROWS // 2
OUT_AT, UP_AT, DOWN_AT, EMB_AT, PIX_AT, VEC_AT = 3 * D, 4 * D, 8 * D, 12 * D, 12 * D + DD, 12 * D + 2 * DD
WIDE = VEC_AT + 128
G1, S1, QB, VB, OB, G2, S2, DB, PB, UB = range(10)
EB, TOK, G3, S3 = range(4)

MIB = 1 << 20


def cost(us):
    return pl.CostEstimate(flops=int(us * 1e9), bytes_accessed=0, transcendentals=0)


def params(mib):
    return pltpu.CompilerParams(
        dimension_semantics=("arbitrary",), vmem_limit_bytes=mib * MIB
    )


def const(*shape):
    return pl.BlockSpec(shape, lambda i, *_: (0,) * len(shape))


def columns(width, at):
    return pl.BlockSpec((D, width), lambda i, *_: (0, at // width))


def tile_columns(at):
    return pl.BlockSpec((D, D), lambda i, *_: (0, at // D + i))


def dot_nn(a, b):
    return lax.dot_general(a, b, (((1,), (0,)), ((), ())), preferred_element_type=jnp.float32)


def dot_nt(a, b):
    return lax.dot_general(a, b, (((1,), (1,)), ((), ())), preferred_element_type=jnp.float32)


def dot_tn(a, b):
    return lax.dot_general(a, b, (((0,), (0,)), ((), ())), preferred_element_type=jnp.float32)


def normalised(values):
    average = jnp.mean(values, axis=-1, keepdims=True)
    centered = values - average
    variance = jnp.mean(centered * centered, axis=-1, keepdims=True)
    inverse = lax.rsqrt(variance + epsilon)
    return centered * inverse, inverse


def norm_back(values, gain, upstream):
    h, inverse = normalised(values)
    dh = upstream * gain
    dv = (
        dh - jnp.mean(dh, axis=-1, keepdims=True) - h * jnp.mean(dh * h, axis=-1, keepdims=True)
    ) * inverse
    return (
        dv,
        jnp.sum(upstream * h, axis=0, keepdims=True),
        jnp.sum(upstream, axis=0, keepdims=True),
    )


def strips(count, body, size=16, at_once=10):
    def some(i, carry):
        for n in range(at_once):
            body(pl.ds(pl.multiple_of((i * at_once + n) * size, size), size))
        return carry

    lax.fori_loop(0, count // (at_once * size), some, 0)


def spread():
    row = lax.broadcasted_iota(jnp.int32, (D, DD), 0)
    col = lax.broadcasted_iota(jnp.int32, (D, DD), 1)
    return (row == 6 * (col // 4) + col % 4).astype(jnp.bfloat16)


def head_masks():
    lane = lax.broadcasted_iota(jnp.int32, (1, 2 * HD), 1)
    low = (lane < HD).astype(jnp.bfloat16)
    return low, (1.0 - low.astype(jnp.float32)).astype(jnp.bfloat16)


def stacked(pair, masks):
    return jnp.concatenate([pair * masks[0], pair * masks[1]], axis=0)


def key_probs(scores, live):
    both = []
    for k in range(2):
        s = jnp.where(live, scores[SLOT * k : SLOT * k + SLOT] * HD ** (-0.5), masked_score)
        e = jnp.exp(s - jnp.max(s, axis=0, keepdims=True))
        both.append(e * (1.0 / jnp.sum(e, axis=0, keepdims=True)))
    return both


def attention_kernel(count_ref, x_ref, w_ref, vec_ref, normed_ref, mixed_ref, att_ref, rows_ref, fours_ref, held):
    step = pl.program_id(0)

    @pl.when(step == 0)
    def _():
        turned = vec_ref[...].astype(jnp.float32).T
        rows_ref[...] = turned[:24]
        fours_ref[...] = dot_nn(turned[16:24].astype(jnp.bfloat16), spread())

    def norm(at):
        h, _ = normalised(x_ref[at].astype(jnp.float32))
        normed_ref[at] = (h * rows_ref[G1 : G1 + 1] + rows_ref[S1 : S1 + 1]).astype(jnp.bfloat16)

    strips(CHUNK, norm)
    for part, bias in ((0, QB), (1, None), (2, VB)):
        m = dot_nn(normed_ref[...], w_ref[:, part * D : part * D + D])
        if bias is not None:
            m = m + rows_ref[bias : bias + 1]
        mixed_ref[:, part * D : part * D + D] = m.astype(jnp.bfloat16)
    masks = head_masks()
    place = lax.broadcasted_iota(jnp.int32, (SLOT, SLOT), 0)

    def one_slot(s, carry):
        at = pl.ds(pl.multiple_of(s * SLOT, SLOT), SLOT)
        live = place < count_ref[step * (CHUNK // SLOT) + s]
        for pair in range(H // 2):
            c = pair * 128
            keys = stacked(mixed_ref[at, D + c : D + c + 128], masks)
            held[pair] = dot_nt(keys, mixed_ref[at, c : c + 128])
        for pair in range(H // 2):
            c = pair * 128
            probs = jnp.concatenate(key_probs(held[pair], live), axis=0).astype(jnp.bfloat16)
            values = stacked(mixed_ref[at, 2 * D + c : 2 * D + c + 128], masks)
            att_ref[at, c : c + 128] = dot_tn(probs, values).astype(jnp.bfloat16)
        return carry

    lax.fori_loop(0, CHUNK // SLOT, one_slot, 0)


def attention(count, patch_rows, whole):
    rows = pl.BlockSpec((CHUNK, D), lambda i: (i, 0))
    return pl.pallas_call(
        attention_kernel,
        grid=(2,),
        in_specs=[
            pl.BlockSpec(memory_space=pltpu.SMEM),
            rows,
            columns(3 * D, 0),
            columns(128, VEC_AT),
        ],
        out_specs=[rows, pl.BlockSpec((CHUNK, 3 * D), lambda i: (i, 0)), rows, const(24, D), const(8, DD)],
        out_shape=[
            jax.ShapeDtypeStruct((ROWS, D), jnp.bfloat16),
            jax.ShapeDtypeStruct((ROWS, 3 * D), jnp.bfloat16),
            jax.ShapeDtypeStruct((ROWS, D), jnp.bfloat16),
            jax.ShapeDtypeStruct((24, D), jnp.float32),
            jax.ShapeDtypeStruct((8, DD), jnp.float32),
        ],
        scratch_shapes=[pltpu.VMEM((H // 2, 2 * SLOT, SLOT), jnp.float32)],
        compiler_params=params(28),
        cost_estimate=cost(11),
        name="attention",
    )(count, patch_rows, whole, whole)


GELU_C = 0.7978845608028654


def in_halves(kernel, half, earlier, in_specs, out_specs, out_shape, shared, mib, name, scratch, args):
    aliases = {}
    if earlier is not None:
        n = len(args)
        inner = kernel

        def kernel(*refs):
            return inner(*refs[:n], *refs[n + len(shared) :])

        aliases = {n + i: out for i, out in enumerate(shared)}
        in_specs = in_specs + [pl.BlockSpec(memory_space=pl.ANY)] * len(shared)
        args = args + [earlier[out] for out in shared]
    return pl.pallas_call(
        kernel,
        grid=(PART,),
        in_specs=in_specs,
        out_specs=out_specs,
        out_shape=out_shape,
        scratch_shapes=scratch,
        input_output_aliases=aliases,
        compiler_params=params(mib),
        cost_estimate=cost(11),
        name=name,
    )(*args)


def rows_of(half, width):
    return pl.BlockSpec((CHUNK, width), lambda j: (half, 0))


def tile_of(half):
    return pl.BlockSpec((CHUNK, D), lambda j: (half, j))


def forward_kernel(x_ref, att_ref, wo_ref, wu_ref, wd_ref, we_ref, rows_ref, fours_ref,
                   resid_ref, n2_ref, act_ref, slope_ref, enc_ref, emb_ref, total):
    j = pl.program_id(0)

    @pl.when(j == 0)
    def _():
        resid = x_ref[...].astype(jnp.float32) + (
            dot_nn(att_ref[...], wo_ref[...]) + rows_ref[OB : OB + 1]
        )
        resid_ref[...] = resid
        h, _ = normalised(resid)
        n2_ref[...] = (h * rows_ref[G2 : G2 + 1] + rows_ref[S2 : S2 + 1]).astype(jnp.bfloat16)
        total[...] = resid + rows_ref[DB : DB + 1]

    v = dot_nn(n2_ref[...], wu_ref[...]) + rows_ref[pl.ds(UB + j, 1)]
    square = v * v
    t = jnp.tanh(v * (GELU_C + 0.044715 * GELU_C * square))
    lift = 0.5 + 0.5 * t
    active = v * lift
    act_ref[...] = active.astype(jnp.bfloat16)
    slope_ref[...] = (
        lift + active * (1.0 - t) * (GELU_C + 3 * 0.044715 * GELU_C * square)
    ).astype(jnp.bfloat16)
    total[...] += dot_nn(act_ref[...], wd_ref[...])

    @pl.when(j == PART - 1)
    def _():
        enc_ref[...] = total[...].astype(jnp.bfloat16)
        emb_ref[...] = (dot_nn(enc_ref[...], we_ref[...]) + fours_ref[EB : EB + 1]).astype(jnp.bfloat16)


def forward(half, earlier, patch_rows, attended, whole, rows, fours):
    return in_halves(
        forward_kernel,
        half,
        earlier,
        [
            rows_of(half, D),
            rows_of(half, D),
            columns(D, OUT_AT),
            tile_columns(UP_AT),
            tile_columns(DOWN_AT),
            columns(DD, EMB_AT),
            const(24, D),
            const(8, DD),
        ],
        [rows_of(half, D), rows_of(half, D), tile_of(half), tile_of(half), rows_of(half, D), const(CHUNK, DD)],
        [
            jax.ShapeDtypeStruct((ROWS, D), jnp.float32),
            jax.ShapeDtypeStruct((ROWS, D), jnp.bfloat16),
            jax.ShapeDtypeStruct((ROWS, FF), jnp.bfloat16),
            jax.ShapeDtypeStruct((ROWS, FF), jnp.bfloat16),
            jax.ShapeDtypeStruct((ROWS, D), jnp.bfloat16),
            jax.ShapeDtypeStruct((CHUNK, DD), jnp.bfloat16),
        ],
        (0, 1, 2, 3, 4),
        30,
        "forward",
        [pltpu.VMEM((CHUNK, D), jnp.float32)],
        [patch_rows, attended, whole, whole, whole, whole, rows, fours],
    )


def grid_kernel(image_ref, count_ref, order_ref, emb_ref, table_ref, w_ref, fours_ref, up_ref, start_ref,
                gemb_ref, dec_ref, dvec_ref):
    s = pl.program_id(0)
    cell = lax.broadcasted_iota(jnp.int32, (GRID, SLOT), 0)
    place = lax.broadcasted_iota(jnp.int32, (GRID, SLOT), 1)
    placed = jnp.where((order_ref[0] == cell) & (place < count_ref[s]), 1.0, 0.0)
    masked = 1.0 - jnp.sum(placed, axis=1, keepdims=True)
    placed = placed.astype(jnp.bfloat16)
    grid = dot_nn(placed, emb_ref[0]) + masked * fours_ref[TOK : TOK + 1] + table_ref[...]
    gain = fours_ref[G3 : G3 + 1]
    h, inverse = normalised(grid)
    dec_ref[0] = (h * gain + fours_ref[S3 : S3 + 1]).astype(jnp.bfloat16)
    grad = dot_nt(up_ref[0], w_ref[...])
    dh = grad * gain
    back = (
        dh - jnp.mean(dh, axis=-1, keepdims=True) - h * jnp.mean(dh * h, axis=-1, keepdims=True)
    ) * inverse
    gemb_ref[0] = dot_tn(placed, back.astype(jnp.bfloat16)).astype(jnp.bfloat16)

    @pl.when(s == 0)
    def _():
        dvec_ref[...] = start_ref[...]

    dvec_ref[...] += jnp.concatenate(
        [
            jnp.zeros((1, DD), jnp.float32),
            jnp.sum(masked * back, axis=0, keepdims=True),
            jnp.sum(grad * h, axis=0, keepdims=True),
            jnp.sum(grad, axis=0, keepdims=True),
            jnp.zeros((4, DD), jnp.float32),
        ],
        axis=0,
    )


def block(*shape):
    return pl.BlockSpec((1, *shape), lambda s, *_: (s, 0, 0))


def of_image(*shape):
    return pl.BlockSpec((1, *shape), lambda s, image, *_: (image[s], 0, 0))


def decoder_grid(image, count, order, embedded, table, pix_weight, fours, pixel_grad, start):
    n = image.shape[0]
    return pl.pallas_call(
        grid_kernel,
        grid_spec=pltpu.PrefetchScalarGridSpec(
            num_scalar_prefetch=2,
            grid=(n,),
            in_specs=[
                block(1, SLOT),
                block(SLOT, DD),
                const(GRID, DD),
                const(DD, PIX),
                const(8, DD),
                of_image(GRID, PIX),
                const(8, DD),
            ],
            out_specs=[block(SLOT, DD), block(GRID, DD), const(8, DD)],
        ),
        out_shape=[
            jax.ShapeDtypeStruct((n, SLOT, DD), jnp.bfloat16),
            jax.ShapeDtypeStruct((n, GRID, DD), jnp.bfloat16),
            jax.ShapeDtypeStruct((8, DD), jnp.float32),
        ],
        compiler_params=params(20),
        cost_estimate=cost(n),
        name="decoder_grid",
    )(image, count, order, embedded, table, pix_weight, fours, pixel_grad, start)


def pixel_kernel(image_ref, dec_ref, up_ref, w_ref, rows_ref, start_ref, bias_ref, *refs):
    pix_ref, dw_ref, dbias_ref = refs[-3:]
    s = pl.program_id(0)
    pix_ref[0] = (dot_nn(dec_ref[0], w_ref[...]) + rows_ref[PB : PB + 1]).astype(jnp.bfloat16)
    dw = dot_tn(dec_ref[0], up_ref[0])
    dbias = jnp.sum(up_ref[0].astype(jnp.float32), axis=0, keepdims=True)

    @pl.when(s == 0)
    def _():
        dw_ref[...] = start_ref[...] + dw
        dbias_ref[...] = bias_ref[...] + dbias

    @pl.when(s > 0)
    def _():
        dw_ref[...] += dw
        dbias_ref[...] += dbias


def decoder_pixels(image, decoded, pixel_grad, pix_weight, rows, start, bias, pixels=None):
    n = image.shape[0]
    args = [image, decoded, pixel_grad, pix_weight, rows, start, bias]
    specs = [block(GRID, DD), of_image(GRID, PIX), const(DD, PIX), const(24, D), const(DD, PIX), const(1, PIX)]
    if pixels is not None:
        args.append(pixels)
        specs.append(pl.BlockSpec(memory_space=pl.ANY))
    return pl.pallas_call(
        pixel_kernel,
        grid_spec=pltpu.PrefetchScalarGridSpec(
            num_scalar_prefetch=1,
            grid=(n,),
            in_specs=specs,
            out_specs=[of_image(GRID, PIX), const(DD, PIX), const(1, PIX)],
        ),
        out_shape=[
            jax.ShapeDtypeStruct((IMG_DEV, GRID, PIX), jnp.bfloat16),
            jax.ShapeDtypeStruct((DD, PIX), jnp.float32),
            jax.ShapeDtypeStruct((1, PIX), jnp.float32),
        ],
        input_output_aliases={} if pixels is None else {7: 0},
        compiler_params=params(20),
        cost_estimate=cost(0.8 * n),
        name="decoder_pixels",
    )(*args)


def with_role(kernel, grid, in_specs, out_specs, out_shape, mib, name, scratch=()):
    return pl.pallas_call(
        kernel,
        grid_spec=pltpu.PrefetchScalarGridSpec(
            num_scalar_prefetch=1,
            grid=grid,
            in_specs=in_specs,
            out_specs=out_specs,
            scratch_shapes=list(scratch),
        ),
        out_shape=out_shape,
        compiler_params=params(mib),
        cost_estimate=cost(0.01 if name == "input_back" else 10),
        name=name,
    )


def half_columns(mine):
    return pl.BlockSpec((ROWS, HALF), lambda i, role: (0, role[0] if mine else 1 - role[0]))


def half_tiles(mine):
    return pl.BlockSpec(
        (ROWS, HALF), lambda i, role: (0, 2 * i + (role[0] if mine else 1 - role[0]))
    )


C_ONE, C_TWO, C_THREE = FF + 2 * DD, FF + D, 3 * D + 128
THREE_CUT = (C_THREE // 128 + 1) // 2 * 128


def line_first():
    to = lax.broadcasted_iota(jnp.int32, (HALF, HALF), 0)
    place = to % 96 // 24 * 96 + to % 24 // 6 * 24 + to // 96 * 6 + to % 6
    return (lax.broadcasted_iota(jnp.int32, (HALF, HALF), 1) == place).astype(jnp.bfloat16)


def down_grad_kernel(role_ref, gemb_ref, gb2_ref, enc_mine, enc_other, act_mine, act_other, pix_mine, pix_other,
                     mine_ref, other_ref, dbias_ref, demb_ref):
    j = pl.program_id(0)

    @pl.when(j == 0)
    def _():
        dbias_ref[...] = jnp.sum(gb2_ref[...].astype(jnp.float32), axis=0, keepdims=True)
        demb_ref[...] = jnp.sum(gemb_ref[...].astype(jnp.float32), axis=0, keepdims=True)
        for ref, enc, pix in ((mine_ref, enc_mine, pix_mine), (other_ref, enc_other, pix_other)):
            ref[:, FF : FF + DD] = dot_tn(enc[...], gemb_ref[...]).astype(jnp.bfloat16)
            ref[:, FF + DD :] = pix[...]

    at = pl.ds(pl.multiple_of(j * D, D), D)
    mine_ref[:, at] = dot_tn(act_mine[...], gb2_ref[...]).astype(jnp.bfloat16)
    other_ref[:, at] = dot_tn(act_other[...], gb2_ref[...]).astype(jnp.bfloat16)


def down_grad(role, gemb, gb2, enc, act, dpix):
    return with_role(
        down_grad_kernel,
        (PART,),
        [
            const(ROWS, DD),
            const(ROWS, D),
            half_columns(True),
            half_columns(False),
            half_tiles(True),
            half_tiles(False),
            pl.BlockSpec((HALF, DD), lambda i, role: (role[0], 0)),
            pl.BlockSpec((HALF, DD), lambda i, role: (1 - role[0], 0)),
        ],
        [const(HALF, C_ONE), const(HALF, C_ONE), const(1, D), const(1, DD)],
        [
            jax.ShapeDtypeStruct((HALF, C_ONE), jnp.bfloat16),
            jax.ShapeDtypeStruct((HALF, C_ONE), jnp.bfloat16),
            jax.ShapeDtypeStruct((1, D), jnp.float32),
            jax.ShapeDtypeStruct((1, DD), jnp.float32),
        ],
        30,
        "down_grad",
    )(role, gemb, gb2, enc, enc, act, act, dpix, dpix)


def lined_kernel(order_ref, mine_ref, came_ref, sum_ref):
    total = (mine_ref[...].astype(jnp.float32) + came_ref[...].astype(jnp.float32)).astype(jnp.bfloat16)
    sum_ref[...] = dot_nn(order_ref[...], total).astype(jnp.bfloat16)


def lined(order, mine, came):
    tile = pl.BlockSpec((HALF, 1024), lambda j: (0, j))
    return pl.pallas_call(
        lined_kernel,
        grid=(C_ONE // 1024,),
        in_specs=[const(HALF, HALF), tile, tile],
        out_specs=tile,
        out_shape=jax.ShapeDtypeStruct((HALF, C_ONE), jnp.bfloat16),
        compiler_params=params(16),
        cost_estimate=cost(4),
        name="lined",
    )(order, mine, came)


def hidden_back_kernel(gemb_ref, we_ref, wd_ref, wu_ref, slope_ref, resid_ref, wo_ref, rows_ref,
                       gb2_ref, gh_ref, gres_ref, gb_ref, gatt_ref, dup_ref, dvec_ref, total, genc):
    j = pl.program_id(0)

    @pl.when(j == 0)
    def _():
        genc[...] = dot_nt(gemb_ref[...], we_ref[...])
        gb2_ref[...] = genc[...].astype(jnp.bfloat16)
        dup_ref[...] = jnp.zeros_like(dup_ref)

    gh = (dot_nt(gb2_ref[...], wd_ref[...]) * slope_ref[...].astype(jnp.float32)).astype(jnp.bfloat16)
    gh_ref[...] = gh
    dup_ref[pl.ds(j, 1)] = jnp.sum(gh.astype(jnp.float32), axis=0, keepdims=True)
    part = dot_nt(gh, wu_ref[...])

    @pl.when(j == 0)
    def _():
        total[...] = part

    @pl.when(j > 0)
    def _():
        total[...] += part

    @pl.when(j == PART - 1)
    def _():
        back, dgain, dshift = norm_back(resid_ref[...], rows_ref[G2 : G2 + 1], total[...])
        gres = genc[...] + back
        gres_ref[...] = gres
        gb = gres.astype(jnp.bfloat16)
        gb_ref[...] = gb
        gatt_ref[...] = dot_nt(gb, wo_ref[...]).astype(jnp.bfloat16)
        dvec_ref[...] = jnp.concatenate(
            [
                dgain,
                dshift,
                jnp.sum(gb.astype(jnp.float32), axis=0, keepdims=True),
                jnp.zeros((5, D), jnp.float32),
            ],
            axis=0,
        )


def hidden_back(half, earlier, gemb, whole, slope, resid, rows):
    return in_halves(
        hidden_back_kernel,
        half,
        earlier,
        [
            const(CHUNK, DD),
            columns(DD, EMB_AT),
            tile_columns(DOWN_AT),
            tile_columns(UP_AT),
            tile_of(half),
            rows_of(half, D),
            columns(D, OUT_AT),
            const(24, D),
        ],
        [
            rows_of(half, D),
            tile_of(half),
            rows_of(half, D),
            rows_of(half, D),
            rows_of(half, D),
            const(8, D),
            const(8, D),
        ],
        [
            jax.ShapeDtypeStruct((ROWS, D), jnp.bfloat16),
            jax.ShapeDtypeStruct((ROWS, FF), jnp.bfloat16),
            jax.ShapeDtypeStruct((ROWS, D), jnp.float32),
            jax.ShapeDtypeStruct((ROWS, D), jnp.bfloat16),
            jax.ShapeDtypeStruct((ROWS, D), jnp.bfloat16),
            jax.ShapeDtypeStruct((8, D), jnp.float32),
            jax.ShapeDtypeStruct((8, D), jnp.float32),
        ],
        (0, 1, 2, 3, 4),
        30,
        "hidden_back",
        [pltpu.VMEM((CHUNK, D), jnp.float32)] * 2,
        [gemb, whole, whole, whole, slope, resid, whole, rows],
    )


BLOCKS = HALF // 24


def put_blocks(ref, columns, rows):
    for n in range(BLOCKS):
        ref[n, :, columns] = rows[24 * n : 24 * n + 24].astype(jnp.bfloat16)


def up_grad_kernel(role_ref, n2_mine, n2_other, gh_ref, att_mine, att_other, gb_ref, mine_ref, other_ref):
    j = pl.program_id(0)
    at = pl.ds(pl.multiple_of(j * D, D), D)
    put_blocks(mine_ref, at, dot_tn(n2_mine[...], gh_ref[...]))
    put_blocks(other_ref, at, dot_tn(n2_other[...], gh_ref[...]))

    @pl.when(j == PART - 1)
    def _():
        put_blocks(mine_ref, slice(FF, C_TWO), dot_tn(att_mine[...], gb_ref[...]))
        put_blocks(other_ref, slice(FF, C_TWO), dot_tn(att_other[...], gb_ref[...]))


def up_grad(role, n2, gh, attended, gb):
    return with_role(
        up_grad_kernel,
        (PART,),
        [
            half_columns(True),
            half_columns(False),
            pl.BlockSpec((ROWS, D), lambda j, role: (0, j)),
            half_columns(True),
            half_columns(False),
            const(ROWS, D),
        ],
        [const(BLOCKS, 24, C_TWO), const(BLOCKS, 24, C_TWO)],
        [
            jax.ShapeDtypeStruct((BLOCKS, 24, C_TWO), jnp.bfloat16),
            jax.ShapeDtypeStruct((BLOCKS, 24, C_TWO), jnp.bfloat16),
        ],
        34,
        "up_grad",
    )(role, n2, n2, gh, attended, attended, gb)


def attention_back_kernel(count_ref, mixed_ref, gatt_ref, gmix_ref, held, gheld):
    live = lax.broadcasted_iota(jnp.int32, (SLOT, SLOT), 0) < count_ref[pl.program_id(0)]
    masks = head_masks()
    low_lane = lax.broadcasted_iota(jnp.int32, (SLOT, 128), 1) < HD
    scale = HD ** (-0.5)
    for pair in range(H // 2):
        c = pair * 128
        held[pair] = dot_nt(stacked(mixed_ref[:, D + c : D + c + 128], masks), mixed_ref[:, c : c + 128])
        gheld[pair] = dot_nt(
            stacked(mixed_ref[:, 2 * D + c : 2 * D + c + 128], masks), gatt_ref[:, c : c + 128]
        )
    for pair in range(H // 2):
        c = pair * 128
        probs = key_probs(held[pair], live)
        gscores = []
        for k in range(2):
            p, g = probs[k], gheld[pair, SLOT * k : SLOT * k + SLOT]
            gscores.append(p * (g - jnp.sum(p * g, axis=0, keepdims=True)))
        gscores = jnp.concatenate(gscores, axis=0).astype(jnp.bfloat16)
        probs = jnp.concatenate(probs, axis=0).astype(jnp.bfloat16)
        gv = dot_nn(probs, gatt_ref[:, c : c + 128])
        gk = dot_nn(gscores, mixed_ref[:, c : c + 128]) * scale
        gq = dot_tn(gscores, stacked(mixed_ref[:, D + c : D + c + 128], masks)) * scale
        gmix_ref[:, c : c + 128] = gq.astype(jnp.bfloat16)
        gmix_ref[:, D + c : D + c + 128] = jnp.where(low_lane, gk[:SLOT], gk[SLOT:]).astype(jnp.bfloat16)
        gmix_ref[:, 2 * D + c : 2 * D + c + 128] = jnp.where(
            low_lane, gv[:SLOT], gv[SLOT:]
        ).astype(jnp.bfloat16)


def attention_back(count, mixed, gatt):
    wide = pl.BlockSpec((SLOT, 3 * D), lambda s: (s, 0))
    return pl.pallas_call(
        attention_back_kernel,
        grid=(IMG_DEV,),
        in_specs=[
            pl.BlockSpec(memory_space=pltpu.SMEM),
            wide,
            pl.BlockSpec((SLOT, D), lambda s: (s, 0)),
        ],
        out_specs=wide,
        out_shape=jax.ShapeDtypeStruct((ROWS, 3 * D), jnp.bfloat16),
        scratch_shapes=[pltpu.VMEM((H // 2, 2 * SLOT, SLOT), jnp.float32)] * 2,
        compiler_params=params(20),
        cost_estimate=cost(0.01),
        name="attention_back",
    )(count, mixed, gatt)


def input_back_kernel(role_ref, gmix_ref, w_ref, x_ref, gres_ref, rows_ref, normed_mine, normed_other,
                      dup_ref, d2_ref, ddown_ref, dpb_ref, d3_ref, demb_ref,
                      pg_ref, mine_ref, other_ref, total, turned):
    j = pl.program_id(0)
    at = pl.ds(pl.multiple_of(j * D, D), D)
    gmix = gmix_ref[...]
    put_blocks(mine_ref, at, dot_tn(normed_mine[...], gmix))
    put_blocks(other_ref, at, dot_tn(normed_other[...], gmix))
    part = dot_nt(gmix, w_ref[...])
    dbias = jnp.sum(gmix.astype(jnp.float32), axis=0, keepdims=True)

    @pl.when(j == 0)
    def _():
        total[...] = part
        turned[QB : QB + 1] = dbias

    @pl.when(j > 0)
    def _():
        total[...] += part

    @pl.when(j == 2)
    def _():
        back, dgain, dshift = norm_back(
            x_ref[...].astype(jnp.float32), rows_ref[G1 : G1 + 1], total[...]
        )
        pg_ref[...] = (gres_ref[...] + back).astype(jnp.bfloat16)
        turned[G1 : G1 + 1] = dgain
        turned[S1 : S1 + 1] = dshift
        turned[VB : VB + 1] = dbias
        turned[OB : OB + 1] = d2_ref[2:3]
        turned[G2 : G2 + 1] = d2_ref[0:1]
        turned[S2 : S2 + 1] = d2_ref[1:2]
        turned[DB : DB + 1] = ddown_ref[...]
        turned[PB : PB + 1] = dpb_ref[...]
        turned[UB : UB + 4] = dup_ref[0:4]
        turned[13:16] = jnp.zeros((3, D), jnp.float32)
        four = jnp.concatenate([demb_ref[...], d3_ref[1:4], jnp.zeros((4, DD), jnp.float32)], axis=0)
        turned[16:24] = dot_nt(four.astype(jnp.bfloat16), spread())
        block = jnp.concatenate([turned[...], jnp.zeros((104, D), jnp.float32)], axis=0).T
        first, second = block[:HALF], block[HALF:]
        up = role_ref[0] == 1
        put_blocks(mine_ref, slice(3 * D, C_THREE), jnp.where(up, second, first))
        put_blocks(other_ref, slice(3 * D, C_THREE), jnp.where(up, first, second))


def input_back(role, gmix, whole, x, gres, rows, normed, dup, d2, ddown, dpb, d3, demb):
    return with_role(
        input_back_kernel,
        (3,),
        [
            pl.BlockSpec((ROWS, D), lambda j, role: (0, j)),
            pl.BlockSpec((D, D), lambda j, role: (0, j)),
            const(ROWS, D),
            const(ROWS, D),
            const(24, D),
            half_columns(True),
            half_columns(False),
            const(8, D),
            const(8, D),
            const(1, D),
            const(1, D),
            const(8, DD),
            const(1, DD),
        ],
        [const(ROWS, D), const(BLOCKS, 24, C_THREE), const(BLOCKS, 24, C_THREE)],
        [
            jax.ShapeDtypeStruct((ROWS, D), jnp.bfloat16),
            jax.ShapeDtypeStruct((BLOCKS, 24, C_THREE), jnp.bfloat16),
            jax.ShapeDtypeStruct((BLOCKS, 24, C_THREE), jnp.bfloat16),
        ],
        30,
        "input_back",
        [pltpu.VMEM((ROWS, D), jnp.float32), pltpu.VMEM((24, D), jnp.float32)],
    )(role, gmix, whole, x, gres, rows, normed, normed, dup, d2, ddown, dpb, d3, demb)


def hot(shape, test):
    return test(
        lax.broadcasted_iota(jnp.int32, shape, 0), lax.broadcasted_iota(jnp.int32, shape, 1)
    ).astype(jnp.bfloat16)


def hidden_order():
    return hot((512, 512), lambda l, c: l == 4 * (c % 128) + c // 128)


def pack_kernel(qkv_ref, out_ref, up_ref, down_ref, emb_ref, pix_ref, *refs):
    six_refs, bias_ref, four_refs, packed_ref = refs[:9], refs[9], refs[10:14], refs[14]
    packed_ref[:, :OUT_AT] = qkv_ref[...]
    packed_ref[:, OUT_AT:UP_AT] = out_ref[...]
    order = hidden_order()
    for r in range(D // 128):
        turned = dot_nn(up_ref[:, 512 * r : 512 * r + 512], order).astype(jnp.bfloat16)
        for j in range(PART):
            at = UP_AT + j * D + 128 * r
            packed_ref[:, at : at + 128] = turned[:, 128 * j : 128 * j + 128]
    for j in range(PART):
        rows = hot((6, 24), lambda i, l: l == 4 * i + j)
        packed_ref[:, DOWN_AT + j * D : DOWN_AT + j * D + D] = dot_nn(rows, down_ref[...]).astype(jnp.bfloat16)
    packed_ref[:, EMB_AT:PIX_AT] = emb_ref[...]
    for t in range(2):
        part = jnp.zeros((6, 256), jnp.float32)
        for s in range(3):
            rows = hot((6, 4), lambda r, i: 2 * r + t == 3 * i + s)
            part = part + dot_nn(rows, pix_ref[:, 256 * s : 256 * s + 256])
        packed_ref[:, PIX_AT + 256 * t : PIX_AT + 256 * t + 256] = part.astype(jnp.bfloat16)
    lane = lax.broadcasted_iota(jnp.int32, (6, 128), 1)
    block = jnp.zeros((6, 128), jnp.float32)

    def put(block, ref, count, start, pick):
        size = ref.shape[0]
        line = jnp.broadcast_to(ref[...].astype(jnp.float32).reshape(1, size), (6, size))
        row = lax.broadcasted_iota(jnp.int32, (6, size), 0)
        at = lax.broadcasted_iota(jnp.int32, (6, size), 1)
        for c in range(count):
            column = jnp.sum(jnp.where(at == pick(row, c), line, 0.0), axis=1, keepdims=True)
            block = jnp.where(lane == start + c, column, block)
        return block

    for n, ref in enumerate(six_refs):
        block = put(block, ref, 1, n, lambda row, c: row)
    block = put(block, bias_ref, PART, UB, lambda row, c: PART * row + c)
    for n, ref in enumerate(four_refs):
        block = put(block, ref, 1, 16 + n, lambda row, c: row)
    packed_ref[:, VEC_AT:] = block.astype(jnp.bfloat16)


def packing_kernel(*refs):
    n = (len(refs) - 2) // 2
    given, packed_ref, held, sems = refs[:n], refs[n], refs[n + 1 : 2 * n + 1], refs[-1]
    copies = [
        pltpu.make_async_copy(source, place, sems.at[i])
        for i, (source, place) in enumerate(zip(given, held))
    ]
    for copy in copies:
        copy.start()
    for copy in copies:
        copy.wait()
    pack_kernel(*held, packed_ref)


def pack(*args):
    return pl.pallas_call(
        packing_kernel,
        in_specs=[pl.BlockSpec(memory_space=pltpu.HBM)] * len(args),
        out_shape=jax.ShapeDtypeStruct((6, WIDE), jnp.bfloat16),
        scratch_shapes=[pltpu.VMEM(arg.shape, arg.dtype) for arg in args]
        + [pltpu.SemaphoreType.DMA((len(args),))],
        compiler_params=pltpu.CompilerParams(vmem_limit_bytes=64 * MIB - 65536),
        cost_estimate=cost(4),
        name="pack",
    )(*args)


def unpack_kernel(kept_one, came_one, kept_two, came_two, qkv_ref, out_ref, up_ref, down_ref, emb_ref, pix_ref, vec_ref):
    first, second = (kept_one, came_one), (kept_two, came_two)

    def total(pair, at, width):
        return sum(ref[:, at : at + width].astype(jnp.float32) for ref in pair)

    def shuffled(pair, dot):
        return dot(pair[0]) + dot(pair[1])

    two_at, three_at = C_TWO // 2, THREE_CUT

    def spot(group, column):
        if group == 2:
            return column if column < two_at else column + three_at
        return column + two_at if column < three_at else column + C_TWO

    for column in range(0, 3 * D, 128):
        qkv_ref[:, column : column + 128] = total(second, spot(3, column), 128)
    for column in range(0, D, 128):
        out_ref[:, column : column + 128] = total(second, spot(2, FF + column), 128)
    emb_ref[...] = total(first, FF, DD)
    vec_ref[...] = total(second, spot(3, 3 * D), 128)
    order = hidden_order()
    for r in range(D // 128):

        def turned(ref):
            starts = [spot(2, j * D + 128 * r) for j in range(PART)]
            parts = [ref[:, at : at + 128] for at in starts]
            return dot_nt(jnp.concatenate(parts, axis=1), order)

        up_ref[:, 512 * r : 512 * r + 512] = shuffled(second, turned)
    down = jnp.zeros((24, D), jnp.float32)
    for j in range(PART):
        rows = hot((24, 6), lambda l, i: l == 4 * i + j)
        down = down + shuffled(first, lambda ref: dot_nn(rows, ref[:, j * D : j * D + D]))
    down_ref[...] = down
    for s in range(3):
        part = jnp.zeros((4, 256), jnp.float32)
        for t in range(2):
            rows = hot((4, 6), lambda i, r: 2 * r + t == 3 * i + s)
            at = FF + DD + 256 * t
            part = part + shuffled(first, lambda ref: dot_nn(rows, ref[:, at : at + 256]))
        pix_ref[:, 256 * s : 256 * s + 256] = part


def turn_kernel(plan, bits_ref, *refs):
    inputs = [len(term) for group in plan for term in group["terms"]]
    given = iter(refs[: sum(inputs)])
    out = iter(refs[sum(inputs) :])
    for group in plan:
        terms = [([next(given) for _ in term], group["columns"]) for term in group["terms"]]
        kept_ref, sent_ref = next(out), next(out)
        bit = bits_ref[group["bit"]]
        column = 0
        for term, columns in terms:
            start, width = columns or (0, term[0].shape[-1])
            source, to = slice(start, start + width), slice(column, column + width)
            column += width

            def added(*at):
                return sum(ref[(*at, slice(None), source)].astype(jnp.float32) for ref in term)

            if group["dim"] is None:
                rows = term[0].shape[-2] // 2
                value = added(*[0] * (len(term[0].shape) - 2))
                low, high = value[:rows], value[rows:]
                kept_ref[:, to] = jnp.where(bit == 1, high, low).astype(jnp.bfloat16)
                sent_ref[:, to] = jnp.where(bit == 1, low, high).astype(jnp.bfloat16)
                continue
            p, q = kept_ref.shape[:2]
            for ref, half in ((kept_ref, bit), (sent_ref, 1 - bit)):
                for i in range(p):
                    for j in range(q):
                        at = (half * p + i, j) if group["dim"] == 0 else (i, half * q + j)
                        ref[i, j, :, to] = added(*at).astype(jnp.bfloat16)


def turn(bits, *groups):
    plan, args, shapes = [], [], []
    for terms, dim, bit, columns in groups:
        plan.append(dict(terms=terms, dim=dim, bit=bit, columns=columns))
        for term in terms:
            args += term
        width = sum(columns[1] if columns else term[0].shape[-1] for term in terms)
        shape = list(terms[0][0].shape[:-1])
        if dim is None:
            shape = [shape[-1] // 2]
        else:
            shape[dim] //= 2
        shapes += [jax.ShapeDtypeStruct((*shape, width), jnp.bfloat16)] * 2
    plan = [dict(group, terms=[[None] * len(term) for term in group["terms"]]) for group in plan]
    out = pl.pallas_call(
        functools.partial(turn_kernel, plan),
        in_specs=[pl.BlockSpec(memory_space=pltpu.SMEM)]
        + [pl.BlockSpec(memory_space=pltpu.VMEM)] * len(args),
        out_shape=shapes,
        compiler_params=pltpu.CompilerParams(vmem_limit_bytes=14 * MIB),
        cost_estimate=cost(3),
        name="turn",
    )(bits, *args)
    return [tuple(out[n : n + 2]) for n in range(0, len(out), 2)]


def unpack(*terms):
    return pl.pallas_call(
        unpack_kernel,
        out_shape=[
            jax.ShapeDtypeStruct(shape, jnp.float32)
            for shape in ((6, 3 * D), (6, D), (6, FF), (24, D), (6, DD), (4, PIX), (6, 128))
        ],
        compiler_params=pltpu.CompilerParams(vmem_limit_bytes=16 * MIB),
        cost_estimate=cost(4),
        name="unpack",
    )(*terms)


PAIRS = {
    "high": [(0, 3), (3, 0), (1, 2), (2, 1)],
    "low": [(0, 1), (1, 0), (2, 3), (3, 2)],
}


ROLE_PAIR = [(0, 1), (1, 0)]


def tie(*arrays):
    return lax.optimization_barrier(arrays)


def moved(images, step, crossing=False):
    pairs = [
        (r * N_DP + p, (r ^ crossing) * N_DP + (p + step) % N_DP)
        for r in range(2)
        for p in range(N_DP)
    ]
    return lax.ppermute(images, ALL, pairs)


def added(mine, came):
    return (mine.astype(jnp.float32) + came.astype(jnp.float32)).astype(jnp.bfloat16)


def sent_on(axis, which, halves):
    return halves[0], lax.ppermute(halves[1], axis, PAIRS[which])


def body(
    patch_rows,
    patch_order,
    visible_count,
    encoded_image,
    first_gain,
    first_shift,
    query_key_value,
    query_bias,
    value_bias,
    output_weight,
    output_bias,
    second_gain,
    second_shift,
    up_weight,
    up_bias,
    down_weight,
    down_bias,
    embed_weight,
    embed_bias,
    mask_token,
    decoder_gain,
    decoder_shift,
    pixel_weight,
    pixel_bias,
    pixel_grad,
):
    device = lax.axis_index(ALL)
    role = lax.axis_index("role").astype(jnp.int32).reshape(1)
    image_count = encoded_image.shape[0]

    own_images = device * IMG_DEV + jnp.arange(IMG_DEV, dtype=jnp.int32)
    found = encoded_image[None, :] == own_images[:, None]
    source_slot = jnp.sum(
        jnp.where(found, jnp.arange(image_count, dtype=jnp.int32)[None, :], 0), axis=1
    )
    source_place = source_slot % IMG_DEV
    image_of = jnp.sum(
        jnp.where(
            source_place[None, :] == jnp.arange(IMG_DEV, dtype=jnp.int32)[:, None],
            jnp.arange(IMG_DEV, dtype=jnp.int32)[None, :],
            0,
        ),
        axis=1,
    )
    own_count = lax.dynamic_slice_in_dim(visible_count, device * IMG_DEV, IMG_DEV)
    own_order = lax.dynamic_slice_in_dim(patch_order, device * IMG_DEV, IMG_DEV, 0)[:, None, :SLOT]
    first, later = image_of[jnp.array([0, 4])], image_of[jnp.array([1, 5, 2, 6, 3, 7])]

    packed = pack(
        query_key_value,
        output_weight,
        up_weight,
        down_weight,
        embed_weight,
        pixel_weight,
        first_gain,
        first_shift,
        query_bias,
        value_bias,
        output_bias,
        second_gain,
        second_shift,
        down_bias,
        pixel_bias,
        up_bias,
        embed_bias,
        mask_token,
        decoder_gain,
        decoder_shift,
    )
    whole = lax.all_gather(packed, "x", tiled=True)
    whole = lax.all_gather(whole, ("role", "y", "z"), tiled=True)
    pix_weight = whole[:, PIX_AT:VEC_AT].reshape(DD, PIX)

    held = lax.dynamic_slice_in_dim(encoded_image, device * IMG_DEV, IMG_DEV)
    count = visible_count[held]

    normed, mixed, attended, rows, fours = attention(count, patch_rows, whole)
    half = forward(1, None, patch_rows, attended, whole, rows, fours)
    high = moved(half[5].reshape(4, SLOT, DD), 4, True)
    half = forward(0, half, patch_rows, attended, whole, rows, fours)
    resid, normed_two, active, slope, encoded, embedded = half
    embedded, high = tie(embedded, high)
    low = moved(embedded.reshape(4, SLOT, DD), 0, True)
    steps = [
        moved(jnp.concatenate([low[s : s + 1], high[s : s + 1]]), s) for s in range(1, 4)
    ]
    table = positions()
    zeros = jnp.zeros((8, DD), jnp.float32), jnp.zeros((DD, PIX), jnp.float32), jnp.zeros((1, PIX), jnp.float32)
    grad_first, decoded, d_three = decoder_grid(
        first,
        own_count[first],
        own_order[first],
        jnp.concatenate([low[:1], high[:1]]),
        table,
        pix_weight,
        fours,
        pixel_grad,
        zeros[0],
    )
    pixels, d_pix, d_pix_bias = decoder_pixels(
        first, decoded, pixel_grad, pix_weight, rows, zeros[1], zeros[2]
    )
    d_pix, *steps = tie(d_pix, *steps)
    grad_later, decoded, d_three = decoder_grid(
        later,
        own_count[later],
        own_order[later],
        jnp.concatenate(steps),
        table,
        pix_weight,
        fours,
        pixel_grad,
        d_three,
    )
    steps = [moved(grad_later[2 * s - 2 : 2 * s], -s) for s in range(1, 4)]
    pixels, d_pix, d_pix_bias = decoder_pixels(
        later, decoded, pixel_grad, pix_weight, rows, d_pix, d_pix_bias, pixels
    )
    d_pix, *steps = tie(d_pix, *steps)
    high = moved(jnp.concatenate([grad_first[1:]] + [s[1:] for s in steps]), -4, True).reshape(CHUNK, DD)
    low = moved(jnp.concatenate([grad_first[:1]] + [s[:1] for s in steps]), 0, True).reshape(CHUNK, DD)
    low, pix_rows, line = tie(low, d_pix.astype(jnp.bfloat16).reshape(D, DD), line_first())
    half = hidden_back(0, None, low, whole, slope, resid, rows)
    d_up_bias, d_second = half[5:]
    high, part = tie(high, half[0])
    half = hidden_back(1, [part, *half[1:]], high, whole, slope, resid, rows)
    branch_two, grad_hidden, grad_resid, grad_branch, grad_attended = half[:5]
    d_up_bias, d_second = d_up_bias + half[5], d_second + half[6]
    mine_one, other_one, d_down_bias, d_emb_bias = down_grad(
        role,
        jnp.concatenate([low, high]),
        branch_two,
        encoded,
        active,
        pix_rows,
    )
    grad_hidden, other_one = tie(grad_hidden, other_one)
    came_one = lax.ppermute(other_one, "role", ROLE_PAIR)
    mine_two, other_two = up_grad(role, normed_two, grad_hidden, attended, grad_branch)
    came_two = lax.ppermute(other_two, "role", ROLE_PAIR)
    mine_one, came_one, mine_two = tie(mine_one, came_one, mine_two)
    part_one, came_two = tie(lined(line, mine_one, came_one), came_two)
    part_one = lax.psum_scatter(part_one, "x", tiled=True)
    ring = [lax.axis_index(axis) for axis in "yzx"]
    bits = jnp.stack([at // 2 for at in ring] + [at % 2 for at in ring]).astype(jnp.int32)
    y_high, z_high, x_high, y_low, z_low, x_low = range(6)

    def in_planes(array):
        return array.reshape(4, 4, 24, array.shape[-1])

    def parted(mine, came, cut):
        term = [in_planes(mine), in_planes(came)]
        width = mine.shape[-1]
        return ([term], 1, z_high, (0, cut)), ([term], 0, y_high, (cut, width - cut))

    first_two, second_two = turn(bits, *parted(mine_two, came_two, C_TWO // 2))
    grad_attended, *both = tie(grad_attended, *first_two, *second_two)
    first_two, second_two = sent_on("z", "high", both[:2]), sent_on("y", "high", both[2:])
    grad_mixed = attention_back(count, mixed, grad_attended)
    patch_grad, mine, other = input_back(
        role,
        grad_mixed,
        whole,
        patch_rows,
        grad_resid,
        rows,
        normed,
        d_up_bias,
        d_second,
        d_down_bias,
        d_pix_bias,
        d_three,
        d_emb_bias,
    )
    mine, other, came_a, came_b = tie(mine, other, first_two[1], second_two[1])
    first_two, second_two = (first_two[0], came_a), (second_two[0], came_b)
    came_three = lax.ppermute(other, "role", ROLE_PAIR)
    first_three, second_three = turn(bits, *parted(mine, came_three, THREE_CUT))
    first_three = sent_on("z", "high", first_three)
    second_three = sent_on("y", "high", second_three)
    one = part_one.reshape(4, 1, 24, C_ONE)
    first, second, one = turn(
        bits,
        ([first_two, first_three], 1, z_low, None),
        ([second_two, second_three], 0, y_low, None),
        ([[one]], 0, y_high, None),
    )
    first, second, one = sent_on("z", "low", first), sent_on("y", "low", second), sent_on("y", "high", one)
    first, second, one = turn(
        bits, ([first], 0, y_high, None), ([second], 1, z_high, None), ([one], 0, y_low, None)
    )
    first, second, one = sent_on("y", "high", first), sent_on("z", "high", second), sent_on("y", "low", one)
    first, second, one = turn(
        bits, ([first], 0, y_low, None), ([second], 1, z_low, None), ([one], None, z_high, None)
    )
    first, second, one = sent_on("y", "low", first), sent_on("z", "low", second), sent_on("z", "high", one)
    rest, one = turn(bits, ([first, second], None, x_high, None), ([one], None, z_low, None))
    rest, one = sent_on("x", "high", rest), sent_on("z", "low", one)
    (rest,) = turn(bits, ([rest], None, x_low, None))
    rest = sent_on("x", "low", rest)
    d_qkv, d_out, d_up, d_down, d_emb, d_pix, vec = unpack(*one, *rest)
    return (
        pixels,
        patch_grad,
        vec[:, G1],
        vec[:, S1],
        d_qkv,
        vec[:, QB],
        vec[:, VB],
        d_out,
        vec[:, OB],
        vec[:, G2],
        vec[:, S2],
        d_up,
        vec[:, UB : UB + PART].reshape(6 * PART),
        d_down,
        vec[:, DB],
        d_emb,
        vec[:4, 16 + EB],
        vec[:4, 16 + TOK],
        vec[:4, 16 + G3],
        vec[:4, 16 + S3],
        d_pix,
        vec[:, PB],
    )


def solution(mesh):
    mesh = Mesh(mesh.devices.reshape(2, 4, 4, 4), ALL)
    two, one = P(ALL, None), P(ALL)
    placed = (two, P(), P(), P(), one, one, two, one, one, two, one, one, one, two, one, two, one)
    placed += (two, one, one, one, one, two, one, P(ALL, None, None))
    given = (P(ALL, None, None), two, one, one, two, one, one, two, one, one, one, two, one, two, one)
    given += (two, one, one, one, one, two, one)
    return jax.shard_map(body, mesh=mesh, in_specs=placed, out_specs=given, check_vma=False)
```

```python
import functools

import jax
import jax.numpy as jnp
from jax import lax
from jax.experimental import pallas as pl
from jax.experimental.pallas import tpu as pltpu
from jax.sharding import Mesh
from jax.sharding import PartitionSpec as P

D = 768
H = 12
HD = 64
FF = 3072
DD = 512
PIX = 768
SIDE = 14
SLOT = 80
IMG_DEV = 8
GRID = 196
N_DP = 64
PART = FF // D

ALL = ("role", "y", "z", "x")

epsilon = 1e-06
masked_score = -1e30

def positions():
    quarter = DD // 4
    frequency = 10000.0 ** (-jnp.arange(quarter, dtype=jnp.float32) / quarter)
    places = jnp.arange(GRID, dtype=jnp.int32)
    row_angle = (places // SIDE).astype(jnp.float32)[:, None] * frequency[None, :]
    col_angle = (places % SIDE).astype(jnp.float32)[:, None] * frequency[None, :]
    return jnp.concatenate(
        [jnp.sin(row_angle), jnp.cos(row_angle), jnp.sin(col_angle), jnp.cos(col_angle)], axis=1
    )


HALF = D // 2
ROWS = IMG_DEV * SLOT
CHUNK = ROWS // 2
OUT_AT, UP_AT, DOWN_AT, EMB_AT, PIX_AT, VEC_AT = 3 * D, 4 * D, 8 * D, 12 * D, 12 * D + DD, 12 * D + 2 * DD
WIDE = VEC_AT + 128
G1, S1, QB, VB, OB, G2, S2, DB, PB, UB = range(10)
EB, TOK, G3, S3 = range(4)

MIB = 1 << 20


def cost(us):
    return pl.CostEstimate(flops=int(us * 1e9), bytes_accessed=0, transcendentals=0)


def params(mib):
    return pltpu.CompilerParams(
        dimension_semantics=("arbitrary",), vmem_limit_bytes=mib * MIB
    )


def const(*shape):
    return pl.BlockSpec(shape, lambda i, *_: (0,) * len(shape))


def columns(width, at):
    return pl.BlockSpec((D, width), lambda i, *_: (0, at // width))


def tile_columns(at):
    return pl.BlockSpec((D, D), lambda i, *_: (0, at // D + i))


def dot_nn(a, b):
    return lax.dot_general(a, b, (((1,), (0,)), ((), ())), preferred_element_type=jnp.float32)


def dot_nt(a, b):
    return lax.dot_general(a, b, (((1,), (1,)), ((), ())), preferred_element_type=jnp.float32)


def dot_tn(a, b):
    return lax.dot_general(a, b, (((0,), (0,)), ((), ())), preferred_element_type=jnp.float32)


def normalised(values):
    average = jnp.mean(values, axis=-1, keepdims=True)
    centered = values - average
    variance = jnp.mean(centered * centered, axis=-1, keepdims=True)
    inverse = lax.rsqrt(variance + epsilon)
    return centered * inverse, inverse


def norm_back(values, gain, upstream):
    h, inverse = normalised(values)
    dh = upstream * gain
    dv = (
        dh - jnp.mean(dh, axis=-1, keepdims=True) - h * jnp.mean(dh * h, axis=-1, keepdims=True)
    ) * inverse
    return (
        dv,
        jnp.sum(upstream * h, axis=0, keepdims=True),
        jnp.sum(upstream, axis=0, keepdims=True),
    )


def strips(count, body, size=16, at_once=10):
    def some(i, carry):
        for n in range(at_once):
            body(pl.ds(pl.multiple_of((i * at_once + n) * size, size), size))
        return carry

    lax.fori_loop(0, count // (at_once * size), some, 0)


def spread():
    row = lax.broadcasted_iota(jnp.int32, (D, DD), 0)
    col = lax.broadcasted_iota(jnp.int32, (D, DD), 1)
    return (row == 6 * (col // 4) + col % 4).astype(jnp.bfloat16)


def head_masks():
    lane = lax.broadcasted_iota(jnp.int32, (1, 2 * HD), 1)
    low = (lane < HD).astype(jnp.bfloat16)
    return low, (1.0 - low.astype(jnp.float32)).astype(jnp.bfloat16)


def stacked(pair, masks):
    return jnp.concatenate([pair * masks[0], pair * masks[1]], axis=0)


def key_probs(scores, live):
    both = []
    for k in range(2):
        s = jnp.where(live, scores[SLOT * k : SLOT * k + SLOT] * HD ** (-0.5), masked_score)
        e = jnp.exp(s - jnp.max(s, axis=0, keepdims=True))
        both.append(e * (1.0 / jnp.sum(e, axis=0, keepdims=True)))
    return both


def attention_kernel(count_ref, x_ref, w_ref, vec_ref, normed_ref, mixed_ref, att_ref, rows_ref, fours_ref, held):
    step = pl.program_id(0)

    @pl.when(step == 0)
    def _():
        turned = vec_ref[...].astype(jnp.float32).T
        rows_ref[...] = turned[:24]
        fours_ref[...] = dot_nn(turned[16:24].astype(jnp.bfloat16), spread())

    def norm(at):
        h, _ = normalised(x_ref[at].astype(jnp.float32))
        normed_ref[at] = (h * rows_ref[G1 : G1 + 1] + rows_ref[S1 : S1 + 1]).astype(jnp.bfloat16)

    strips(CHUNK, norm)
    for part, bias in ((0, QB), (1, None), (2, VB)):
        m = dot_nn(normed_ref[...], w_ref[:, part * D : part * D + D])
        if bias is not None:
            m = m + rows_ref[bias : bias + 1]
        mixed_ref[:, part * D : part * D + D] = m.astype(jnp.bfloat16)
    masks = head_masks()
    place = lax.broadcasted_iota(jnp.int32, (SLOT, SLOT), 0)

    def one_slot(s, carry):
        at = pl.ds(pl.multiple_of(s * SLOT, SLOT), SLOT)
        live = place < count_ref[step * (CHUNK // SLOT) + s]
        for pair in range(H // 2):
            c = pair * 128
            keys = stacked(mixed_ref[at, D + c : D + c + 128], masks)
            held[pair] = dot_nt(keys, mixed_ref[at, c : c + 128])
        for pair in range(H // 2):
            c = pair * 128
            probs = jnp.concatenate(key_probs(held[pair], live), axis=0).astype(jnp.bfloat16)
            values = stacked(mixed_ref[at, 2 * D + c : 2 * D + c + 128], masks)
            att_ref[at, c : c + 128] = dot_tn(probs, values).astype(jnp.bfloat16)
        return carry

    lax.fori_loop(0, CHUNK // SLOT, one_slot, 0)


def attention(count, patch_rows, whole):
    rows = pl.BlockSpec((CHUNK, D), lambda i: (i, 0))
    return pl.pallas_call(
        attention_kernel,
        grid=(2,),
        in_specs=[
            pl.BlockSpec(memory_space=pltpu.SMEM),
            rows,
            columns(3 * D, 0),
            columns(128, VEC_AT),
        ],
        out_specs=[rows, pl.BlockSpec((CHUNK, 3 * D), lambda i: (i, 0)), rows, const(24, D), const(8, DD)],
        out_shape=[
            jax.ShapeDtypeStruct((ROWS, D), jnp.bfloat16),
            jax.ShapeDtypeStruct((ROWS, 3 * D), jnp.bfloat16),
            jax.ShapeDtypeStruct((ROWS, D), jnp.bfloat16),
            jax.ShapeDtypeStruct((24, D), jnp.float32),
            jax.ShapeDtypeStruct((8, DD), jnp.float32),
        ],
        scratch_shapes=[pltpu.VMEM((H // 2, 2 * SLOT, SLOT), jnp.float32)],
        compiler_params=params(28),
        cost_estimate=cost(11),
        name="attention",
    )(count, patch_rows, whole, whole)


GELU_C = 0.7978845608028654


def in_halves(kernel, half, earlier, in_specs, out_specs, out_shape, shared, mib, name, scratch, args):
    aliases = {}
    if earlier is not None:
        n = len(args)
        inner = kernel

        def kernel(*refs):
            return inner(*refs[:n], *refs[n + len(shared) :])

        aliases = {n + i: out for i, out in enumerate(shared)}
        in_specs = in_specs + [pl.BlockSpec(memory_space=pl.ANY)] * len(shared)
        args = args + [earlier[out] for out in shared]
    return pl.pallas_call(
        kernel,
        grid=(PART,),
        in_specs=in_specs,
        out_specs=out_specs,
        out_shape=out_shape,
        scratch_shapes=scratch,
        input_output_aliases=aliases,
        compiler_params=params(mib),
        cost_estimate=cost(11),
        name=name,
    )(*args)


def rows_of(half, width):
    return pl.BlockSpec((CHUNK, width), lambda j: (half, 0))


def tile_of(half):
    return pl.BlockSpec((CHUNK, D), lambda j: (half, j))


def forward_kernel(x_ref, att_ref, wo_ref, wu_ref, wd_ref, we_ref, rows_ref, fours_ref,
                   resid_ref, n2_ref, act_ref, slope_ref, enc_ref, emb_ref, total):
    j = pl.program_id(0)

    @pl.when(j == 0)
    def _():
        resid = x_ref[...].astype(jnp.float32) + (
            dot_nn(att_ref[...], wo_ref[...]) + rows_ref[OB : OB + 1]
        )
        resid_ref[...] = resid
        h, _ = normalised(resid)
        n2_ref[...] = (h * rows_ref[G2 : G2 + 1] + rows_ref[S2 : S2 + 1]).astype(jnp.bfloat16)
        total[...] = resid + rows_ref[DB : DB + 1]

    v = dot_nn(n2_ref[...], wu_ref[...]) + rows_ref[pl.ds(UB + j, 1)]
    square = v * v
    t = jnp.tanh(v * (GELU_C + 0.044715 * GELU_C * square))
    lift = 0.5 + 0.5 * t
    active = v * lift
    act_ref[...] = active.astype(jnp.bfloat16)
    slope_ref[...] = (
        lift + active * (1.0 - t) * (GELU_C + 3 * 0.044715 * GELU_C * square)
    ).astype(jnp.bfloat16)
    total[...] += dot_nn(act_ref[...], wd_ref[...])

    @pl.when(j == PART - 1)
    def _():
        enc_ref[...] = total[...].astype(jnp.bfloat16)
        emb_ref[...] = (dot_nn(enc_ref[...], we_ref[...]) + fours_ref[EB : EB + 1]).astype(jnp.bfloat16)


def forward(half, earlier, patch_rows, attended, whole, rows, fours):
    return in_halves(
        forward_kernel,
        half,
        earlier,
        [
            rows_of(half, D),
            rows_of(half, D),
            columns(D, OUT_AT),
            tile_columns(UP_AT),
            tile_columns(DOWN_AT),
            columns(DD, EMB_AT),
            const(24, D),
            const(8, DD),
        ],
        [rows_of(half, D), rows_of(half, D), tile_of(half), tile_of(half), rows_of(half, D), const(CHUNK, DD)],
        [
            jax.ShapeDtypeStruct((ROWS, D), jnp.float32),
            jax.ShapeDtypeStruct((ROWS, D), jnp.bfloat16),
            jax.ShapeDtypeStruct((ROWS, FF), jnp.bfloat16),
            jax.ShapeDtypeStruct((ROWS, FF), jnp.bfloat16),
            jax.ShapeDtypeStruct((ROWS, D), jnp.bfloat16),
            jax.ShapeDtypeStruct((CHUNK, DD), jnp.bfloat16),
        ],
        (0, 1, 2, 3, 4),
        30,
        "forward",
        [pltpu.VMEM((CHUNK, D), jnp.float32)],
        [patch_rows, attended, whole, whole, whole, whole, rows, fours],
    )


def grid_kernel(image_ref, count_ref, order_ref, emb_ref, table_ref, w_ref, fours_ref, up_ref, start_ref,
                gemb_ref, dec_ref, dvec_ref):
    s = pl.program_id(0)
    cell = lax.broadcasted_iota(jnp.int32, (GRID, SLOT), 0)
    place = lax.broadcasted_iota(jnp.int32, (GRID, SLOT), 1)
    placed = jnp.where((order_ref[0] == cell) & (place < count_ref[s]), 1.0, 0.0)
    masked = 1.0 - jnp.sum(placed, axis=1, keepdims=True)
    placed = placed.astype(jnp.bfloat16)
    grid = dot_nn(placed, emb_ref[0]) + masked * fours_ref[TOK : TOK + 1] + table_ref[...]
    gain = fours_ref[G3 : G3 + 1]
    h, inverse = normalised(grid)
    dec_ref[0] = (h * gain + fours_ref[S3 : S3 + 1]).astype(jnp.bfloat16)
    grad = dot_nt(up_ref[0], w_ref[...])
    dh = grad * gain
    back = (
        dh - jnp.mean(dh, axis=-1, keepdims=True) - h * jnp.mean(dh * h, axis=-1, keepdims=True)
    ) * inverse
    gemb_ref[0] = dot_tn(placed, back.astype(jnp.bfloat16)).astype(jnp.bfloat16)

    @pl.when(s == 0)
    def _():
        dvec_ref[...] = start_ref[...]

    dvec_ref[...] += jnp.concatenate(
        [
            jnp.zeros((1, DD), jnp.float32),
            jnp.sum(masked * back, axis=0, keepdims=True),
            jnp.sum(grad * h, axis=0, keepdims=True),
            jnp.sum(grad, axis=0, keepdims=True),
            jnp.zeros((4, DD), jnp.float32),
        ],
        axis=0,
    )


def block(*shape):
    return pl.BlockSpec((1, *shape), lambda s, *_: (s, 0, 0))


def of_image(*shape):
    return pl.BlockSpec((1, *shape), lambda s, image, *_: (image[s], 0, 0))


def decoder_grid(image, count, order, embedded, table, pix_weight, fours, pixel_grad, start):
    n = image.shape[0]
    return pl.pallas_call(
        grid_kernel,
        grid_spec=pltpu.PrefetchScalarGridSpec(
            num_scalar_prefetch=2,
            grid=(n,),
            in_specs=[
                block(1, SLOT),
                block(SLOT, DD),
                const(GRID, DD),
                const(DD, PIX),
                const(8, DD),
                of_image(GRID, PIX),
                const(8, DD),
            ],
            out_specs=[block(SLOT, DD), block(GRID, DD), const(8, DD)],
        ),
        out_shape=[
            jax.ShapeDtypeStruct((n, SLOT, DD), jnp.bfloat16),
            jax.ShapeDtypeStruct((n, GRID, DD), jnp.bfloat16),
            jax.ShapeDtypeStruct((8, DD), jnp.float32),
        ],
        compiler_params=params(20),
        cost_estimate=cost(n),
        name="decoder_grid",
    )(image, count, order, embedded, table, pix_weight, fours, pixel_grad, start)


def pixel_kernel(image_ref, dec_ref, up_ref, w_ref, rows_ref, start_ref, bias_ref, *refs):
    pix_ref, dw_ref, dbias_ref = refs[-3:]
    s = pl.program_id(0)
    pix_ref[0] = (dot_nn(dec_ref[0], w_ref[...]) + rows_ref[PB : PB + 1]).astype(jnp.bfloat16)
    dw = dot_tn(dec_ref[0], up_ref[0])
    dbias = jnp.sum(up_ref[0].astype(jnp.float32), axis=0, keepdims=True)

    @pl.when(s == 0)
    def _():
        dw_ref[...] = start_ref[...] + dw
        dbias_ref[...] = bias_ref[...] + dbias

    @pl.when(s > 0)
    def _():
        dw_ref[...] += dw
        dbias_ref[...] += dbias


def decoder_pixels(image, decoded, pixel_grad, pix_weight, rows, start, bias, pixels=None):
    n = image.shape[0]
    args = [image, decoded, pixel_grad, pix_weight, rows, start, bias]
    specs = [block(GRID, DD), of_image(GRID, PIX), const(DD, PIX), const(24, D), const(DD, PIX), const(1, PIX)]
    if pixels is not None:
        args.append(pixels)
        specs.append(pl.BlockSpec(memory_space=pl.ANY))
    return pl.pallas_call(
        pixel_kernel,
        grid_spec=pltpu.PrefetchScalarGridSpec(
            num_scalar_prefetch=1,
            grid=(n,),
            in_specs=specs,
            out_specs=[of_image(GRID, PIX), const(DD, PIX), const(1, PIX)],
        ),
        out_shape=[
            jax.ShapeDtypeStruct((IMG_DEV, GRID, PIX), jnp.bfloat16),
            jax.ShapeDtypeStruct((DD, PIX), jnp.float32),
            jax.ShapeDtypeStruct((1, PIX), jnp.float32),
        ],
        input_output_aliases={} if pixels is None else {7: 0},
        compiler_params=params(20),
        cost_estimate=cost(0.8 * n),
        name="decoder_pixels",
    )(*args)


def with_role(kernel, grid, in_specs, out_specs, out_shape, mib, name, scratch=()):
    return pl.pallas_call(
        kernel,
        grid_spec=pltpu.PrefetchScalarGridSpec(
            num_scalar_prefetch=1,
            grid=grid,
            in_specs=in_specs,
            out_specs=out_specs,
            scratch_shapes=list(scratch),
        ),
        out_shape=out_shape,
        compiler_params=params(mib),
        cost_estimate=cost(0.01 if name == "input_back" else 10),
        name=name,
    )


def half_columns(mine):
    return pl.BlockSpec((ROWS, HALF), lambda i, role: (0, role[0] if mine else 1 - role[0]))


def half_tiles(mine):
    return pl.BlockSpec(
        (ROWS, HALF), lambda i, role: (0, 2 * i + (role[0] if mine else 1 - role[0]))
    )


C_ONE, C_TWO, C_THREE = FF + 2 * DD, FF + D, 3 * D + 128
THREE_CUT = (C_THREE // 128 + 1) // 2 * 128


def line_first():
    to = lax.broadcasted_iota(jnp.int32, (HALF, HALF), 0)
    place = to % 96 // 24 * 96 + to % 24 // 6 * 24 + to // 96 * 6 + to % 6
    return (lax.broadcasted_iota(jnp.int32, (HALF, HALF), 1) == place).astype(jnp.bfloat16)


def down_grad_kernel(role_ref, gemb_ref, gb2_ref, enc_mine, enc_other, act_mine, act_other, pix_mine, pix_other,
                     mine_ref, other_ref, dbias_ref, demb_ref):
    j = pl.program_id(0)

    @pl.when(j == 0)
    def _():
        dbias_ref[...] = jnp.sum(gb2_ref[...].astype(jnp.float32), axis=0, keepdims=True)
        demb_ref[...] = jnp.sum(gemb_ref[...].astype(jnp.float32), axis=0, keepdims=True)
        for ref, enc, pix in ((mine_ref, enc_mine, pix_mine), (other_ref, enc_other, pix_other)):
            ref[:, FF : FF + DD] = dot_tn(enc[...], gemb_ref[...]).astype(jnp.bfloat16)
            ref[:, FF + DD :] = pix[...]

    at = pl.ds(pl.multiple_of(j * D, D), D)
    mine_ref[:, at] = dot_tn(act_mine[...], gb2_ref[...]).astype(jnp.bfloat16)
    other_ref[:, at] = dot_tn(act_other[...], gb2_ref[...]).astype(jnp.bfloat16)


def down_grad(role, gemb, gb2, enc, act, dpix):
    return with_role(
        down_grad_kernel,
        (PART,),
        [
            const(ROWS, DD),
            const(ROWS, D),
            half_columns(True),
            half_columns(False),
            half_tiles(True),
            half_tiles(False),
            pl.BlockSpec((HALF, DD), lambda i, role: (role[0], 0)),
            pl.BlockSpec((HALF, DD), lambda i, role: (1 - role[0], 0)),
        ],
        [const(HALF, C_ONE), const(HALF, C_ONE), const(1, D), const(1, DD)],
        [
            jax.ShapeDtypeStruct((HALF, C_ONE), jnp.bfloat16),
            jax.ShapeDtypeStruct((HALF, C_ONE), jnp.bfloat16),
            jax.ShapeDtypeStruct((1, D), jnp.float32),
            jax.ShapeDtypeStruct((1, DD), jnp.float32),
        ],
        30,
        "down_grad",
    )(role, gemb, gb2, enc, enc, act, act, dpix, dpix)


def lined_kernel(order_ref, mine_ref, came_ref, sum_ref):
    total = (mine_ref[...].astype(jnp.float32) + came_ref[...].astype(jnp.float32)).astype(jnp.bfloat16)
    sum_ref[...] = dot_nn(order_ref[...], total).astype(jnp.bfloat16)


def lined(order, mine, came):
    tile = pl.BlockSpec((HALF, 1024), lambda j: (0, j))
    return pl.pallas_call(
        lined_kernel,
        grid=(C_ONE // 1024,),
        in_specs=[const(HALF, HALF), tile, tile],
        out_specs=tile,
        out_shape=jax.ShapeDtypeStruct((HALF, C_ONE), jnp.bfloat16),
        compiler_params=params(60),
        cost_estimate=cost(4),
        name="lined",
    )(order, mine, came)


def hidden_back_kernel(gemb_ref, we_ref, wd_ref, wu_ref, slope_ref, resid_ref, wo_ref, rows_ref,
                       gb2_ref, gh_ref, gres_ref, gb_ref, gatt_ref, dup_ref, dvec_ref, total, genc):
    j = pl.program_id(0)

    @pl.when(j == 0)
    def _():
        genc[...] = dot_nt(gemb_ref[...], we_ref[...])
        gb2_ref[...] = genc[...].astype(jnp.bfloat16)
        dup_ref[...] = jnp.zeros_like(dup_ref)

    gh = (dot_nt(gb2_ref[...], wd_ref[...]) * slope_ref[...].astype(jnp.float32)).astype(jnp.bfloat16)
    gh_ref[...] = gh
    dup_ref[pl.ds(j, 1)] = jnp.sum(gh.astype(jnp.float32), axis=0, keepdims=True)
    part = dot_nt(gh, wu_ref[...])

    @pl.when(j == 0)
    def _():
        total[...] = part

    @pl.when(j > 0)
    def _():
        total[...] += part

    @pl.when(j == PART - 1)
    def _():
        back, dgain, dshift = norm_back(resid_ref[...], rows_ref[G2 : G2 + 1], total[...])
        gres = genc[...] + back
        gres_ref[...] = gres
        gb = gres.astype(jnp.bfloat16)
        gb_ref[...] = gb
        gatt_ref[...] = dot_nt(gb, wo_ref[...]).astype(jnp.bfloat16)
        dvec_ref[...] = jnp.concatenate(
            [
                dgain,
                dshift,
                jnp.sum(gb.astype(jnp.float32), axis=0, keepdims=True),
                jnp.zeros((5, D), jnp.float32),
            ],
            axis=0,
        )


def hidden_back(half, earlier, gemb, whole, slope, resid, rows):
    return in_halves(
        hidden_back_kernel,
        half,
        earlier,
        [
            const(CHUNK, DD),
            columns(DD, EMB_AT),
            tile_columns(DOWN_AT),
            tile_columns(UP_AT),
            tile_of(half),
            rows_of(half, D),
            columns(D, OUT_AT),
            const(24, D),
        ],
        [
            rows_of(half, D),
            tile_of(half),
            rows_of(half, D),
            rows_of(half, D),
            rows_of(half, D),
            const(8, D),
            const(8, D),
        ],
        [
            jax.ShapeDtypeStruct((ROWS, D), jnp.bfloat16),
            jax.ShapeDtypeStruct((ROWS, FF), jnp.bfloat16),
            jax.ShapeDtypeStruct((ROWS, D), jnp.float32),
            jax.ShapeDtypeStruct((ROWS, D), jnp.bfloat16),
            jax.ShapeDtypeStruct((ROWS, D), jnp.bfloat16),
            jax.ShapeDtypeStruct((8, D), jnp.float32),
            jax.ShapeDtypeStruct((8, D), jnp.float32),
        ],
        (0, 1, 2, 3, 4),
        30,
        "hidden_back",
        [pltpu.VMEM((CHUNK, D), jnp.float32)] * 2,
        [gemb, whole, whole, whole, slope, resid, whole, rows],
    )


BLOCKS = HALF // 24


def put_blocks(ref, columns, rows):
    for n in range(BLOCKS):
        ref[n, :, columns] = rows[24 * n : 24 * n + 24].astype(jnp.bfloat16)


def up_grad_kernel(role_ref, n2_mine, n2_other, gh_ref, att_mine, att_other, gb_ref, mine_ref, other_ref):
    j = pl.program_id(0)
    at = pl.ds(pl.multiple_of(j * D, D), D)
    put_blocks(mine_ref, at, dot_tn(n2_mine[...], gh_ref[...]))
    put_blocks(other_ref, at, dot_tn(n2_other[...], gh_ref[...]))

    @pl.when(j == PART - 1)
    def _():
        put_blocks(mine_ref, slice(FF, C_TWO), dot_tn(att_mine[...], gb_ref[...]))
        put_blocks(other_ref, slice(FF, C_TWO), dot_tn(att_other[...], gb_ref[...]))


def up_grad(role, n2, gh, attended, gb):
    return with_role(
        up_grad_kernel,
        (PART,),
        [
            half_columns(True),
            half_columns(False),
            pl.BlockSpec((ROWS, D), lambda j, role: (0, j)),
            half_columns(True),
            half_columns(False),
            const(ROWS, D),
        ],
        [const(BLOCKS, 24, C_TWO), const(BLOCKS, 24, C_TWO)],
        [
            jax.ShapeDtypeStruct((BLOCKS, 24, C_TWO), jnp.bfloat16),
            jax.ShapeDtypeStruct((BLOCKS, 24, C_TWO), jnp.bfloat16),
        ],
        34,
        "up_grad",
    )(role, n2, n2, gh, attended, attended, gb)


def attention_back_kernel(count_ref, mixed_ref, gatt_ref, gmix_ref, held, gheld):
    live = lax.broadcasted_iota(jnp.int32, (SLOT, SLOT), 0) < count_ref[pl.program_id(0)]
    masks = head_masks()
    low_lane = lax.broadcasted_iota(jnp.int32, (SLOT, 128), 1) < HD
    scale = HD ** (-0.5)
    for pair in range(H // 2):
        c = pair * 128
        held[pair] = dot_nt(stacked(mixed_ref[:, D + c : D + c + 128], masks), mixed_ref[:, c : c + 128])
        gheld[pair] = dot_nt(
            stacked(mixed_ref[:, 2 * D + c : 2 * D + c + 128], masks), gatt_ref[:, c : c + 128]
        )
    for pair in range(H // 2):
        c = pair * 128
        probs = key_probs(held[pair], live)
        gscores = []
        for k in range(2):
            p, g = probs[k], gheld[pair, SLOT * k : SLOT * k + SLOT]
            gscores.append(p * (g - jnp.sum(p * g, axis=0, keepdims=True)))
        gscores = jnp.concatenate(gscores, axis=0).astype(jnp.bfloat16)
        probs = jnp.concatenate(probs, axis=0).astype(jnp.bfloat16)
        gv = dot_nn(probs, gatt_ref[:, c : c + 128])
        gk = dot_nn(gscores, mixed_ref[:, c : c + 128]) * scale
        gq = dot_tn(gscores, stacked(mixed_ref[:, D + c : D + c + 128], masks)) * scale
        gmix_ref[:, c : c + 128] = gq.astype(jnp.bfloat16)
        gmix_ref[:, D + c : D + c + 128] = jnp.where(low_lane, gk[:SLOT], gk[SLOT:]).astype(jnp.bfloat16)
        gmix_ref[:, 2 * D + c : 2 * D + c + 128] = jnp.where(
            low_lane, gv[:SLOT], gv[SLOT:]
        ).astype(jnp.bfloat16)


def attention_back(count, mixed, gatt):
    wide = pl.BlockSpec((SLOT, 3 * D), lambda s: (s, 0))
    return pl.pallas_call(
        attention_back_kernel,
        grid=(IMG_DEV,),
        in_specs=[
            pl.BlockSpec(memory_space=pltpu.SMEM),
            wide,
            pl.BlockSpec((SLOT, D), lambda s: (s, 0)),
        ],
        out_specs=wide,
        out_shape=jax.ShapeDtypeStruct((ROWS, 3 * D), jnp.bfloat16),
        scratch_shapes=[pltpu.VMEM((H // 2, 2 * SLOT, SLOT), jnp.float32)] * 2,
        compiler_params=params(20),
        cost_estimate=cost(0.01),
        name="attention_back",
    )(count, mixed, gatt)


def input_back_kernel(role_ref, gmix_ref, w_ref, x_ref, gres_ref, rows_ref, normed_mine, normed_other,
                      dup_ref, d2_ref, ddown_ref, dpb_ref, d3_ref, demb_ref,
                      pg_ref, mine_ref, other_ref, total, turned):
    j = pl.program_id(0)
    at = pl.ds(pl.multiple_of(j * D, D), D)
    gmix = gmix_ref[...]
    put_blocks(mine_ref, at, dot_tn(normed_mine[...], gmix))
    put_blocks(other_ref, at, dot_tn(normed_other[...], gmix))
    part = dot_nt(gmix, w_ref[...])
    dbias = jnp.sum(gmix.astype(jnp.float32), axis=0, keepdims=True)

    @pl.when(j == 0)
    def _():
        total[...] = part
        turned[QB : QB + 1] = dbias

    @pl.when(j > 0)
    def _():
        total[...] += part

    @pl.when(j == 2)
    def _():
        back, dgain, dshift = norm_back(
            x_ref[...].astype(jnp.float32), rows_ref[G1 : G1 + 1], total[...]
        )
        pg_ref[...] = (gres_ref[...] + back).astype(jnp.bfloat16)
        turned[G1 : G1 + 1] = dgain
        turned[S1 : S1 + 1] = dshift
        turned[VB : VB + 1] = dbias
        turned[OB : OB + 1] = d2_ref[2:3]
        turned[G2 : G2 + 1] = d2_ref[0:1]
        turned[S2 : S2 + 1] = d2_ref[1:2]
        turned[DB : DB + 1] = ddown_ref[...]
        turned[PB : PB + 1] = dpb_ref[...]
        turned[UB : UB + 4] = dup_ref[0:4]
        turned[13:16] = jnp.zeros((3, D), jnp.float32)
        four = jnp.concatenate([demb_ref[...], d3_ref[1:4], jnp.zeros((4, DD), jnp.float32)], axis=0)
        turned[16:24] = dot_nt(four.astype(jnp.bfloat16), spread())
        block = jnp.concatenate([turned[...], jnp.zeros((104, D), jnp.float32)], axis=0).T
        first, second = block[:HALF], block[HALF:]
        up = role_ref[0] == 1
        put_blocks(mine_ref, slice(3 * D, C_THREE), jnp.where(up, second, first))
        put_blocks(other_ref, slice(3 * D, C_THREE), jnp.where(up, first, second))


def input_back(role, gmix, whole, x, gres, rows, normed, dup, d2, ddown, dpb, d3, demb):
    return with_role(
        input_back_kernel,
        (3,),
        [
            pl.BlockSpec((ROWS, D), lambda j, role: (0, j)),
            pl.BlockSpec((D, D), lambda j, role: (0, j)),
            const(ROWS, D),
            const(ROWS, D),
            const(24, D),
            half_columns(True),
            half_columns(False),
            const(8, D),
            const(8, D),
            const(1, D),
            const(1, D),
            const(8, DD),
            const(1, DD),
        ],
        [const(ROWS, D), const(BLOCKS, 24, C_THREE), const(BLOCKS, 24, C_THREE)],
        [
            jax.ShapeDtypeStruct((ROWS, D), jnp.bfloat16),
            jax.ShapeDtypeStruct((BLOCKS, 24, C_THREE), jnp.bfloat16),
            jax.ShapeDtypeStruct((BLOCKS, 24, C_THREE), jnp.bfloat16),
        ],
        30,
        "input_back",
        [pltpu.VMEM((ROWS, D), jnp.float32), pltpu.VMEM((24, D), jnp.float32)],
    )(role, gmix, whole, x, gres, rows, normed, normed, dup, d2, ddown, dpb, d3, demb)


def hot(shape, test):
    return test(
        lax.broadcasted_iota(jnp.int32, shape, 0), lax.broadcasted_iota(jnp.int32, shape, 1)
    ).astype(jnp.bfloat16)


def hidden_order():
    return hot((512, 512), lambda l, c: l == 4 * (c % 128) + c // 128)


def pack_kernel(qkv_ref, out_ref, up_ref, down_ref, emb_ref, pix_ref, *refs):
    six_refs, bias_ref, four_refs, packed_ref = refs[:9], refs[9], refs[10:14], refs[14]
    packed_ref[:, :OUT_AT] = qkv_ref[...]
    packed_ref[:, OUT_AT:UP_AT] = out_ref[...]
    order = hidden_order()
    for r in range(D // 128):
        turned = dot_nn(up_ref[:, 512 * r : 512 * r + 512], order).astype(jnp.bfloat16)
        for j in range(PART):
            at = UP_AT + j * D + 128 * r
            packed_ref[:, at : at + 128] = turned[:, 128 * j : 128 * j + 128]
    for j in range(PART):
        rows = hot((6, 24), lambda i, l: l == 4 * i + j)
        packed_ref[:, DOWN_AT + j * D : DOWN_AT + j * D + D] = dot_nn(rows, down_ref[...]).astype(jnp.bfloat16)
    packed_ref[:, EMB_AT:PIX_AT] = emb_ref[...]
    for t in range(2):
        part = jnp.zeros((6, 256), jnp.float32)
        for s in range(3):
            rows = hot((6, 4), lambda r, i: 2 * r + t == 3 * i + s)
            part = part + dot_nn(rows, pix_ref[:, 256 * s : 256 * s + 256])
        packed_ref[:, PIX_AT + 256 * t : PIX_AT + 256 * t + 256] = part.astype(jnp.bfloat16)
    lane = lax.broadcasted_iota(jnp.int32, (6, 128), 1)
    block = jnp.zeros((6, 128), jnp.float32)

    def put(block, ref, count, start, pick):
        size = ref.shape[0]
        line = jnp.broadcast_to(ref[...].astype(jnp.float32).reshape(1, size), (6, size))
        row = lax.broadcasted_iota(jnp.int32, (6, size), 0)
        at = lax.broadcasted_iota(jnp.int32, (6, size), 1)
        for c in range(count):
            column = jnp.sum(jnp.where(at == pick(row, c), line, 0.0), axis=1, keepdims=True)
            block = jnp.where(lane == start + c, column, block)
        return block

    for n, ref in enumerate(six_refs):
        block = put(block, ref, 1, n, lambda row, c: row)
    block = put(block, bias_ref, PART, UB, lambda row, c: PART * row + c)
    for n, ref in enumerate(four_refs):
        block = put(block, ref, 1, 16 + n, lambda row, c: row)
    packed_ref[:, VEC_AT:] = block.astype(jnp.bfloat16)


def packing_kernel(*refs):
    n = (len(refs) - 2) // 2
    given, packed_ref, held, sems = refs[:n], refs[n], refs[n + 1 : 2 * n + 1], refs[-1]
    copies = [
        pltpu.make_async_copy(source, place, sems.at[i])
        for i, (source, place) in enumerate(zip(given, held))
    ]
    for copy in copies:
        copy.start()
    for copy in copies:
        copy.wait()
    pack_kernel(*held, packed_ref)


def pack(*args):
    return pl.pallas_call(
        packing_kernel,
        in_specs=[pl.BlockSpec(memory_space=pltpu.HBM)] * len(args),
        out_shape=jax.ShapeDtypeStruct((6, WIDE), jnp.bfloat16),
        scratch_shapes=[pltpu.VMEM(arg.shape, arg.dtype) for arg in args]
        + [pltpu.SemaphoreType.DMA((len(args),))],
        compiler_params=pltpu.CompilerParams(vmem_limit_bytes=64 * MIB - 65536),
        cost_estimate=cost(4),
        name="pack",
    )(*args)


def unpack_kernel(kept_one, came_one, kept_two, came_two, qkv_ref, out_ref, up_ref, down_ref, emb_ref, pix_ref, vec_ref):
    first, second = (kept_one, came_one), (kept_two, came_two)

    def total(pair, at, width):
        return sum(ref[:, at : at + width].astype(jnp.float32) for ref in pair)

    def shuffled(pair, dot):
        return dot(pair[0]) + dot(pair[1])

    two_at, three_at = C_TWO // 2, THREE_CUT

    def spot(group, column):
        if group == 2:
            return column if column < two_at else column + three_at
        return column + two_at if column < three_at else column + C_TWO

    for column in range(0, 3 * D, 128):
        qkv_ref[:, column : column + 128] = total(second, spot(3, column), 128)
    for column in range(0, D, 128):
        out_ref[:, column : column + 128] = total(second, spot(2, FF + column), 128)
    emb_ref[...] = total(first, FF, DD)
    vec_ref[...] = total(second, spot(3, 3 * D), 128)
    order = hidden_order()
    for r in range(D // 128):

        def turned(ref):
            starts = [spot(2, j * D + 128 * r) for j in range(PART)]
            parts = [ref[:, at : at + 128] for at in starts]
            return dot_nt(jnp.concatenate(parts, axis=1), order)

        up_ref[:, 512 * r : 512 * r + 512] = shuffled(second, turned)
    down = jnp.zeros((24, D), jnp.float32)
    for j in range(PART):
        rows = hot((24, 6), lambda l, i: l == 4 * i + j)
        down = down + shuffled(first, lambda ref: dot_nn(rows, ref[:, j * D : j * D + D]))
    down_ref[...] = down
    for s in range(3):
        part = jnp.zeros((4, 256), jnp.float32)
        for t in range(2):
            rows = hot((4, 6), lambda i, r: 2 * r + t == 3 * i + s)
            at = FF + DD + 256 * t
            part = part + shuffled(first, lambda ref: dot_nn(rows, ref[:, at : at + 256]))
        pix_ref[:, 256 * s : 256 * s + 256] = part


def turn_kernel(plan, bits_ref, *refs):
    inputs = [len(term) for group in plan for term in group["terms"]]
    given = iter(refs[: sum(inputs)])
    out = iter(refs[sum(inputs) :])
    for group in plan:
        terms = [([next(given) for _ in term], group["columns"]) for term in group["terms"]]
        kept_ref, sent_ref = next(out), next(out)
        bit = bits_ref[group["bit"]]
        column = 0
        for term, columns in terms:
            start, width = columns or (0, term[0].shape[-1])
            source, to = slice(start, start + width), slice(column, column + width)
            column += width

            def added(*at):
                return sum(ref[(*at, slice(None), source)].astype(jnp.float32) for ref in term)

            if group["dim"] is None:
                rows = term[0].shape[-2] // 2
                value = added(*[0] * (len(term[0].shape) - 2))
                low, high = value[:rows], value[rows:]
                kept_ref[:, to] = jnp.where(bit == 1, high, low).astype(jnp.bfloat16)
                sent_ref[:, to] = jnp.where(bit == 1, low, high).astype(jnp.bfloat16)
                continue
            p, q = kept_ref.shape[:2]
            for ref, half in ((kept_ref, bit), (sent_ref, 1 - bit)):
                for i in range(p):
                    for j in range(q):
                        at = (half * p + i, j) if group["dim"] == 0 else (i, half * q + j)
                        ref[i, j, :, to] = added(*at).astype(jnp.bfloat16)


def turn(bits, *groups):
    plan, args, shapes = [], [], []
    for terms, dim, bit, columns in groups:
        plan.append(dict(terms=terms, dim=dim, bit=bit, columns=columns))
        for term in terms:
            args += term
        width = sum(columns[1] if columns else term[0].shape[-1] for term in terms)
        shape = list(terms[0][0].shape[:-1])
        if dim is None:
            shape = [shape[-1] // 2]
        else:
            shape[dim] //= 2
        shapes += [jax.ShapeDtypeStruct((*shape, width), jnp.bfloat16)] * 2
    plan = [dict(group, terms=[[None] * len(term) for term in group["terms"]]) for group in plan]
    out = pl.pallas_call(
        functools.partial(turn_kernel, plan),
        in_specs=[pl.BlockSpec(memory_space=pltpu.SMEM)]
        + [pl.BlockSpec(memory_space=pltpu.VMEM)] * len(args),
        out_shape=shapes,
        compiler_params=pltpu.CompilerParams(vmem_limit_bytes=14 * MIB),
        cost_estimate=cost(3),
        name="turn",
    )(bits, *args)
    return [tuple(out[n : n + 2]) for n in range(0, len(out), 2)]


def unpack(*terms):
    return pl.pallas_call(
        unpack_kernel,
        out_shape=[
            jax.ShapeDtypeStruct(shape, jnp.float32)
            for shape in ((6, 3 * D), (6, D), (6, FF), (24, D), (6, DD), (4, PIX), (6, 128))
        ],
        compiler_params=pltpu.CompilerParams(vmem_limit_bytes=16 * MIB),
        cost_estimate=cost(4),
        name="unpack",
    )(*terms)


PAIRS = {
    "high": [(0, 3), (3, 0), (1, 2), (2, 1)],
    "low": [(0, 1), (1, 0), (2, 3), (3, 2)],
}


ROLE_PAIR = [(0, 1), (1, 0)]


def tie(*arrays):
    return lax.optimization_barrier(arrays)


def moved(images, step, crossing=False):
    pairs = [
        (r * N_DP + p, (r ^ crossing) * N_DP + (p + step) % N_DP)
        for r in range(2)
        for p in range(N_DP)
    ]
    return lax.ppermute(images, ALL, pairs)


def added(mine, came):
    return (mine.astype(jnp.float32) + came.astype(jnp.float32)).astype(jnp.bfloat16)


def sent_on(axis, which, halves):
    return halves[0], lax.ppermute(halves[1], axis, PAIRS[which])


def body(
    patch_rows,
    patch_order,
    visible_count,
    encoded_image,
    first_gain,
    first_shift,
    query_key_value,
    query_bias,
    value_bias,
    output_weight,
    output_bias,
    second_gain,
    second_shift,
    up_weight,
    up_bias,
    down_weight,
    down_bias,
    embed_weight,
    embed_bias,
    mask_token,
    decoder_gain,
    decoder_shift,
    pixel_weight,
    pixel_bias,
    pixel_grad,
):
    device = lax.axis_index(ALL)
    role = lax.axis_index("role").astype(jnp.int32).reshape(1)
    image_count = encoded_image.shape[0]

    own_images = device * IMG_DEV + jnp.arange(IMG_DEV, dtype=jnp.int32)
    found = encoded_image[None, :] == own_images[:, None]
    source_slot = jnp.sum(
        jnp.where(found, jnp.arange(image_count, dtype=jnp.int32)[None, :], 0), axis=1
    )
    source_place = source_slot % IMG_DEV
    image_of = jnp.sum(
        jnp.where(
            source_place[None, :] == jnp.arange(IMG_DEV, dtype=jnp.int32)[:, None],
            jnp.arange(IMG_DEV, dtype=jnp.int32)[None, :],
            0,
        ),
        axis=1,
    )
    own_count = lax.dynamic_slice_in_dim(visible_count, device * IMG_DEV, IMG_DEV)
    own_order = lax.dynamic_slice_in_dim(patch_order, device * IMG_DEV, IMG_DEV, 0)[:, None, :SLOT]
    first, later = image_of[jnp.array([0, 4])], image_of[jnp.array([1, 5, 2, 6, 3, 7])]

    packed = pack(
        query_key_value,
        output_weight,
        up_weight,
        down_weight,
        embed_weight,
        pixel_weight,
        first_gain,
        first_shift,
        query_bias,
        value_bias,
        output_bias,
        second_gain,
        second_shift,
        down_bias,
        pixel_bias,
        up_bias,
        embed_bias,
        mask_token,
        decoder_gain,
        decoder_shift,
    )
    whole = lax.all_gather(packed, "x", tiled=True)
    whole = lax.all_gather(whole, ("role", "y", "z"), tiled=True)
    pix_weight = whole[:, PIX_AT:VEC_AT].reshape(DD, PIX)

    held = lax.dynamic_slice_in_dim(encoded_image, device * IMG_DEV, IMG_DEV)
    count = visible_count[held]

    normed, mixed, attended, rows, fours = attention(count, patch_rows, whole)
    half = forward(1, None, patch_rows, attended, whole, rows, fours)
    high = moved(half[5].reshape(4, SLOT, DD), 4, True)
    half = forward(0, half, patch_rows, attended, whole, rows, fours)
    resid, normed_two, active, slope, encoded, embedded = half
    embedded, high = tie(embedded, high)
    low = moved(embedded.reshape(4, SLOT, DD), 0, True)
    steps = [
        moved(jnp.concatenate([low[s : s + 1], high[s : s + 1]]), s) for s in range(1, 4)
    ]
    table = positions()
    zeros = jnp.zeros((8, DD), jnp.float32), jnp.zeros((DD, PIX), jnp.float32), jnp.zeros((1, PIX), jnp.float32)
    grad_first, decoded, d_three = decoder_grid(
        first,
        own_count[first],
        own_order[first],
        jnp.concatenate([low[:1], high[:1]]),
        table,
        pix_weight,
        fours,
        pixel_grad,
        zeros[0],
    )
    pixels, d_pix, d_pix_bias = decoder_pixels(
        first, decoded, pixel_grad, pix_weight, rows, zeros[1], zeros[2]
    )
    d_pix, *steps = tie(d_pix, *steps)
    grad_later, decoded, d_three = decoder_grid(
        later,
        own_count[later],
        own_order[later],
        jnp.concatenate(steps),
        table,
        pix_weight,
        fours,
        pixel_grad,
        d_three,
    )
    steps = [moved(grad_later[2 * s - 2 : 2 * s], -s) for s in range(1, 4)]
    pixels, d_pix, d_pix_bias = decoder_pixels(
        later, decoded, pixel_grad, pix_weight, rows, d_pix, d_pix_bias, pixels
    )
    d_pix, *steps = tie(d_pix, *steps)
    high = moved(jnp.concatenate([grad_first[1:]] + [s[1:] for s in steps]), -4, True).reshape(CHUNK, DD)
    low = moved(jnp.concatenate([grad_first[:1]] + [s[:1] for s in steps]), 0, True).reshape(CHUNK, DD)
    low, pix_rows, line = tie(low, d_pix.astype(jnp.bfloat16).reshape(D, DD), line_first())
    half = hidden_back(0, None, low, whole, slope, resid, rows)
    d_up_bias, d_second = half[5:]
    high, part = tie(high, half[0])
    half = hidden_back(1, [part, *half[1:]], high, whole, slope, resid, rows)
    branch_two, grad_hidden, grad_resid, grad_branch, grad_attended = half[:5]
    d_up_bias, d_second = d_up_bias + half[5], d_second + half[6]
    mine_one, other_one, d_down_bias, d_emb_bias = down_grad(
        role,
        jnp.concatenate([low, high]),
        branch_two,
        encoded,
        active,
        pix_rows,
    )
    grad_hidden, other_one = tie(grad_hidden, other_one)
    came_one = lax.ppermute(other_one, "role", ROLE_PAIR)
    mine_two, other_two = up_grad(role, normed_two, grad_hidden, attended, grad_branch)
    came_two = lax.ppermute(other_two, "role", ROLE_PAIR)
    mine_one, came_one, mine_two = tie(mine_one, came_one, mine_two)
    part_one, came_two = tie(lined(line, mine_one, came_one), came_two)
    part_one = lax.psum_scatter(part_one, "x", tiled=True)
    ring = [lax.axis_index(axis) for axis in "yzx"]
    bits = jnp.stack([at // 2 for at in ring] + [at % 2 for at in ring]).astype(jnp.int32)
    y_high, z_high, x_high, y_low, z_low, x_low = range(6)

    def in_planes(array):
        return array.reshape(4, 4, 24, array.shape[-1])

    def parted(mine, came, cut):
        term = [in_planes(mine), in_planes(came)]
        width = mine.shape[-1]
        return ([term], 1, z_high, (0, cut)), ([term], 0, y_high, (cut, width - cut))

    first_two, second_two = turn(bits, *parted(mine_two, came_two, C_TWO // 2))
    grad_attended, *both = tie(grad_attended, *first_two, *second_two)
    first_two, second_two = sent_on("z", "high", both[:2]), sent_on("y", "high", both[2:])
    grad_mixed = attention_back(count, mixed, grad_attended)
    patch_grad, mine, other = input_back(
        role,
        grad_mixed,
        whole,
        patch_rows,
        grad_resid,
        rows,
        normed,
        d_up_bias,
        d_second,
        d_down_bias,
        d_pix_bias,
        d_three,
        d_emb_bias,
    )
    mine, other, came_a, came_b = tie(mine, other, first_two[1], second_two[1])
    first_two, second_two = (first_two[0], came_a), (second_two[0], came_b)
    came_three = lax.ppermute(other, "role", ROLE_PAIR)
    first_three, second_three = turn(bits, *parted(mine, came_three, THREE_CUT))
    first_three = sent_on("z", "high", first_three)
    second_three = sent_on("y", "high", second_three)
    one = part_one.reshape(4, 1, 24, C_ONE)
    first, second, one = turn(
        bits,
        ([first_two, first_three], 1, z_low, None),
        ([second_two, second_three], 0, y_low, None),
        ([[one]], 0, y_high, None),
    )
    first, second, one = sent_on("z", "low", first), sent_on("y", "low", second), sent_on("y", "high", one)
    first, second, one = turn(
        bits, ([first], 0, y_high, None), ([second], 1, z_high, None), ([one], 0, y_low, None)
    )
    first, second, one = sent_on("y", "high", first), sent_on("z", "high", second), sent_on("y", "low", one)
    first, second, one = turn(
        bits, ([first], 0, y_low, None), ([second], 1, z_low, None), ([one], None, z_high, None)
    )
    first, second, one = sent_on("y", "low", first), sent_on("z", "low", second), sent_on("z", "high", one)
    rest, one = turn(bits, ([first, second], None, x_high, None), ([one], None, z_low, None))
    rest, one = sent_on("x", "high", rest), sent_on("z", "low", one)
    (rest,) = turn(bits, ([rest], None, x_low, None))
    rest = sent_on("x", "low", rest)
    d_qkv, d_out, d_up, d_down, d_emb, d_pix, vec = unpack(*one, *rest)
    return (
        pixels,
        patch_grad,
        vec[:, G1],
        vec[:, S1],
        d_qkv,
        vec[:, QB],
        vec[:, VB],
        d_out,
        vec[:, OB],
        vec[:, G2],
        vec[:, S2],
        d_up,
        vec[:, UB : UB + PART].reshape(6 * PART),
        d_down,
        vec[:, DB],
        d_emb,
        vec[:4, 16 + EB],
        vec[:4, 16 + TOK],
        vec[:4, 16 + G3],
        vec[:4, 16 + S3],
        d_pix,
        vec[:, PB],
    )


def solution(mesh):
    mesh = Mesh(mesh.devices.reshape(2, 4, 4, 4), ALL)
    two, one = P(ALL, None), P(ALL)
    placed = (two, P(), P(), P(), one, one, two, one, one, two, one, one, one, two, one, two, one)
    placed += (two, one, one, one, one, two, one, P(ALL, None, None))
    given = (P(ALL, None, None), two, one, one, two, one, one, two, one, one, one, two, one, two, one)
    given += (two, one, one, one, one, two, one)
    return jax.shard_map(body, mesh=mesh, in_specs=placed, out_specs=given, check_vma=False)
```
